128 devices in a mesh: doc: 4 (over z), seq: 32 (over y, x, core).
Axes of the slice: x: 4, y: 4, z: 4, core: 2. Of those that a mesh axis runs over, the one named last changes fastest.
Arguments:
- text: bfloat16 [16384, 4096], P(('doc', 'seq')), may hold values from -6 to 6
- norm_gain: float32 [4096], replicated, may hold values from 0.1 to 1.9
- q_weight: bfloat16 [4096, 2048], P('seq'), may hold values from -0.09375 to 0.09375
- k_weight: bfloat16 [4096, 512], P('seq'), may hold values from -0.09375 to 0.09375
- v_weight: bfloat16 [4096, 512], P('seq'), may hold values from -0.09375 to 0.09375
- q_gain: float32 [128], replicated, may hold values from 1.4 to 7
- k_gain: float32 [128], replicated, may hold values from 1.4 to 7
- vision: bfloat16 [128, 1601, 4096], P(('doc', 'seq')), may hold values from -6 to 6
- tiles_per_image: int32 [4, 2], replicated, may hold values from 0 to 4, as said below
- image_start: int32 [4, 2], replicated, may hold values from 0 to 4096, as said below
- tile_owner: int32 [4, 4], replicated, may hold values from 0 to 31, as said below
Outputs:
- context: bfloat16 [16384, 2048], P(('doc', 'seq'))
The draws below stay inside these ranges and needn't reach their ends.
Inputs may be any that keep to these rules, and one draw needn't show every extreme that they name: `tiles_per_image`: A document's present images come first, each with 1 or more tiles, and the absent ones have 0; each document has 1 to 2 present images; some document has exactly 1 image and some other has 2; a document's tiles sum to at most 4, and some document has exactly 4. `image_start`: strictly increasing over a document's present images; images with 0 tiles start at 4096. `tile_owner`: the 4 entries of a document are distinct.
All inputs are finite; a program needn't handle non-finite values.
Results may differ from the reference program's by a relative error of at most 0.006.
The reference program's roundings to bfloat16 on the way (of `normed`, `query` and `probs_low`) count: a program that leaves them out, or rounds other values in their place, can miss the bound.
Values may be sent and summed in bfloat16 or wider, within the bound.
No kernel may reach another device: no remote copies, remote signals or barrier semaphores. Data moves between devices by JAX's collectives and lax.ppermute only.
A program may use at most 256 MiB of HBM per device.

```python
import jax
import jax.numpy as jnp
from jax import lax

D = 4096
HQ = 16
HK = 4
HD = 128
TILE = 1601
IMG_MAX = 2
MAXT = 4
TOK_DEV = 128
NDOC = 4
LEN = 4096
TOKENS = 16384
SLOTS = 128
N_SEQ = 32


def doc_layout(key):
    keys = jax.random.split(key, 5)
    image_ids = jnp.arange(IMG_MAX, dtype=jnp.int32)
    doc_ids = jnp.arange(NDOC, dtype=jnp.int32)
    counts = jax.random.randint(keys[0], (NDOC,), 1, IMG_MAX + 1)
    single_doc = jax.random.randint(keys[1], (), 0, NDOC)
    multi_doc = (single_doc + 1) % NDOC
    counts = jnp.where(doc_ids == single_doc, 1, counts)
    counts = jnp.where(doc_ids == multi_doc, IMG_MAX, counts)
    single_tiles = jax.random.randint(keys[2], (NDOC,), 1, MAXT + 1)
    single_tiles = jnp.where(doc_ids == single_doc, MAXT, single_tiles)
    shared_tiles = jax.random.randint(keys[3], (NDOC, IMG_MAX), 1, MAXT // IMG_MAX + 1)
    shared_tiles = jnp.where(image_ids[None, :] < counts[:, None], shared_tiles, 0)
    lone = jnp.where(image_ids[None, :] == 0, single_tiles[:, None], 0)
    tiles = jnp.where(counts[:, None] == 1, lone, shared_tiles)
    span_low = image_ids * (LEN // IMG_MAX)
    span_width = LEN // (2 * IMG_MAX)
    raw_starts = span_low[None, :] + jax.random.randint(keys[4], (NDOC, IMG_MAX), 0, span_width)
    starts = jnp.where(image_ids[None, :] < counts[:, None], raw_starts, LEN)
    return (tiles.astype(jnp.int32), starts.astype(jnp.int32))


def draw_tiles_per_image(key, part):
    layout = doc_layout(key)
    return layout[0]


def draw_image_start(key, part):
    layout = doc_layout(key)
    return layout[1]


def draw_tile_owner(key, part):
    key = jax.random.fold_in(key, 11)
    doc_keys = jax.random.split(key, NDOC)
    shard_count = SLOTS // NDOC

    def one_doc(doc_key):
        return jax.random.permutation(doc_key, shard_count)[:MAXT]
    return jax.vmap(one_doc)(doc_keys).astype(jnp.int32)


def draw_q_gain(key, part):
    key = jax.random.fold_in(key, 7)
    return jax.random.uniform(key, (HD,), jnp.float32, 1.4, 2.2)


def draw_k_gain(key, part):
    key = jax.random.fold_in(key, 8)
    return jax.random.uniform(key, (HD,), jnp.float32, 1.4, 2.2)


def block_scale(own_key, extent, cuts, least, high):
    level = 1.0
    for axis_at, blocks in cuts:
        steps = jax.random.uniform(jax.random.fold_in(jax.random.fold_in(own_key, 6), axis_at), (blocks,), jnp.float32, least / len(cuts), high / len(cuts))
        level = level * jnp.repeat(jnp.exp(steps), extent[axis_at] // blocks).reshape((-1,) + (1,) * (len(extent) - 1 - axis_at))
    return level


def scatter_about(stream_key, dims, width, bound, cuts=(), kind=jnp.bfloat16):
    drawn = jax.random.normal(stream_key, dims, jnp.float32) * width
    if len(cuts) > 0:
        drawn = block_scale(stream_key, dims, cuts, -0.22, 0.18) * drawn
    return jnp.clip(drawn, min=-bound, max=bound).astype(kind)


def setup_inputs(seed: int = 0) -> dict:
    splits = jax.random.split(jax.random.key(seed), 12)
    return {
        "text": scatter_about(splits[0], (TOKENS, D), 1.0, 6.0, ((0, 128),)),
        "norm_gain": jnp.clip(1.0 + 0.18 * jax.random.normal(splits[1], (D,), jnp.float32), 0.1, 1.9),
        "q_weight": scatter_about(splits[2], (D, HQ * HD), D ** -0.5, 0.09375, ((0, 32),)),
        "k_weight": scatter_about(splits[3], (D, HK * HD), D ** -0.5, 0.09375, ((0, 32),)),
        "v_weight": scatter_about(splits[4], (D, HK * HD), D ** -0.5, 0.09375, ((0, 32),)),
        "q_gain": draw_q_gain(jax.random.fold_in(splits[11], 71), 0),
        "k_gain": draw_k_gain(jax.random.fold_in(splits[11], 71), 0),
        "vision": scatter_about(splits[7], (SLOTS, TILE, D), 1.0, 6.0, ((0, 128),)),
        "tiles_per_image": draw_tiles_per_image(jax.random.fold_in(splits[11], 71), 0),
        "image_start": draw_image_start(jax.random.fold_in(splits[11], 71), 0),
        "tile_owner": draw_tile_owner(jax.random.fold_in(splits[11], 71), 0),
    }


def head_norm(values, gain):
    return values * lax.rsqrt(lax.optimization_barrier(jnp.mean(values * values, axis=-1, keepdims=True)) + 1e-05) * gain

def tile_spans(tile_counts, starts, length):
    slots = tile_counts.shape[0]
    most_tiles = MAXT
    span_ends = jnp.concatenate([starts[1:], jnp.full((1,), length, jnp.int32)])
    offsets = jnp.cumsum(tile_counts) - tile_counts
    tile_total = jnp.sum(tile_counts)
    tile_ids = jnp.arange(most_tiles, dtype=jnp.int32)
    image_of = lax.optimization_barrier(jnp.sum((offsets[None, :] <= tile_ids[:, None]).astype(jnp.int32), axis=1)) - 1
    member = jnp.arange(slots, dtype=jnp.int32)[None, :] == image_of[:, None]
    tile_low = lax.optimization_barrier(jnp.sum(jnp.where(member, starts[None, :], 0), axis=1))
    tile_high = lax.optimization_barrier(jnp.sum(jnp.where(member, span_ends[None, :], 0), axis=1))
    return (tile_low, tile_high, tile_ids < tile_total)

def attend_block(query, gathered, allowed):
    row_count, heads_q, head_dim = query.shape
    most_tiles, tile_len, double_width = gathered.shape
    kv_width = double_width // 2
    heads_kv = kv_width // head_dim
    group = heads_q // heads_kv
    score_scale = 1.0 / head_dim ** 0.5
    head_outputs = []
    for kv_head in range(heads_kv):
        query_head = query[:, kv_head * group:(kv_head + 1) * group, :].reshape(row_count * group, head_dim)
        key_head = gathered[:, :, kv_head * head_dim:(kv_head + 1) * head_dim].reshape(most_tiles * tile_len, head_dim)
        value_head = gathered[:, :, kv_width + kv_head * head_dim:kv_width + (kv_head + 1) * head_dim].reshape(most_tiles * tile_len, head_dim)
        scores = lax.dot_general(query_head, key_head, (((1,), (1,)), ((), ())), preferred_element_type=jnp.float32) * score_scale
        scores = scores.reshape(row_count, group, most_tiles, tile_len)
        usable = allowed[:, None, :, None]
        row_max = lax.optimization_barrier(jnp.max(jnp.where(usable, scores, -1e+30), axis=(2, 3), keepdims=True))
        probs = jnp.where(usable, jnp.exp(scores - row_max), 0.0)
        weight_sum = lax.optimization_barrier(jnp.sum(probs, axis=(2, 3)))
        probs_low = probs.astype(jnp.bfloat16).reshape(row_count * group, most_tiles * tile_len)
        numer = jnp.dot(probs_low, value_head, preferred_element_type=jnp.float32).reshape(row_count, group, head_dim)
        head_outputs.append((numer / jnp.maximum(weight_sum, 1.0)[..., None]).reshape(row_count, group * head_dim))
    return jnp.concatenate(head_outputs, axis=1).astype(jnp.bfloat16)

def reference(text, norm_gain, q_weight, k_weight, v_weight, q_gain, k_gain, vision, tiles_per_image, image_start, tile_owner):
    both_weights = jnp.concatenate([k_weight, v_weight], axis=1)
    kv_width = HK * HD
    outputs = []
    for doc_index in range(NDOC):
        doc_text = text[doc_index * LEN:(doc_index + 1) * LEN].astype(jnp.float32)
        normed = (doc_text * lax.rsqrt(lax.optimization_barrier(jnp.mean(doc_text * doc_text, axis=-1, keepdims=True)) + 1e-05) * norm_gain).astype(jnp.bfloat16)
        query_all = jnp.dot(normed, q_weight, preferred_element_type=jnp.float32).reshape(LEN, HQ, HD)
        query_all = head_norm(query_all, q_gain).astype(jnp.bfloat16)
        tile_low, tile_high, tile_valid = tile_spans(tiles_per_image[doc_index], image_start[doc_index], LEN)
        keyval_list = []
        for tile_slot in range(MAXT):
            slot_index = (doc_index * N_SEQ + tile_owner[doc_index, tile_slot]).astype(jnp.int32)
            tile_rows = lax.dynamic_index_in_dim(vision, slot_index, 0, keepdims=False)
            projected = jnp.dot(tile_rows, both_weights, preferred_element_type=jnp.float32)
            key_rows = head_norm(projected[:, :kv_width].reshape(TILE, HK, HD), k_gain).astype(jnp.bfloat16).reshape(TILE, kv_width)
            value_rows = projected[:, kv_width:].astype(jnp.bfloat16)
            keyval_list.append(jnp.concatenate([key_rows, value_rows], axis=1))
        gathered = jnp.stack(keyval_list)
        positions = jnp.arange(LEN, dtype=jnp.int32).reshape(N_SEQ, TOK_DEV)
        blocks = query_all.reshape(N_SEQ, TOK_DEV, HQ, HD)

        def one_block(pair):
            block_query, block_pos = pair
            allowed = tile_valid[None, :] & (block_pos[:, None] >= tile_low[None, :]) & (block_pos[:, None] < tile_high[None, :])
            return attend_block(block_query, gathered, allowed)
        outputs.append(lax.map(one_block, (blocks, positions)).reshape(LEN, HQ * HD))
    return jnp.concatenate(outputs, axis=0)
```

```python
import functools

import jax
import jax.numpy as jnp
from jax import lax
from jax.experimental import pallas as pl
from jax.experimental.pallas import tpu as pltpu
from jax.sharding import Mesh
from jax.sharding import PartitionSpec as P

SEQ = ("y", "x", "c")
PLANE = ("y", "x")
PARTS = 8
ROWS = 208
HALF = 4 * ROWS
NONE = -1e30
MASKED = -2e30
LOG2E = 1.4426950408889634


def tile_spans(tile_counts, starts, length, most_tiles):
    slots = tile_counts.shape[0]
    span_ends = jnp.concatenate([starts[1:], jnp.full((1,), length, jnp.int32)])
    offsets = jnp.cumsum(tile_counts) - tile_counts
    tile_total = jnp.sum(tile_counts)
    tile_ids = jnp.arange(most_tiles, dtype=jnp.int32)
    image_of = jnp.sum((offsets[None, :] <= tile_ids[:, None]).astype(jnp.int32), axis=1) - 1
    member = jnp.arange(slots, dtype=jnp.int32)[None, :] == image_of[:, None]
    tile_low = jnp.sum(jnp.where(member, starts[None, :], 0), axis=1)
    tile_high = jnp.sum(jnp.where(member, span_ends[None, :], 0), axis=1)
    return (tile_low, tile_high, tile_ids < tile_total)


def norm_rows(values, gain):
    return values * lax.rsqrt(jnp.mean(values * values, axis=-1, keepdims=True) + 1e-05) * gain


def kv_kernel(tile_ref, weight_ref, gain_ref, out_ref, acc_ref):
    step = pl.program_id(0)
    part = jnp.dot(tile_ref[...], weight_ref[...], preferred_element_type=jnp.float32)

    @pl.when(step == 0)
    def _():
        acc_ref[...] = part

    @pl.when(step > 0)
    def _():
        acc_ref[...] += part

    @pl.when(step == pl.num_programs(0) - 1)
    def _():
        for y in range(4):
            for h in range(4):
                block = acc_ref[y * ROWS : (y + 1) * ROWS, h * 256 : (h + 1) * 256]
                out_ref[y * 4 + h, :, :128] = norm_rows(block[:, :128], gain_ref[...]).astype(jnp.bfloat16)
                out_ref[y * 4 + h, :, 128:] = block[:, 128:].astype(jnp.bfloat16)


def project_kv(tile_half, weights, k_gain):
    depth, width = weights.shape
    chunk = 512
    return pl.pallas_call(
        kv_kernel,
        grid=(depth // chunk,),
        in_specs=[
            pl.BlockSpec((HALF, chunk), lambda i: (0, i)),
            pl.BlockSpec((chunk, width), lambda i: (i, 0)),
            pl.BlockSpec((1, 128), lambda i: (0, 0)),
        ],
        out_specs=pl.BlockSpec((16, ROWS, 256), lambda i: (0, 0, 0)),
        out_shape=jax.ShapeDtypeStruct((16, ROWS, 256), jnp.bfloat16),
        scratch_shapes=[pltpu.VMEM((HALF, width), jnp.float32)],
        compiler_params=pltpu.CompilerParams(vmem_limit_bytes=40 * 2**20),
        cost_estimate=pl.CostEstimate(
            flops=2 * HALF * depth * width, bytes_accessed=2 * (HALF + width) * depth, transcendentals=0
        ),
        name="kv_projection",
    )(tile_half, weights, k_gain)


def attend_kernel(tile_len, meta_ref, q_ref, kv_ref, out_ref, m_ref, l_ref, acc_ref):
    block, tile = pl.program_id(0), pl.program_id(1)
    heads = q_ref.shape[2] // 128
    keys = PARTS * ROWS
    tail = keys - 128
    factor = LOG2E / 128**0.5

    @pl.when(tile == 0)
    def _():
        m_ref[...] = jnp.full_like(m_ref, NONE)
        l_ref[...] = jnp.zeros_like(l_ref)
        acc_ref[...] = jnp.zeros_like(acc_ref)

    low, high, first = meta_ref[tile], meta_ref[4 + tile], meta_ref[8 + block]
    rows = q_ref.shape[1]
    some = (low < first + rows) & (high > first)
    every = (low <= first) & (high >= first + rows)

    def step(partial):
        kv = kv_ref[...].reshape(keys, 256)
        key, value = kv[:, :128], kv[:, 128:]
        for g in range(heads):
            scores = lax.dot_general(
                q_ref[0, :, g * 128 : (g + 1) * 128],
                key,
                (((1,), (1,)), ((), ())),
                preferred_element_type=jnp.float32,
            )
            if partial:
                at = first + lax.broadcasted_iota(jnp.int32, (rows, 1), 0)
                scores = jnp.where((at >= low) & (at < high), scores, MASKED)
            at_key = tail + lax.broadcasted_iota(jnp.int32, (rows, 128), 1)
            last = jnp.where(at_key < tile_len, scores[:, tail:], MASKED)
            scores = jnp.concatenate([scores[:, :tail], last], axis=1)
            m_old = m_ref[g]
            m_new = jnp.maximum(m_old, jnp.max(scores, axis=1, keepdims=True))
            probs = jnp.exp2((scores - m_new) * factor)
            alpha = jnp.exp2((m_old - m_new) * factor)
            m_ref[g] = m_new
            l_ref[g] = l_ref[g] * alpha + jnp.sum(probs, axis=1, keepdims=True)
            acc_ref[g] = acc_ref[g] * alpha + jnp.dot(
                probs.astype(jnp.bfloat16), value, preferred_element_type=jnp.float32
            )

    pl.when(every)(lambda: step(False))
    pl.when(some & jnp.logical_not(every))(lambda: step(True))

    @pl.when(tile == pl.num_programs(1) - 1)
    def _():
        for g in range(heads):
            out_ref[0, :, g * 128 : (g + 1) * 128] = (acc_ref[g] / jnp.maximum(l_ref[g], 1.0)).astype(jnp.bfloat16)


def attend(query, keyvals, meta, tile_len):
    blocks, rows, width = query.shape
    tiles = keyvals.shape[1]
    heads = width // 128
    return pl.pallas_call(
        functools.partial(attend_kernel, tile_len),
        grid_spec=pltpu.PrefetchScalarGridSpec(
            num_scalar_prefetch=1,
            grid=(blocks, tiles),
            in_specs=[
                pl.BlockSpec((1, rows, width), lambda b, j, meta: (b, 0, 0)),
                pl.BlockSpec((PARTS, 1, ROWS, 256), lambda b, j, meta: (0, j, 0, 0)),
            ],
            out_specs=pl.BlockSpec((1, rows, width), lambda b, j, meta: (b, 0, 0)),
            scratch_shapes=[
                pltpu.VMEM((heads, rows, 1), jnp.float32),
                pltpu.VMEM((heads, rows, 1), jnp.float32),
                pltpu.VMEM((heads, rows, 128), jnp.float32),
            ],
        ),
        out_shape=jax.ShapeDtypeStruct(query.shape, jnp.bfloat16),
        compiler_params=pltpu.CompilerParams(vmem_limit_bytes=40 * 2**20),
        name="attention",
    )(meta, query, keyvals)


def local(
    text,
    norm_gain,
    q_weight,
    k_weight,
    v_weight,
    q_gain,
    k_gain,
    vision,
    tiles_per_image,
    image_start,
    tile_owner,
):
    row_count = text.shape[0]
    head_dim = q_gain.shape[0]
    heads_kv = k_weight.shape[1] // head_dim
    tile_rows = vision[0]
    tile_len = tile_rows.shape[0]
    most_tiles = tile_owner.shape[1]
    length = row_count * lax.axis_size(SEQ)
    at_doc, at_y, at_x, at_core = (lax.axis_index(a) for a in ("z", "y", "x", "c"))

    by_head = [
        w[:, h * head_dim : (h + 1) * head_dim] for h in range(heads_kv) for w in (k_weight, v_weight)
    ]
    kv_weights = lax.all_gather(jnp.concatenate(by_head, axis=1), SEQ, axis=0, tiled=True)
    late_q, kv_weights = lax.optimization_barrier((q_weight, kv_weights))
    q_weights = lax.all_gather(late_q, SEQ, axis=0, tiled=True)

    totals = jnp.sum(tiles_per_image, axis=1)
    valid = jnp.arange(most_tiles, dtype=jnp.int32)[None, :] < totals[:, None]
    owned = jnp.any(
        (tile_owner[:, :, None] == jnp.arange(lax.axis_size(SEQ), dtype=jnp.int32)) & valid[:, :, None], axis=1
    )
    owned = owned.reshape(owned.shape[0], -1, 2)
    crowded = jnp.any(owned[:, :, 0] & owned[:, :, 1])
    picked = jnp.arange(tiles_per_image.shape[0], dtype=jnp.int32) == at_doc
    tile_counts = jnp.sum(jnp.where(picked[:, None], tiles_per_image, 0), axis=0)
    starts = jnp.sum(jnp.where(picked[:, None], image_start, 0), axis=0)
    owners = jnp.sum(jnp.where(picked[:, None], tile_owner, 0), axis=0)
    first_core = jnp.any(owned & picked[:, None, None], axis=0)[:, 0]
    tile_low, tile_high, tile_valid = tile_spans(tile_counts, starts, length, most_tiles)
    tile_low = jnp.where(tile_valid, tile_low, 2 * length)
    tile_high = jnp.where(tile_valid, tile_high, 0)

    upper = tile_rows[:HALF]
    lower = jnp.pad(tile_rows[HALF:], ((0, 2 * HALF - tile_len), (0, 0)))
    mine = jnp.where(at_core == 0, upper, lower)
    other = lax.ppermute(jnp.where(at_core == 0, lower, upper), "c", [(0, 1), (1, 0)])
    chip_first = jnp.sum(
        jnp.where(jnp.arange(first_core.shape[0]) == at_y * 4 + at_x, first_core.astype(jnp.int32), 0)
    )
    source = 1 - chip_first
    halves = (jnp.where(at_core == source, mine, other), jnp.where(at_core == 1, mine, other))
    gain_row = k_gain.reshape(1, head_dim)
    chip_of = owners // 2
    turn = jnp.where((owners % 2 == 1) & first_core[chip_of], 1, 0)

    def spread(rounds):
        def run():
            pieces = [project_kv(halves[r], kv_weights, gain_row) for r in range(rounds)]
            pieces = pieces[0][:, None] if rounds == 1 else jnp.stack(pieces, axis=1)
            got = lax.all_to_all(pieces, PLANE, 0, 0, tiled=True)
            at_turn = turn if rounds > 1 else jnp.zeros_like(turn)
            return jnp.stack([got[chip_of[j], at_turn[j]] for j in range(most_tiles)])

        return run

    chosen = lax.cond(crowded, spread(2), spread(1))
    keyvals = lax.all_gather(chosen, ("y", "c"), axis=0)

    text_wide = text.astype(jnp.float32)
    normed = norm_rows(text_wide, norm_gain).astype(jnp.bfloat16)
    query = jnp.dot(normed, q_weights, preferred_element_type=jnp.float32)
    query = norm_rows(query.reshape(row_count, -1, head_dim), q_gain).astype(jnp.bfloat16)
    query = query.reshape(row_count, heads_kv, -1).transpose(1, 0, 2)
    query = lax.all_to_all(query, "x", 0, 0, tiled=True)

    blocks = ((at_y * 4 + jnp.arange(4, dtype=jnp.int32)) * 2 + at_core) * row_count
    meta = jnp.concatenate([tile_low, tile_high, blocks]).astype(jnp.int32)
    context = attend(query, keyvals, meta, tile_len)
    context = lax.all_to_all(context, "x", 0, 0, tiled=True)
    return context.transpose(1, 0, 2).reshape(row_count, -1)


def solution(mesh):
    grid = Mesh(mesh.devices.reshape(4, 4, 4, 2), ("z", "y", "x", "c"))
    rows = ("z", "y", "x", "c")
    return jax.shard_map(
        local,
        mesh=grid,
        in_specs=(
            P(rows, None),
            P(),
            P(SEQ, None),
            P(SEQ, None),
            P(SEQ, None),
            P(),
            P(),
            P(rows, None, None),
            P(),
            P(),
            P(),
        ),
        out_specs=P(rows, None),
        check_vma=False,
    )
```

```python
import functools

import jax
import jax.numpy as jnp
from jax import lax
from jax.experimental import pallas as pl
from jax.experimental.pallas import tpu as pltpu
from jax.sharding import Mesh
from jax.sharding import PartitionSpec as P

SEQ = ("y", "x", "c")
PLANE = ("y", "x")
PARTS = 8
ROWS = 208
HALF = 4 * ROWS
NONE = -1e30
MASKED = -2e30
LOG2E = 1.4426950408889634


def tile_spans(tile_counts, starts, length, most_tiles):
    slots = tile_counts.shape[0]
    span_ends = jnp.concatenate([starts[1:], jnp.full((1,), length, jnp.int32)])
    offsets = jnp.cumsum(tile_counts) - tile_counts
    tile_total = jnp.sum(tile_counts)
    tile_ids = jnp.arange(most_tiles, dtype=jnp.int32)
    image_of = jnp.sum((offsets[None, :] <= tile_ids[:, None]).astype(jnp.int32), axis=1) - 1
    member = jnp.arange(slots, dtype=jnp.int32)[None, :] == image_of[:, None]
    tile_low = jnp.sum(jnp.where(member, starts[None, :], 0), axis=1)
    tile_high = jnp.sum(jnp.where(member, span_ends[None, :], 0), axis=1)
    return (tile_low, tile_high, tile_ids < tile_total)


def norm_rows(values, gain):
    return values * lax.rsqrt(jnp.mean(values * values, axis=-1, keepdims=True) + 1e-05) * gain


def kv_kernel(tile_ref, weight_ref, gain_ref, out_ref, acc_ref):
    step = pl.program_id(0)
    part = jnp.dot(tile_ref[...], weight_ref[...], preferred_element_type=jnp.float32)

    @pl.when(step == 0)
    def _():
        acc_ref[...] = part

    @pl.when(step > 0)
    def _():
        acc_ref[...] += part

    @pl.when(step == pl.num_programs(0) - 1)
    def _():
        for y in range(4):
            for h in range(4):
                at = slice(y * ROWS, (y + 1) * ROWS)
                keys = norm_rows(acc_ref[at, h * 128 : (h + 1) * 128], gain_ref[...])
                out_ref[y * 4 + h, :, :128] = keys.astype(jnp.bfloat16)
                out_ref[y * 4 + h, :, 128:] = acc_ref[at, (h + 4) * 128 : (h + 5) * 128].astype(jnp.bfloat16)


def project_kv(tile_half, weights, k_gain):
    depth, width = weights.shape
    chunk = 1024
    return pl.pallas_call(
        kv_kernel,
        grid=(depth // chunk,),
        in_specs=[
            pl.BlockSpec((HALF, chunk), lambda i: (0, i)),
            pl.BlockSpec((chunk, width), lambda i: (i, 0)),
            pl.BlockSpec((1, 128), lambda i: (0, 0)),
        ],
        out_specs=pl.BlockSpec((16, ROWS, 256), lambda i: (0, 0, 0)),
        out_shape=jax.ShapeDtypeStruct((16, ROWS, 256), jnp.bfloat16),
        scratch_shapes=[pltpu.VMEM((HALF, width), jnp.float32)],
        compiler_params=pltpu.CompilerParams(vmem_limit_bytes=40 * 2**20),
        cost_estimate=pl.CostEstimate(
            flops=2 * HALF * depth * width, bytes_accessed=2 * (HALF + width) * depth, transcendentals=0
        ),
        name="kv_projection",
    )(tile_half, weights, k_gain)


def attend_kernel(tile_len, meta_ref, q_ref, kv_ref, out_ref, m_ref, l_ref, acc_ref):
    tile = pl.program_id(0)
    blocks, rows, width = q_ref.shape
    heads = width // 128
    keys = PARTS * ROWS
    tail = keys - 128
    factor = LOG2E / 128**0.5
    pairs = heads // 2

    @pl.when(tile == 0)
    def _():
        m_ref[...] = jnp.full_like(m_ref, NONE)
        l_ref[...] = jnp.zeros_like(l_ref)
        acc_ref[...] = jnp.zeros_like(acc_ref)

    low, high = meta_ref[tile], meta_ref[4 + tile]
    some, every = False, True
    for b in range(blocks):
        first = meta_ref[8 + b]
        some = some | ((low < first + rows) & (high > first))
        every = every & (low <= first) & (high >= first + rows)

    def step(partial):
        kv = kv_ref[...].reshape(keys, 256)
        key = kv[:, :128]
        value = jnp.concatenate([kv[:, 128:], jnp.ones((keys, 128), jnp.bfloat16)], axis=1)

        def score(group):
            b, h = group // pairs, group % pairs * 2
            both = [q_ref[b, :, i * 128 : (i + 1) * 128] for i in (h, h + 1)]
            return lax.dot_general(
                jnp.concatenate(both, axis=0), key, (((1,), (1,)), ((), ())), preferred_element_type=jnp.float32
            )

        def soften(group, scores):
            at_key = tail + lax.broadcasted_iota(jnp.int32, (2 * rows, 128), 1)
            last = jnp.where(at_key < tile_len, scores[:, tail:], MASKED)
            scores = jnp.concatenate([scores[:, :tail], last], axis=1)
            if partial:
                at = meta_ref[8 + group // pairs] + lax.broadcasted_iota(jnp.int32, (2 * rows, 1), 0) % rows
                scores = jnp.where((at >= low) & (at < high), scores, MASKED)
            m_old = m_ref[group]
            m_new = jnp.maximum(m_old, jnp.max(scores, axis=1, keepdims=True))
            probs = jnp.exp2((scores - m_new) * factor)
            alpha = jnp.exp2((m_old - m_new) * factor)
            m_ref[group] = m_new
            summed = jnp.dot(probs.astype(jnp.bfloat16), value, preferred_element_type=jnp.float32)
            l_ref[group] = l_ref[group] * alpha + summed[:, 128:129]
            acc_ref[group] = acc_ref[group] * alpha + summed[:, :128]

        scores = score(0)
        for group in range(blocks * pairs):
            ahead = score(group + 1) if group + 1 < blocks * pairs else None
            soften(group, scores)
            scores = ahead

    pl.when(every)(lambda: step(False))
    pl.when(some & jnp.logical_not(every))(lambda: step(True))

    @pl.when(tile == pl.num_programs(0) - 1)
    def _():
        for b in range(blocks):
            for h in range(heads):
                group, at = b * pairs + h // 2, slice(h % 2 * rows, (h % 2 + 1) * rows)
                out_ref[b, :, h * 128 : (h + 1) * 128] = (
                    acc_ref[group, at] / jnp.maximum(l_ref[group, at], 1.0)
                ).astype(jnp.bfloat16)


def attend(query, keyvals, meta, tile_len):
    blocks, rows, width = query.shape
    tiles = keyvals.shape[1]
    groups = blocks * width // 256
    return pl.pallas_call(
        functools.partial(attend_kernel, tile_len),
        grid_spec=pltpu.PrefetchScalarGridSpec(
            num_scalar_prefetch=1,
            grid=(tiles,),
            in_specs=[
                pl.BlockSpec((blocks, rows, width), lambda j, meta: (0, 0, 0)),
                pl.BlockSpec((PARTS, 1, ROWS, 256), lambda j, meta: (0, j, 0, 0)),
            ],
            out_specs=pl.BlockSpec((blocks, rows, width), lambda j, meta: (0, 0, 0)),
            scratch_shapes=[
                pltpu.VMEM((groups, 2 * rows, 1), jnp.float32),
                pltpu.VMEM((groups, 2 * rows, 1), jnp.float32),
                pltpu.VMEM((groups, 2 * rows, 128), jnp.float32),
            ],
        ),
        out_shape=jax.ShapeDtypeStruct(query.shape, jnp.bfloat16),
        compiler_params=pltpu.CompilerParams(vmem_limit_bytes=40 * 2**20),
        name="attention",
    )(meta, query, keyvals)


def query_kernel(*refs):
    text_refs, (core0_ref, core1_ref, gain_ref, out_ref, acc_ref) = refs[:4], refs[4:]
    step = pl.program_id(0)
    text = jnp.concatenate([ref[...] for ref in text_refs], axis=0)
    weights = jnp.stack([core0_ref[...], core1_ref[...]], axis=1).reshape(text.shape[1], -1)
    part = jnp.dot(text, weights, preferred_element_type=jnp.float32)

    @pl.when(step == 0)
    def _():
        acc_ref[...] = part

    @pl.when(step > 0)
    def _():
        acc_ref[...] += part

    @pl.when(step == pl.num_programs(0) - 1)
    def _():
        for b in range(4):
            for h in range(acc_ref.shape[1] // 128):
                block = acc_ref[b * 128 : (b + 1) * 128, h * 128 : (h + 1) * 128]
                out_ref[b, :, h * 128 : (h + 1) * 128] = norm_rows(block, gain_ref[...]).astype(jnp.bfloat16)


def project_query(texts, core_weights, gain):
    rows, depth = texts[0].shape
    chips, share, width = core_weights[0].shape
    chunk = 4
    return pl.pallas_call(
        query_kernel,
        grid=(chips // chunk,),
        in_specs=[pl.BlockSpec((rows, chunk * 2 * share), lambda i: (0, i))] * 4
        + [pl.BlockSpec((chunk, share, width), lambda i: (i, 0, 0))] * 2
        + [pl.BlockSpec((1, 128), lambda i: (0, 0))],
        out_specs=pl.BlockSpec((4, rows, width), lambda i: (0, 0, 0)),
        out_shape=jax.ShapeDtypeStruct((4, rows, width), jnp.bfloat16),
        scratch_shapes=[pltpu.VMEM((4 * rows, width), jnp.float32)],
        compiler_params=pltpu.CompilerParams(vmem_limit_bytes=32 * 2**20),
        cost_estimate=pl.CostEstimate(
            flops=8 * rows * depth * width, bytes_accessed=2 * (4 * rows + width) * depth, transcendentals=0
        ),
        name="query_projection",
    )(*texts, *core_weights, gain)


def local(
    text,
    norm_gain,
    q_weight,
    k_weight,
    v_weight,
    q_gain,
    k_gain,
    vision,
    tiles_per_image,
    image_start,
    tile_owner,
):
    row_count = text.shape[0]
    head_dim = q_gain.shape[0]
    heads_kv = k_weight.shape[1] // head_dim
    tile_rows = vision[0]
    tile_len = tile_rows.shape[0]
    most_tiles = tile_owner.shape[1]
    length = row_count * lax.axis_size(SEQ)
    at_doc, at_y, at_x, at_core = (lax.axis_index(a) for a in ("z", "y", "x", "c"))

    kv_weights = lax.all_gather(jnp.concatenate([k_weight, v_weight], axis=1), SEQ, axis=0, tiled=True)

    totals = jnp.sum(tiles_per_image, axis=1)
    valid = jnp.arange(most_tiles, dtype=jnp.int32)[None, :] < totals[:, None]
    owned = jnp.any(
        (tile_owner[:, :, None] == jnp.arange(lax.axis_size(SEQ), dtype=jnp.int32)) & valid[:, :, None], axis=1
    )
    owned = owned.reshape(owned.shape[0], -1, 2)
    crowded = jnp.any(owned[:, :, 0] & owned[:, :, 1])
    picked = jnp.arange(tiles_per_image.shape[0], dtype=jnp.int32) == at_doc
    tile_counts = jnp.sum(jnp.where(picked[:, None], tiles_per_image, 0), axis=0)
    starts = jnp.sum(jnp.where(picked[:, None], image_start, 0), axis=0)
    owners = jnp.sum(jnp.where(picked[:, None], tile_owner, 0), axis=0)
    first_core = jnp.any(owned & picked[:, None, None], axis=0)[:, 0]
    tile_low, tile_high, tile_valid = tile_spans(tile_counts, starts, length, most_tiles)
    tile_low = jnp.where(tile_valid, tile_low, 2 * length)
    tile_high = jnp.where(tile_valid, tile_high, 0)

    upper = tile_rows[:HALF]
    lower = jnp.pad(tile_rows[HALF:], ((0, 2 * HALF - tile_len), (0, 0)))
    mine = jnp.where(at_core == 0, upper, lower)
    other = lax.ppermute(jnp.where(at_core == 0, lower, upper), "c", [(0, 1), (1, 0)])
    chip_first = jnp.sum(
        jnp.where(jnp.arange(first_core.shape[0]) == at_y * 4 + at_x, first_core.astype(jnp.int32), 0)
    )
    source = 1 - chip_first
    halves = (jnp.where(at_core == source, mine, other), jnp.where(at_core == 1, mine, other))
    gain_row = k_gain.reshape(1, head_dim)
    chip_of = owners // 2
    turn = jnp.where((owners % 2 == 1) & first_core[chip_of], 1, 0)

    def spread(half):
        pieces = project_kv(half, kv_weights, gain_row)
        got = lax.all_to_all(pieces, PLANE, 0, 0, tiled=True)
        return jnp.stack([got[chip_of[j]] for j in range(most_tiles)])

    chosen = spread(halves[0])
    chosen = lax.cond(
        crowded, lambda: jnp.where((turn > 0)[:, None, None], spread(halves[1]), chosen), lambda: chosen
    )
    keyvals = lax.all_gather(chosen, ("y", "c"), axis=0)

    text_wide = text.astype(jnp.float32)
    normed = norm_rows(text_wide, norm_gain).astype(jnp.bfloat16)
    around = [normed] + [
        lax.ppermute(normed, "z", [(i, (i + step) % 4) for i in range(4)]) for step in (1, 2, 3)
    ]
    group_width = q_weight.shape[1] // heads_kv
    share = lax.dynamic_slice_in_dim(q_weight, at_doc * group_width, group_width, 1)
    same_core = lax.all_to_all(jnp.broadcast_to(share, (16,) + share.shape), PLANE, 0, 0, tiled=True)
    other_core = lax.ppermute(same_core, "c", [(0, 1), (1, 0)])
    core_weights = (
        jnp.where(at_core == 0, same_core, other_core),
        jnp.where(at_core == 0, other_core, same_core),
    )
    query = project_query(around, core_weights, q_gain.reshape(1, head_dim))
    query = jnp.stack([query[(at_doc - d) % 4] for d in range(4)])
    query = lax.all_to_all(query, "z", 0, 0, tiled=True)
    query = lax.all_to_all(query, "x", 0, 0, tiled=True)

    blocks = ((at_y * 4 + jnp.arange(4, dtype=jnp.int32)) * 2 + at_core) * row_count
    meta = jnp.concatenate([tile_low, tile_high, blocks]).astype(jnp.int32)
    context = attend(query, keyvals, meta, tile_len)
    context = lax.all_to_all(context, "x", 0, 0, tiled=True)
    return context.transpose(1, 0, 2).reshape(row_count, -1)


def solution(mesh):
    grid = Mesh(mesh.devices.reshape(4, 4, 4, 2), ("z", "y", "x", "c"))
    rows = ("z", "y", "x", "c")
    return jax.shard_map(
        local,
        mesh=grid,
        in_specs=(
            P(rows, None),
            P(),
            P(SEQ, None),
            P(SEQ, None),
            P(SEQ, None),
            P(),
            P(),
            P(rows, None, None),
            P(),
            P(),
            P(),
        ),
        out_specs=P(rows, None),
        check_vma=False,
    )
```

```python
import functools

import jax
import jax.numpy as jnp
from jax import lax
from jax.experimental import pallas as pl
from jax.experimental.pallas import tpu as pltpu
from jax.sharding import Mesh
from jax.sharding import PartitionSpec as P

SEQ = ("y", "x", "c")
PLANE = ("y", "x")
PARTS = 8
ROWS = 208
HALF = 4 * ROWS
NONE = -1e30
MASKED = -2e30
LOG2E = 1.4426950408889634


def tile_spans(tile_counts, starts, length, most_tiles):
    slots = tile_counts.shape[0]
    span_ends = jnp.concatenate([starts[1:], jnp.full((1,), length, jnp.int32)])
    offsets = jnp.cumsum(tile_counts) - tile_counts
    tile_total = jnp.sum(tile_counts)
    tile_ids = jnp.arange(most_tiles, dtype=jnp.int32)
    image_of = jnp.sum((offsets[None, :] <= tile_ids[:, None]).astype(jnp.int32), axis=1) - 1
    member = jnp.arange(slots, dtype=jnp.int32)[None, :] == image_of[:, None]
    tile_low = jnp.sum(jnp.where(member, starts[None, :], 0), axis=1)
    tile_high = jnp.sum(jnp.where(member, span_ends[None, :], 0), axis=1)
    return (tile_low, tile_high, tile_ids < tile_total)


def norm_rows(values, gain):
    return values * lax.rsqrt(jnp.mean(values * values, axis=-1, keepdims=True) + 1e-05) * gain


def kv_kernel(tile_len, meta_ref, own_ref, other_ref, weight_ref, gain_ref, out_ref, acc_ref):
    step = pl.program_id(0)
    core, own = meta_ref[0], meta_ref[1]

    def project(tile_ref):
        part = jnp.dot(tile_ref[...], weight_ref[...], preferred_element_type=jnp.float32)

        @pl.when(step == 0)
        def _():
            acc_ref[...] = part

        @pl.when(step > 0)
        def _():
            acc_ref[...] += part

    pl.when(own == 1)(lambda: project(own_ref))
    pl.when(own == 0)(lambda: project(other_ref))

    @pl.when(step == pl.num_programs(0) - 1)
    def _():
        for y in range(4):
            held = tile_len - core * HALF - y * ROWS
            kept = lax.broadcasted_iota(jnp.int32, (ROWS, 128), 0) < held
            for h in range(4):
                at = slice(y * ROWS, (y + 1) * ROWS)
                keys = acc_ref[at, h * 128 : (h + 1) * 128]
                values = acc_ref[at, (h + 4) * 128 : (h + 5) * 128]
                if y == 3:
                    keys, values = jnp.where(kept, keys, 0.0), jnp.where(kept, values, 0.0)
                out_ref[y * 4 + h, :, :128] = norm_rows(keys, gain_ref[...]).astype(jnp.bfloat16)
                out_ref[y * 4 + h, :, 128:] = values.astype(jnp.bfloat16)


def project_kv(own, other, weights, k_gain, core, use_own):
    tile_len, depth = own.shape
    width = 1024
    chunk = 1024
    meta = jnp.stack([core, use_own]).astype(jnp.int32)
    return pl.pallas_call(
        functools.partial(kv_kernel, tile_len),
        grid_spec=pltpu.PrefetchScalarGridSpec(
            num_scalar_prefetch=1,
            grid=(depth // chunk,),
            in_specs=[
                pl.BlockSpec((HALF, chunk), lambda i, meta: (meta[0], i * meta[1])),
                pl.BlockSpec((HALF, chunk), lambda i, meta: (meta[0], i * (1 - meta[1]))),
                pl.BlockSpec((chunk, width), lambda i, meta: (i, 0)),
                pl.BlockSpec((1, 128), lambda i, meta: (0, 0)),
            ],
            out_specs=pl.BlockSpec((16, ROWS, 256), lambda i, meta: (0, 0, 0)),
            scratch_shapes=[pltpu.VMEM((HALF, width), jnp.float32)],
        ),
        out_shape=jax.ShapeDtypeStruct((16, ROWS, 256), jnp.bfloat16),
        compiler_params=pltpu.CompilerParams(vmem_limit_bytes=40 * 2**20),
        cost_estimate=pl.CostEstimate(
            flops=2 * HALF * depth * width, bytes_accessed=2 * (HALF + width) * depth, transcendentals=0
        ),
        name="kv_projection",
    )(meta, own, other, weights, k_gain)


def attend_kernel(tile_len, meta_ref, q_ref, kv_ref, out_ref, m_ref, l_ref, acc_ref):
    tile = pl.program_id(0)
    blocks, rows, width = q_ref.shape
    heads = width // 128
    keys = PARTS * ROWS
    tail = keys - 128
    factor = LOG2E / 128**0.5
    pairs = heads // 2

    @pl.when(tile == 0)
    def _():
        m_ref[...] = jnp.full_like(m_ref, NONE)
        l_ref[...] = jnp.zeros_like(l_ref)
        acc_ref[...] = jnp.zeros_like(acc_ref)

    low, high = meta_ref[tile], meta_ref[4 + tile]
    some, every = False, True
    for b in range(blocks):
        first = meta_ref[8 + b]
        some = some | ((low < first + rows) & (high > first))
        every = every & (low <= first) & (high >= first + rows)

    def step(partial):
        kv = kv_ref[...].reshape(keys, 256)
        key = kv[:, :128]
        value = jnp.concatenate([kv[:, 128:], jnp.ones((keys, 128), jnp.bfloat16)], axis=1)

        def score(group):
            b, h = group // pairs, group % pairs * 2
            both = [q_ref[b, :, i * 128 : (i + 1) * 128] for i in (h, h + 1)]
            return lax.dot_general(
                jnp.concatenate(both, axis=0), key, (((1,), (1,)), ((), ())), preferred_element_type=jnp.float32
            )

        def soften(group, scores):
            at_key = tail + lax.broadcasted_iota(jnp.int32, (2 * rows, 128), 1)
            last = jnp.where(at_key < tile_len, scores[:, tail:], MASKED)
            scores = jnp.concatenate([scores[:, :tail], last], axis=1)
            if partial:
                at = meta_ref[8 + group // pairs] + lax.broadcasted_iota(jnp.int32, (2 * rows, 1), 0) % rows
                scores = jnp.where((at >= low) & (at < high), scores, MASKED)
            m_old = m_ref[group]
            m_new = jnp.maximum(m_old, jnp.max(scores, axis=1, keepdims=True))
            probs = jnp.exp2((scores - m_new) * factor)
            alpha = jnp.exp2((m_old - m_new) * factor)
            m_ref[group] = m_new
            summed = jnp.dot(probs.astype(jnp.bfloat16), value, preferred_element_type=jnp.float32)
            l_ref[group] = l_ref[group] * alpha + summed[:, 128:129]
            acc_ref[group] = acc_ref[group] * alpha + summed[:, :128]

        scores = score(0)
        for group in range(blocks * pairs):
            ahead = score(group + 1) if group + 1 < blocks * pairs else None
            soften(group, scores)
            scores = ahead

    pl.when(every)(lambda: step(False))
    pl.when(some & jnp.logical_not(every))(lambda: step(True))

    @pl.when(tile == pl.num_programs(0) - 1)
    def _():
        for b in range(blocks):
            for h in range(heads):
                group, at = b * pairs + h // 2, slice(h % 2 * rows, (h % 2 + 1) * rows)
                out_ref[b, :, h * 128 : (h + 1) * 128] = (
                    acc_ref[group, at] / jnp.maximum(l_ref[group, at], 1.0)
                ).astype(jnp.bfloat16)


def attend(query, keyvals, meta, tile_len):
    blocks, rows, width = query.shape
    tiles = keyvals.shape[1]
    groups = blocks * width // 256
    return pl.pallas_call(
        functools.partial(attend_kernel, tile_len),
        grid_spec=pltpu.PrefetchScalarGridSpec(
            num_scalar_prefetch=1,
            grid=(tiles,),
            in_specs=[
                pl.BlockSpec((blocks, rows, width), lambda j, meta: (0, 0, 0)),
                pl.BlockSpec((PARTS, 1, ROWS, 256), lambda j, meta: (0, j, 0, 0)),
            ],
            out_specs=pl.BlockSpec((blocks, rows, width), lambda j, meta: (0, 0, 0)),
            scratch_shapes=[
                pltpu.VMEM((groups, 2 * rows, 1), jnp.float32),
                pltpu.VMEM((groups, 2 * rows, 1), jnp.float32),
                pltpu.VMEM((groups, 2 * rows, 128), jnp.float32),
            ],
        ),
        out_shape=jax.ShapeDtypeStruct(query.shape, jnp.bfloat16),
        compiler_params=pltpu.CompilerParams(vmem_limit_bytes=40 * 2**20),
        name="attention",
    )(meta, query, keyvals)


def query_kernel(text0, text1, text2, text3, weight_ref, gain_ref, out_ref, acc_ref):
    step = pl.program_id(0)
    text = jnp.concatenate([ref[...] for ref in (text0, text1, text2, text3)], axis=0)
    part = jnp.dot(text, weight_ref[...], preferred_element_type=jnp.float32)

    @pl.when(step == 0)
    def _():
        acc_ref[...] = part

    @pl.when(step > 0)
    def _():
        acc_ref[...] += part

    @pl.when(step == pl.num_programs(0) - 1)
    def _():
        for b in range(4):
            for h in range(acc_ref.shape[1] // 128):
                block = acc_ref[b * 128 : (b + 1) * 128, h * 128 : (h + 1) * 128]
                out_ref[b, :, h * 128 : (h + 1) * 128] = norm_rows(block, gain_ref[...]).astype(jnp.bfloat16)


def project_query(texts, weights, gain):
    rows, depth = texts[0].shape
    width = 512
    chunk = 1024
    last = weights.shape[1] // width - 1
    return pl.pallas_call(
        query_kernel,
        grid=(depth // chunk,),
        in_specs=[pl.BlockSpec((rows, chunk), lambda i: (0, i))] * 4
        + [pl.BlockSpec((chunk, width), lambda i: (i, last)), pl.BlockSpec((1, 128), lambda i: (0, 0))],
        out_specs=pl.BlockSpec((4, rows, width), lambda i: (0, 0, 0)),
        out_shape=jax.ShapeDtypeStruct((4, rows, width), jnp.bfloat16),
        scratch_shapes=[pltpu.VMEM((4 * rows, width), jnp.float32)],
        compiler_params=pltpu.CompilerParams(vmem_limit_bytes=32 * 2**20),
        cost_estimate=pl.CostEstimate(
            flops=8 * rows * depth * width, bytes_accessed=2 * (4 * rows + width) * depth, transcendentals=0
        ),
        name="query_projection",
    )(*texts, weights, gain)


def local(
    text,
    norm_gain,
    q_weight,
    k_weight,
    v_weight,
    q_gain,
    k_gain,
    vision,
    tiles_per_image,
    image_start,
    tile_owner,
):
    row_count = text.shape[0]
    head_dim = q_gain.shape[0]
    heads_kv = k_weight.shape[1] // head_dim
    tile_rows = vision[0]
    tile_len = tile_rows.shape[0]
    most_tiles = tile_owner.shape[1]
    length = row_count * lax.axis_size(SEQ)
    at_doc, at_y, at_x, at_core = (lax.axis_index(a) for a in ("z", "y", "x", "c"))

    group_width = q_weight.shape[1] // heads_kv
    q_share = lax.dynamic_slice_in_dim(q_weight, at_doc * group_width, group_width, 1)
    weights = lax.all_gather(jnp.concatenate([k_weight, v_weight, q_share], axis=1), SEQ, axis=0, tiled=True)
    other_rows = lax.ppermute(tile_rows, "c", [(0, 1), (1, 0)])
    text_wide = text.astype(jnp.float32)
    normed = norm_rows(text_wide, norm_gain).astype(jnp.bfloat16)
    around = [normed] + [
        lax.ppermute(normed, "z", [(i, (i + step) % 4) for i in range(4)]) for step in (1, 2, 3)
    ]
    weights, other_rows, *around = lax.optimization_barrier((weights, other_rows, *around))

    totals = jnp.sum(tiles_per_image, axis=1)
    valid = jnp.arange(most_tiles, dtype=jnp.int32)[None, :] < totals[:, None]
    owned = jnp.any(
        (tile_owner[:, :, None] == jnp.arange(lax.axis_size(SEQ), dtype=jnp.int32)) & valid[:, :, None], axis=1
    )
    owned = owned.reshape(owned.shape[0], -1, 2)
    crowded = jnp.any(owned[:, :, 0] & owned[:, :, 1])
    picked = jnp.arange(tiles_per_image.shape[0], dtype=jnp.int32) == at_doc
    tile_counts = jnp.sum(jnp.where(picked[:, None], tiles_per_image, 0), axis=0)
    starts = jnp.sum(jnp.where(picked[:, None], image_start, 0), axis=0)
    owners = jnp.sum(jnp.where(picked[:, None], tile_owner, 0), axis=0)
    first_core = jnp.any(owned & picked[:, None, None], axis=0)[:, 0]
    tile_low, tile_high, tile_valid = tile_spans(tile_counts, starts, length, most_tiles)
    tile_low = jnp.where(tile_valid, tile_low, 2 * length)
    tile_high = jnp.where(tile_valid, tile_high, 0)

    chip_first = jnp.sum(
        jnp.where(jnp.arange(first_core.shape[0]) == at_y * 4 + at_x, first_core.astype(jnp.int32), 0)
    )
    source = 1 - chip_first
    gain_row = k_gain.reshape(1, head_dim)
    chip_of = owners // 2
    turn = jnp.where((owners % 2 == 1) & first_core[chip_of], 1, 0)

    def project(from_core):
        use_own = (at_core == from_core).astype(jnp.int32)
        return project_kv(tile_rows, other_rows, weights, gain_row, at_core, use_own)

    def spread(pieces):
        got = lax.all_to_all(pieces, PLANE, 0, 0, tiled=True)
        return jnp.stack([got[chip_of[j]] for j in range(most_tiles)])

    pieces, weights = lax.optimization_barrier((project(source), weights))
    query = project_query(around, weights, q_gain.reshape(1, head_dim))
    chosen = spread(pieces)
    chosen = lax.cond(
        crowded, lambda: jnp.where((turn > 0)[:, None, None], spread(project(1)), chosen), lambda: chosen
    )
    chosen, query = lax.optimization_barrier((chosen, query))
    keyvals = lax.all_gather(chosen, ("y", "c"), axis=0)
    query = jnp.stack([query[(at_doc - d) % 4] for d in range(4)])
    query = lax.all_to_all(query, "z", 0, 0, tiled=True)
    query = lax.all_to_all(query, "x", 0, 0, tiled=True)

    blocks = ((at_y * 4 + jnp.arange(4, dtype=jnp.int32)) * 2 + at_core) * row_count
    meta = jnp.concatenate([tile_low, tile_high, blocks]).astype(jnp.int32)
    context = attend(query, keyvals, meta, tile_len)
    context = lax.all_to_all(context, "x", 0, 0, tiled=True)
    return context.transpose(1, 0, 2).reshape(row_count, -1)


def solution(mesh):
    grid = Mesh(mesh.devices.reshape(4, 4, 4, 2), ("z", "y", "x", "c"))
    rows = ("z", "y", "x", "c")
    return jax.shard_map(
        local,
        mesh=grid,
        in_specs=(
            P(rows, None),
            P(),
            P(SEQ, None),
            P(SEQ, None),
            P(SEQ, None),
            P(),
            P(),
            P(rows, None, None),
            P(),
            P(),
            P(),
        ),
        out_specs=P(rows, None),
        check_vma=False,
    )
```

```python
import functools

import jax
import jax.numpy as jnp
from jax import lax
from jax.experimental import pallas as pl
from jax.experimental.pallas import tpu as pltpu
from jax.sharding import Mesh
from jax.sharding import PartitionSpec as P

SEQ = ("y", "x", "c")
PLANE = ("y", "x")
PARTS = 8
ROWS = 208
HALF = 4 * ROWS
NONE = -1e30
MASKED = -2e30
LOG2E = 1.4426950408889634


def tile_spans(tile_counts, starts, length, most_tiles):
    slots = tile_counts.shape[0]
    span_ends = jnp.concatenate([starts[1:], jnp.full((1,), length, jnp.int32)])
    offsets = jnp.cumsum(tile_counts) - tile_counts
    tile_total = jnp.sum(tile_counts)
    tile_ids = jnp.arange(most_tiles, dtype=jnp.int32)
    image_of = jnp.sum((offsets[None, :] <= tile_ids[:, None]).astype(jnp.int32), axis=1) - 1
    member = jnp.arange(slots, dtype=jnp.int32)[None, :] == image_of[:, None]
    tile_low = jnp.sum(jnp.where(member, starts[None, :], 0), axis=1)
    tile_high = jnp.sum(jnp.where(member, span_ends[None, :], 0), axis=1)
    return (tile_low, tile_high, tile_ids < tile_total)


def norm_rows(values, gain):
    return values * lax.rsqrt(jnp.mean(values * values, axis=-1, keepdims=True) + 1e-05) * gain


CHUNKS = ((0, 512), (512, 1024), (1024, 2048), (2048, 3072), (3072, 4096))


def kv_kernel(
    tile_len, meta_ref, own_ref, other_ref, own_tail, other_tail, weight_ref, gain_ref, out_ref,
    tile_buf, weight_buf, acc_ref, tile_sem, tail_sem, weight_sem,
):
    core, own = meta_ref[0], meta_ref[1]
    whole = tile_len // 16 * 16 - HALF
    kv_width = weight_buf.shape[1]

    def weight_copy(k):
        low, high = CHUNKS[k]
        at = pl.ds(low, high - low)
        return pltpu.make_async_copy(weight_ref.at[at, pl.ds(0, kv_width)], weight_buf.at[at], weight_sem.at[k])

    def tile_copies(k, source, tail, lower):
        low, high = CHUNKS[k]
        at = pl.ds(low, high - low)
        if not lower:
            rows = pl.ds(0, HALF)
            return [pltpu.make_async_copy(source.at[rows, at], tile_buf.at[rows, at], tile_sem.at[k])]
        return [
            pltpu.make_async_copy(
                source.at[pl.ds(HALF, whole), at], tile_buf.at[pl.ds(0, whole), at], tile_sem.at[k]
            ),
            pltpu.make_async_copy(tail.at[:, at], tile_buf.at[pl.ds(whole, 16), at], tail_sem.at[k]),
        ]

    for k in range(len(CHUNKS)):
        weight_copy(k).start()
        for from_own, source, tail in ((1, own_ref, own_tail), (0, other_ref, other_tail)):
            for lower in (0, 1):

                @pl.when((own == from_own) & (core == lower))
                def _(k=k, source=source, tail=tail, lower=lower):
                    for copy in tile_copies(k, source, tail, lower):
                        copy.start()

    for k, (low, high) in enumerate(CHUNKS):
        weight_copy(k).wait()
        for lower in (0, 1):

            @pl.when(core == lower)
            def _(k=k, lower=lower):
                for copy in tile_copies(k, own_ref, own_tail, lower):
                    copy.wait()

        part = jnp.dot(tile_buf[:, low:high], weight_buf[low:high, :], preferred_element_type=jnp.float32)
        if k == 0:
            acc_ref[...] = part
        else:
            acc_ref[...] += part

    for y in range(4):
        held = tile_len - core * HALF - y * ROWS
        kept = lax.broadcasted_iota(jnp.int32, (ROWS, 128), 0) < held
        for h in range(4):
            at = slice(y * ROWS, (y + 1) * ROWS)
            keys = acc_ref[at, h * 128 : (h + 1) * 128]
            values = acc_ref[at, (h + 4) * 128 : (h + 5) * 128]
            if y == 3:
                keys, values = jnp.where(kept, keys, 0.0), jnp.where(kept, values, 0.0)
            out_ref[y * 4 + h, :, :128] = norm_rows(keys, gain_ref[...]).astype(jnp.bfloat16)
            out_ref[y * 4 + h, :, 128:] = values.astype(jnp.bfloat16)


def project_kv(own, other, weights, k_gain, core, use_own):
    tile_len, depth = own.shape
    width = 1024
    whole = tile_len // 16 * 16
    tails = [jnp.pad(tile[whole:], ((0, 16 - tile_len + whole), (0, 0))) for tile in (own, other)]
    meta = jnp.stack([core, use_own]).astype(jnp.int32)
    chunks = len(CHUNKS)
    return pl.pallas_call(
        functools.partial(kv_kernel, tile_len),
        in_specs=[pl.BlockSpec(memory_space=pltpu.SMEM)]
        + [pl.BlockSpec(memory_space=pl.ANY)] * 5
        + [pl.BlockSpec(memory_space=pltpu.VMEM)],
        out_specs=pl.BlockSpec(memory_space=pltpu.VMEM),
        out_shape=jax.ShapeDtypeStruct((16, ROWS, 256), jnp.bfloat16),
        scratch_shapes=[
            pltpu.VMEM((HALF, depth), jnp.bfloat16),
            pltpu.VMEM((depth, width), jnp.bfloat16),
            pltpu.VMEM((HALF, width), jnp.float32),
            pltpu.SemaphoreType.DMA((chunks,)),
            pltpu.SemaphoreType.DMA((chunks,)),
            pltpu.SemaphoreType.DMA((chunks,)),
        ],
        compiler_params=pltpu.CompilerParams(vmem_limit_bytes=40 * 2**20),
        cost_estimate=pl.CostEstimate(
            flops=2 * HALF * depth * width, bytes_accessed=2 * (HALF + width) * depth, transcendentals=0
        ),
        name="kv_projection",
    )(meta, own, other, *tails, weights, k_gain)


def attend_kernel(pad, meta_ref, q_ref, *refs):
    part_refs, (out_ref, m_ref, l_ref, acc_ref) = refs[:PARTS], refs[PARTS:]
    tile = pl.program_id(0)
    blocks, rows, width = q_ref.shape
    heads = width // 128
    keys = PARTS * ROWS
    factor = LOG2E / 128**0.5
    pairs = heads // 2

    @pl.when(tile == 0)
    def _():
        m_ref[...] = jnp.full_like(m_ref, NONE)
        l_ref[...] = jnp.zeros_like(l_ref)
        acc_ref[...] = jnp.zeros_like(acc_ref)

    low, high = meta_ref[tile], meta_ref[4 + tile]
    some, every = False, True
    for b in range(blocks):
        first = meta_ref[8 + b]
        some = some | ((low < first + rows) & (high > first))
        every = every & (low <= first) & (high >= first + rows)

    def step(partial):
        kv = jnp.concatenate([ref[0] for ref in part_refs], axis=0)
        row = lax.broadcasted_iota(jnp.int32, (keys, 128), 0)
        padding = (row >= meta_ref[12]) & (row < meta_ref[12] + pad)
        lane = lax.broadcasted_iota(jnp.int32, (keys, 128), 1) == 0
        bias = jnp.where(padding & lane, MASKED, 0.0).astype(jnp.bfloat16)
        key = jnp.concatenate([kv[:, :128], bias], axis=1)
        value = jnp.concatenate([kv[:, 128:], jnp.ones((keys, 128), jnp.bfloat16)], axis=1)
        one = (lax.broadcasted_iota(jnp.int32, (2 * rows, 128), 1) == 0).astype(jnp.bfloat16)

        def score(group):
            b, h = group // pairs, group % pairs * 2
            both = [q_ref[b, :, i * 128 : (i + 1) * 128] for i in (h, h + 1)]
            deep = jnp.concatenate([jnp.concatenate(both, axis=0), one], axis=1)
            return lax.dot_general(deep, key, (((1,), (1,)), ((), ())), preferred_element_type=jnp.float32)

        def soften(group, scores):
            if partial:
                at = meta_ref[8 + group // pairs] + lax.broadcasted_iota(jnp.int32, (2 * rows, 1), 0) % rows
                scores = jnp.where((at >= low) & (at < high), scores, MASKED)
            m_old = m_ref[group]
            m_new = jnp.maximum(m_old, jnp.max(scores, axis=1, keepdims=True))
            probs = jnp.exp2((scores - m_new) * factor)
            alpha = jnp.exp2((m_old - m_new) * factor)
            m_ref[group] = m_new
            summed = jnp.dot(probs.astype(jnp.bfloat16), value, preferred_element_type=jnp.float32)
            l_ref[group] = l_ref[group] * alpha + summed[:, 128:129]
            acc_ref[group] = acc_ref[group] * alpha + summed[:, :128]

        scores = score(0)
        for group in range(blocks * pairs):
            ahead = score(group + 1) if group + 1 < blocks * pairs else None
            soften(group, scores)
            scores = ahead

    pl.when(every)(lambda: step(False))
    pl.when(some & jnp.logical_not(every))(lambda: step(True))

    @pl.when(tile == pl.num_programs(0) - 1)
    def _():
        for b in range(blocks):
            for h in range(heads):
                group, at = b * pairs + h // 2, slice(h % 2 * rows, (h % 2 + 1) * rows)
                out_ref[b, :, h * 128 : (h + 1) * 128] = (
                    acc_ref[group, at] / jnp.maximum(l_ref[group, at], 1.0)
                ).astype(jnp.bfloat16)


def attend(query, parts, meta, pad):
    blocks, rows, width = query.shape
    tiles = parts[0].shape[0]
    groups = blocks * width // 256
    return pl.pallas_call(
        functools.partial(attend_kernel, pad),
        grid_spec=pltpu.PrefetchScalarGridSpec(
            num_scalar_prefetch=1,
            grid=(tiles,),
            in_specs=[
                pl.BlockSpec((blocks, rows, width), lambda j, meta: (0, 0, 0)),
            ]
            + [pl.BlockSpec((1, ROWS, 256), lambda j, meta: (j, 0, 0))] * PARTS,
            out_specs=pl.BlockSpec((blocks, rows, width), lambda j, meta: (0, 0, 0)),
            scratch_shapes=[
                pltpu.VMEM((groups, 2 * rows, 1), jnp.float32),
                pltpu.VMEM((groups, 2 * rows, 1), jnp.float32),
                pltpu.VMEM((groups, 2 * rows, 128), jnp.float32),
            ],
        ),
        out_shape=jax.ShapeDtypeStruct(query.shape, jnp.bfloat16),
        compiler_params=pltpu.CompilerParams(vmem_limit_bytes=40 * 2**20),
        name="attention",
    )(meta, query, *parts)


def query_kernel(text0, text1, text2, text3, weight_ref, gain_ref, out_ref, acc_ref):
    step = pl.program_id(0)
    text = jnp.concatenate([ref[...] for ref in (text0, text1, text2, text3)], axis=0)
    part = jnp.dot(text, weight_ref[...], preferred_element_type=jnp.float32)

    @pl.when(step == 0)
    def _():
        acc_ref[...] = part

    @pl.when(step > 0)
    def _():
        acc_ref[...] += part

    @pl.when(step == pl.num_programs(0) - 1)
    def _():
        for b in range(4):
            for h in range(acc_ref.shape[1] // 128):
                block = acc_ref[b * 128 : (b + 1) * 128, h * 128 : (h + 1) * 128]
                out_ref[b, :, h * 128 : (h + 1) * 128] = norm_rows(block, gain_ref[...]).astype(jnp.bfloat16)


def project_query(texts, weights, gain):
    rows, depth = texts[0].shape
    width = 512
    chunk = 1024
    last = weights.shape[1] // width - 1
    return pl.pallas_call(
        query_kernel,
        grid=(depth // chunk,),
        in_specs=[pl.BlockSpec((rows, chunk), lambda i: (0, i))] * 4
        + [pl.BlockSpec((chunk, width), lambda i: (i, last)), pl.BlockSpec((1, 128), lambda i: (0, 0))],
        out_specs=pl.BlockSpec((4, rows, width), lambda i: (0, 0, 0)),
        out_shape=jax.ShapeDtypeStruct((4, rows, width), jnp.bfloat16),
        scratch_shapes=[pltpu.VMEM((4 * rows, width), jnp.float32)],
        compiler_params=pltpu.CompilerParams(vmem_limit_bytes=32 * 2**20),
        cost_estimate=pl.CostEstimate(
            flops=8 * rows * depth * width, bytes_accessed=2 * (4 * rows + width) * depth, transcendentals=0
        ),
        name="query_projection",
    )(*texts, weights, gain)


def local(
    text,
    norm_gain,
    q_weight,
    k_weight,
    v_weight,
    q_gain,
    k_gain,
    vision,
    tiles_per_image,
    image_start,
    tile_owner,
):
    row_count = text.shape[0]
    head_dim = q_gain.shape[0]
    heads_kv = k_weight.shape[1] // head_dim
    tile_rows = vision[0]
    tile_len = tile_rows.shape[0]
    most_tiles = tile_owner.shape[1]
    length = row_count * lax.axis_size(SEQ)
    at_doc, at_y, at_x, at_core = (lax.axis_index(a) for a in ("z", "y", "x", "c"))

    group_width = q_weight.shape[1] // heads_kv
    q_share = lax.dynamic_slice_in_dim(q_weight, at_doc * group_width, group_width, 1)
    weights = lax.all_gather(jnp.concatenate([k_weight, v_weight, q_share], axis=1), SEQ, axis=0, tiled=True)
    other_rows = lax.ppermute(tile_rows, "c", [(0, 1), (1, 0)])
    text_wide = text.astype(jnp.float32)
    normed = norm_rows(text_wide, norm_gain).astype(jnp.bfloat16)
    around = [normed] + [
        lax.ppermute(normed, "z", [(i, (i + step) % 4) for i in range(4)]) for step in (1, 2, 3)
    ]
    weights, other_rows, *around = lax.optimization_barrier((weights, other_rows, *around))

    totals = jnp.sum(tiles_per_image, axis=1)
    valid = jnp.arange(most_tiles, dtype=jnp.int32)[None, :] < totals[:, None]
    owned = jnp.any(
        (tile_owner[:, :, None] == jnp.arange(lax.axis_size(SEQ), dtype=jnp.int32)) & valid[:, :, None], axis=1
    )
    owned = owned.reshape(owned.shape[0], -1, 2)
    crowded = jnp.any(owned[:, :, 0] & owned[:, :, 1])
    picked = jnp.arange(tiles_per_image.shape[0], dtype=jnp.int32) == at_doc
    tile_counts = jnp.sum(jnp.where(picked[:, None], tiles_per_image, 0), axis=0)
    starts = jnp.sum(jnp.where(picked[:, None], image_start, 0), axis=0)
    owners = jnp.sum(jnp.where(picked[:, None], tile_owner, 0), axis=0)
    first_core = jnp.any(owned & picked[:, None, None], axis=0)[:, 0]
    tile_low, tile_high, tile_valid = tile_spans(tile_counts, starts, length, most_tiles)
    tile_low = jnp.where(tile_valid, tile_low, 2 * length)
    tile_high = jnp.where(tile_valid, tile_high, 0)

    chip_first = jnp.sum(
        jnp.where(jnp.arange(first_core.shape[0]) == at_y * 4 + at_x, first_core.astype(jnp.int32), 0)
    )
    source = 1 - chip_first
    gain_row = k_gain.reshape(1, head_dim)
    chip_of = owners // 2
    turn = jnp.where((owners % 2 == 1) & first_core[chip_of], 1, 0)

    def project(from_core):
        use_own = (at_core == from_core).astype(jnp.int32)
        return project_kv(tile_rows, other_rows, weights, gain_row, at_core, use_own)

    pieces, weights = lax.optimization_barrier((project(source), weights))

    def spread(rounds):
        def run():
            if rounds == 1:
                sent = pieces[:, None]
            else:
                sent = jnp.stack([pieces, project(1)], axis=1)
            got = lax.all_to_all(sent, PLANE, 0, 0, tiled=True)
            query = project_query(around, weights, q_gain.reshape(1, head_dim))
            query = jnp.stack([query[(at_doc - d) % 4] for d in range(4)])
            query = lax.all_to_all(query, "z", 0, 0, tiled=True)
            got, query = lax.optimization_barrier((got, query))
            at_turn = turn if rounds > 1 else jnp.zeros_like(turn)
            return jnp.stack([got[chip_of[j], at_turn[j]] for j in range(most_tiles)]), query

        return run

    chosen, query = lax.cond(crowded, spread(2), spread(1))
    query = lax.all_to_all(query, "x", 0, 0, tiled=True)

    after, before = [(i, (i + 1) % 4) for i in range(4)], [(i, (i + 3) % 4) for i in range(4)]
    swap = [(0, 1), (1, 0)]
    from_before, from_after = lax.ppermute(chosen, "y", after), lax.ppermute(chosen, "y", before)
    half = most_tiles // 2
    opposite = jnp.concatenate(
        [lax.ppermute(from_before[:half], "y", after), lax.ppermute(from_after[half:], "y", before)], axis=0
    )
    parts = [chosen, from_before, from_after, opposite]
    parts += [lax.ppermute(part, "c", swap) for part in parts]
    last_slot = jnp.array([1, 3, 2, 0], jnp.int32)[at_y]
    last_part = jnp.where(at_core == 1, last_slot, last_slot + 4)
    pad = 2 * HALF - tile_len
    pad_row = (last_part + 1) * ROWS - pad

    blocks = ((at_y * 4 + jnp.arange(4, dtype=jnp.int32)) * 2 + at_core) * row_count
    meta = jnp.concatenate([tile_low, tile_high, blocks, pad_row[None]]).astype(jnp.int32)
    context = attend(query, parts, meta, pad)
    context = lax.all_to_all(context, "x", 0, 0, tiled=True)
    return context.transpose(1, 0, 2).reshape(row_count, -1)


def solution(mesh):
    grid = Mesh(mesh.devices.reshape(4, 4, 4, 2), ("z", "y", "x", "c"))
    rows = ("z", "y", "x", "c")
    return jax.shard_map(
        local,
        mesh=grid,
        in_specs=(
            P(rows, None),
            P(),
            P(SEQ, None),
            P(SEQ, None),
            P(SEQ, None),
            P(),
            P(),
            P(rows, None, None),
            P(),
            P(),
            P(),
        ),
        out_specs=P(rows, None),
        check_vma=False,
    )
```

```python
import functools

import jax
import jax.numpy as jnp
from jax import lax
from jax.experimental import pallas as pl
from jax.experimental.pallas import tpu as pltpu
from jax.sharding import Mesh
from jax.sharding import PartitionSpec as P

SEQ = ("y", "x", "c")
PLANE = ("y", "x")
PARTS = 8
ROWS = 208
HALF = 4 * ROWS
NONE = -1e30
MASKED = -2e30
LOG2E = 1.4426950408889634


def tile_spans(tile_counts, starts, length, most_tiles):
    slots = tile_counts.shape[0]
    span_ends = jnp.concatenate([starts[1:], jnp.full((1,), length, jnp.int32)])
    offsets = jnp.cumsum(tile_counts) - tile_counts
    tile_total = jnp.sum(tile_counts)
    tile_ids = jnp.arange(most_tiles, dtype=jnp.int32)
    image_of = jnp.sum((offsets[None, :] <= tile_ids[:, None]).astype(jnp.int32), axis=1) - 1
    member = jnp.arange(slots, dtype=jnp.int32)[None, :] == image_of[:, None]
    tile_low = jnp.sum(jnp.where(member, starts[None, :], 0), axis=1)
    tile_high = jnp.sum(jnp.where(member, span_ends[None, :], 0), axis=1)
    return (tile_low, tile_high, tile_ids < tile_total)


def ring(step):
    return [(i, (i + step) % 4) for i in range(4)]


def norm_rows(values, gain):
    return values * lax.rsqrt(jnp.mean(values * values, axis=-1, keepdims=True) + 1e-05) * gain


CHUNKS = ((0, 512), (512, 1024), (1024, 2048), (2048, 3072), (3072, 4096))


def kv_kernel(
    tile_len, meta_ref, own_ref, other_ref, own_tail, other_tail, weight_ref, gain_ref, out_ref,
    tile_buf, weight_buf, acc_ref, tile_sem, tail_sem, weight_sem,
):
    core, own = meta_ref[0], meta_ref[1]
    whole = tile_len // 16 * 16 - HALF
    kv_width = weight_buf.shape[1]

    def weight_copy(k):
        low, high = CHUNKS[k]
        at = pl.ds(low, high - low)
        return pltpu.make_async_copy(weight_ref.at[at, pl.ds(0, kv_width)], weight_buf.at[at], weight_sem.at[k])

    def tile_copies(k, source, tail, lower):
        low, high = CHUNKS[k]
        at = pl.ds(low, high - low)
        if not lower:
            rows = pl.ds(0, HALF)
            return [pltpu.make_async_copy(source.at[rows, at], tile_buf.at[rows, at], tile_sem.at[k])]
        return [
            pltpu.make_async_copy(
                source.at[pl.ds(HALF, whole), at], tile_buf.at[pl.ds(0, whole), at], tile_sem.at[k]
            ),
            pltpu.make_async_copy(tail.at[:, at], tile_buf.at[pl.ds(whole, 16), at], tail_sem.at[k]),
        ]

    for k in range(len(CHUNKS)):
        weight_copy(k).start()
        for from_own, source, tail in ((1, own_ref, own_tail), (0, other_ref, other_tail)):
            for lower in (0, 1):

                @pl.when((own == from_own) & (core == lower))
                def _(k=k, source=source, tail=tail, lower=lower):
                    for copy in tile_copies(k, source, tail, lower):
                        copy.start()

    for k, (low, high) in enumerate(CHUNKS):
        weight_copy(k).wait()
        for lower in (0, 1):

            @pl.when(core == lower)
            def _(k=k, lower=lower):
                for copy in tile_copies(k, own_ref, own_tail, lower):
                    copy.wait()

        part = jnp.dot(tile_buf[:, low:high], weight_buf[low:high, :], preferred_element_type=jnp.float32)
        if k == 0:
            acc_ref[...] = part
        else:
            acc_ref[...] += part

    for y in range(4):
        held = tile_len - core * HALF - y * ROWS
        kept = lax.broadcasted_iota(jnp.int32, (ROWS, 128), 0) < held
        for h in range(4):
            at = slice(y * ROWS, (y + 1) * ROWS)
            keys = acc_ref[at, h * 128 : (h + 1) * 128]
            values = acc_ref[at, (h + 4) * 128 : (h + 5) * 128]
            if y == 3:
                keys, values = jnp.where(kept, keys, 0.0), jnp.where(kept, values, 0.0)
            out_ref[y * 4 + h, :, :128] = norm_rows(keys, gain_ref[...]).astype(jnp.bfloat16)
            out_ref[y * 4 + h, :, 128:] = values.astype(jnp.bfloat16)


def project_kv(own, other, weights, k_gain, core, use_own):
    tile_len, depth = own.shape
    width = 1024
    whole = tile_len // 16 * 16
    tails = [jnp.pad(tile[whole:], ((0, 16 - tile_len + whole), (0, 0))) for tile in (own, other)]
    meta = jnp.stack([core, use_own]).astype(jnp.int32)
    chunks = len(CHUNKS)
    return pl.pallas_call(
        functools.partial(kv_kernel, tile_len),
        in_specs=[pl.BlockSpec(memory_space=pltpu.SMEM)]
        + [pl.BlockSpec(memory_space=pl.ANY)] * 5
        + [pl.BlockSpec(memory_space=pltpu.VMEM)],
        out_specs=pl.BlockSpec(memory_space=pltpu.VMEM),
        out_shape=jax.ShapeDtypeStruct((16, ROWS, 256), jnp.bfloat16),
        scratch_shapes=[
            pltpu.VMEM((HALF, depth), jnp.bfloat16),
            pltpu.VMEM((depth, width), jnp.bfloat16),
            pltpu.VMEM((HALF, width), jnp.float32),
            pltpu.SemaphoreType.DMA((chunks,)),
            pltpu.SemaphoreType.DMA((chunks,)),
            pltpu.SemaphoreType.DMA((chunks,)),
        ],
        compiler_params=pltpu.CompilerParams(vmem_limit_bytes=40 * 2**20),
        cost_estimate=pl.CostEstimate(
            flops=2 * HALF * depth * width, bytes_accessed=2 * (HALF + width) * depth, transcendentals=0
        ),
        name="kv_projection",
    )(meta, own, other, *tails, weights, k_gain)


def attend_kernel(pad, meta_ref, q_ref, *refs):
    part_refs, (out_ref, m_ref, l_ref, acc_ref) = refs[:-4], refs[-4:]
    tile = pl.program_id(0)
    blocks, rows, width = q_ref.shape
    heads = width // 128
    keys = PARTS * ROWS
    factor = LOG2E / 128**0.5
    pairs = heads // 2

    @pl.when(tile == 0)
    def _():
        m_ref[...] = jnp.full_like(m_ref, NONE)
        l_ref[...] = jnp.zeros_like(l_ref)
        acc_ref[...] = jnp.zeros_like(acc_ref)

    low, high = meta_ref[tile], meta_ref[4 + tile]
    some, every = False, True
    for b in range(blocks):
        first = meta_ref[8 + b]
        some = some | ((low < first + rows) & (high > first))
        every = every & (low <= first) & (high >= first + rows)

    def step(partial):
        held = []
        for own, before, after, low_tiles, high_tiles in (part_refs[:5], part_refs[5:]):
            opposite = jnp.where(tile < 2, low_tiles[0], high_tiles[0])
            held += [own[0], before[0], after[0], opposite]
        kv = jnp.concatenate(held, axis=0)
        row = lax.broadcasted_iota(jnp.int32, (keys, 128), 0)
        padding = (row >= meta_ref[12]) & (row < meta_ref[12] + pad)
        lane = lax.broadcasted_iota(jnp.int32, (keys, 128), 1) == 0
        bias = jnp.where(padding & lane, MASKED, 0.0).astype(jnp.bfloat16)
        key = jnp.concatenate([kv[:, :128], bias], axis=1)
        value = jnp.concatenate([kv[:, 128:], jnp.ones((keys, 128), jnp.bfloat16)], axis=1)
        one = (lax.broadcasted_iota(jnp.int32, (2 * rows, 128), 1) == 0).astype(jnp.bfloat16)

        def score(group):
            b, h = group // pairs, group % pairs * 2
            both = [q_ref[b, :, i * 128 : (i + 1) * 128] for i in (h, h + 1)]
            deep = jnp.concatenate([jnp.concatenate(both, axis=0), one], axis=1)
            return lax.dot_general(deep, key, (((1,), (1,)), ((), ())), preferred_element_type=jnp.float32)

        def soften(group, scores):
            if partial:
                at = meta_ref[8 + group // pairs] + lax.broadcasted_iota(jnp.int32, (2 * rows, 1), 0) % rows
                scores = jnp.where((at >= low) & (at < high), scores, MASKED)
            m_old = m_ref[group]
            m_new = jnp.maximum(m_old, jnp.max(scores, axis=1, keepdims=True))
            probs = jnp.exp2((scores - m_new) * factor)
            alpha = jnp.exp2((m_old - m_new) * factor)
            m_ref[group] = m_new
            summed = jnp.dot(probs.astype(jnp.bfloat16), value, preferred_element_type=jnp.float32)
            l_ref[group] = l_ref[group] * alpha + summed[:, 128:129]
            acc_ref[group] = acc_ref[group] * alpha + summed[:, :128]

        scores = score(0)
        for group in range(blocks * pairs):
            ahead = score(group + 1) if group + 1 < blocks * pairs else None
            soften(group, scores)
            scores = ahead

    pl.when(every)(lambda: step(False))
    pl.when(some & jnp.logical_not(every))(lambda: step(True))

    @pl.when(tile == pl.num_programs(0) - 1)
    def _():
        for b in range(blocks):
            for h in range(heads):
                group, at = b * pairs + h // 2, slice(h % 2 * rows, (h % 2 + 1) * rows)
                out_ref[b, :, h * 128 : (h + 1) * 128] = (
                    acc_ref[group, at] / jnp.maximum(l_ref[group, at], 1.0)
                ).astype(jnp.bfloat16)


def attend(query, parts, meta, pad):
    blocks, rows, width = query.shape
    tiles = parts[0].shape[0]
    groups = blocks * width // 256
    return pl.pallas_call(
        functools.partial(attend_kernel, pad),
        grid_spec=pltpu.PrefetchScalarGridSpec(
            num_scalar_prefetch=1,
            grid=(tiles,),
            in_specs=[
                pl.BlockSpec((blocks, rows, width), lambda j, meta: (0, 0, 0)),
            ]
            + (
                [pl.BlockSpec((1, ROWS, 256), lambda j, meta: (j, 0, 0))] * 3
                + [pl.BlockSpec((1, ROWS, 256), lambda j, meta: (jnp.minimum(j, 1), 0, 0))]
                + [pl.BlockSpec((1, ROWS, 256), lambda j, meta: (jnp.maximum(j - 2, 0), 0, 0))]
            )
            * 2,
            out_specs=pl.BlockSpec((blocks, rows, width), lambda j, meta: (0, 0, 0)),
            scratch_shapes=[
                pltpu.VMEM((groups, 2 * rows, 1), jnp.float32),
                pltpu.VMEM((groups, 2 * rows, 1), jnp.float32),
                pltpu.VMEM((groups, 2 * rows, 128), jnp.float32),
            ],
        ),
        out_shape=jax.ShapeDtypeStruct(query.shape, jnp.bfloat16),
        compiler_params=pltpu.CompilerParams(vmem_limit_bytes=40 * 2**20),
        name="attention",
    )(meta, query, *parts)


def query_kernel(text0, text1, text2, text3, weight_ref, gain_ref, out_ref, acc_ref):
    step = pl.program_id(0)
    text = jnp.concatenate([ref[...] for ref in (text0, text1, text2, text3)], axis=0)
    part = jnp.dot(text, weight_ref[...], preferred_element_type=jnp.float32)

    @pl.when(step == 0)
    def _():
        acc_ref[...] = part

    @pl.when(step > 0)
    def _():
        acc_ref[...] += part

    @pl.when(step == pl.num_programs(0) - 1)
    def _():
        for b in range(4):
            for h in range(acc_ref.shape[1] // 128):
                block = acc_ref[b * 128 : (b + 1) * 128, h * 128 : (h + 1) * 128]
                out_ref[b, :, h * 128 : (h + 1) * 128] = norm_rows(block, gain_ref[...]).astype(jnp.bfloat16)


def project_query(texts, weights, gain):
    rows, depth = texts[0].shape
    width = 512
    chunk = 1024
    last = weights.shape[1] // width - 1
    return pl.pallas_call(
        query_kernel,
        grid=(depth // chunk,),
        in_specs=[pl.BlockSpec((rows, chunk), lambda i: (0, i))] * 4
        + [pl.BlockSpec((chunk, width), lambda i: (i, last)), pl.BlockSpec((1, 128), lambda i: (0, 0))],
        out_specs=pl.BlockSpec((4, rows, width), lambda i: (0, 0, 0)),
        out_shape=jax.ShapeDtypeStruct((4, rows, width), jnp.bfloat16),
        scratch_shapes=[pltpu.VMEM((4 * rows, width), jnp.float32)],
        compiler_params=pltpu.CompilerParams(vmem_limit_bytes=32 * 2**20),
        cost_estimate=pl.CostEstimate(
            flops=8 * rows * depth * width, bytes_accessed=2 * (4 * rows + width) * depth, transcendentals=0
        ),
        name="query_projection",
    )(*texts, weights, gain)


def local(
    text,
    norm_gain,
    q_weight,
    k_weight,
    v_weight,
    q_gain,
    k_gain,
    vision,
    tiles_per_image,
    image_start,
    tile_owner,
):
    row_count = text.shape[0]
    head_dim = q_gain.shape[0]
    heads_kv = k_weight.shape[1] // head_dim
    tile_rows = vision[0]
    tile_len = tile_rows.shape[0]
    most_tiles = tile_owner.shape[1]
    length = row_count * lax.axis_size(SEQ)
    at_doc, at_y, at_x, at_core = (lax.axis_index(a) for a in ("z", "y", "x", "c"))

    group_width = q_weight.shape[1] // heads_kv
    q_share = lax.dynamic_slice_in_dim(q_weight, at_doc * group_width, group_width, 1)
    weights = lax.all_gather(jnp.concatenate([k_weight, v_weight, q_share], axis=1), SEQ, axis=0, tiled=True)
    other_rows = lax.ppermute(tile_rows, "c", [(0, 1), (1, 0)])
    text_wide = text.astype(jnp.float32)
    normed = norm_rows(text_wide, norm_gain).astype(jnp.bfloat16)
    around = [normed] + [
        lax.ppermute(normed, "z", ring(step)) for step in (1, 2, 3)
    ]
    weights, other_rows, *around = lax.optimization_barrier((weights, other_rows, *around))

    totals = jnp.sum(tiles_per_image, axis=1)
    valid = jnp.arange(most_tiles, dtype=jnp.int32)[None, :] < totals[:, None]
    owned = jnp.any(
        (tile_owner[:, :, None] == jnp.arange(lax.axis_size(SEQ), dtype=jnp.int32)) & valid[:, :, None], axis=1
    )
    owned = owned.reshape(owned.shape[0], -1, 2)
    crowded = jnp.any(owned[:, :, 0] & owned[:, :, 1])
    picked = jnp.arange(tiles_per_image.shape[0], dtype=jnp.int32) == at_doc
    tile_counts = jnp.sum(jnp.where(picked[:, None], tiles_per_image, 0), axis=0)
    starts = jnp.sum(jnp.where(picked[:, None], image_start, 0), axis=0)
    owners = jnp.sum(jnp.where(picked[:, None], tile_owner, 0), axis=0)
    first_core = jnp.any(owned & picked[:, None, None], axis=0)[:, 0]
    tile_low, tile_high, tile_valid = tile_spans(tile_counts, starts, length, most_tiles)
    tile_low = jnp.where(tile_valid, tile_low, 2 * length)
    tile_high = jnp.where(tile_valid, tile_high, 0)

    chip_first = jnp.sum(
        jnp.where(jnp.arange(first_core.shape[0]) == at_y * 4 + at_x, first_core.astype(jnp.int32), 0)
    )
    source = 1 - chip_first
    gain_row = k_gain.reshape(1, head_dim)
    chip_of = owners // 2
    turn = jnp.where((owners % 2 == 1) & first_core[chip_of], 1, 0)

    def project(from_core):
        use_own = (at_core == from_core).astype(jnp.int32)
        return project_kv(tile_rows, other_rows, weights, gain_row, at_core, use_own)

    pieces, weights = lax.optimization_barrier((project(source), weights))

    def spread(rounds):
        def run():
            if rounds == 1:
                sent = pieces[:, None]
            else:
                sent = jnp.stack([pieces, project(1)], axis=1)
            got = lax.all_to_all(sent, PLANE, 0, 0, tiled=True)
            query = project_query(around, weights, q_gain.reshape(1, head_dim))
            mine = [query[0]] + [lax.ppermute(query[k], "z", ring(-k)) for k in (1, 2, 3)]
            mine = jnp.stack(mine)
            query = [mine[(at_x + s - at_doc) % 4] for s in range(4)]
            query = jnp.stack([query[0]] + [lax.ppermute(query[s], "x", ring(s)) for s in (1, 2, 3)])
            got, query = lax.optimization_barrier((got, query))
            at_turn = turn if rounds > 1 else jnp.zeros_like(turn)
            return jnp.stack([got[chip_of[j], at_turn[j]] for j in range(most_tiles)]), query

        return run

    chosen, query = lax.cond(crowded, spread(2), spread(1))

    after, before, swap = ring(1), ring(-1), [(0, 1), (1, 0)]
    from_before, from_after = lax.ppermute(chosen, "y", after), lax.ppermute(chosen, "y", before)
    half = most_tiles // 2
    opposite = [lax.ppermute(from_before[:half], "y", after), lax.ppermute(from_after[half:], "y", before)]
    parts = [chosen, from_before, from_after, *opposite]
    parts += [lax.ppermute(part, "c", swap) for part in parts]
    last_slot = jnp.array([1, 3, 2, 0], jnp.int32)[at_y]
    last_part = jnp.where(at_core == 1, last_slot, last_slot + 4)
    pad = 2 * HALF - tile_len
    pad_row = (last_part + 1) * ROWS - pad

    token_x = (at_x - jnp.arange(4, dtype=jnp.int32)) % 4
    blocks = ((at_y * 4 + token_x) * 2 + at_core) * row_count
    meta = jnp.concatenate([tile_low, tile_high, blocks, pad_row[None]]).astype(jnp.int32)
    context = attend(query, parts, meta, pad)
    context = [context[0]] + [lax.ppermute(context[k], "x", ring(-k)) for k in (1, 2, 3)]
    context = jnp.stack(context)
    return jnp.concatenate([context[(h - at_x) % 4] for h in range(heads_kv)], axis=1)


def solution(mesh):
    grid = Mesh(mesh.devices.reshape(4, 4, 4, 2), ("z", "y", "x", "c"))
    rows = ("z", "y", "x", "c")
    return jax.shard_map(
        local,
        mesh=grid,
        in_specs=(
            P(rows, None),
            P(),
            P(SEQ, None),
            P(SEQ, None),
            P(SEQ, None),
            P(),
            P(),
            P(rows, None, None),
            P(),
            P(),
            P(),
        ),
        out_specs=P(rows, None),
        check_vma=False,
    )
```

```python
import functools

import jax
import jax.numpy as jnp
from jax import lax
from jax.experimental import pallas as pl
from jax.experimental.pallas import tpu as pltpu
from jax.sharding import Mesh
from jax.sharding import PartitionSpec as P

SEQ = ("y", "x", "c")
PLANE = ("y", "x")
PARTS = 8
ROWS = 208
HALF = 4 * ROWS
NONE = -1e30
MASKED = -2e30
LOG2E = 1.4426950408889634


def tile_spans(tile_counts, starts, length, most_tiles):
    slots = tile_counts.shape[0]
    span_ends = jnp.concatenate([starts[1:], jnp.full((1,), length, jnp.int32)])
    offsets = jnp.cumsum(tile_counts) - tile_counts
    tile_total = jnp.sum(tile_counts)
    tile_ids = jnp.arange(most_tiles, dtype=jnp.int32)
    image_of = jnp.sum((offsets[None, :] <= tile_ids[:, None]).astype(jnp.int32), axis=1) - 1
    member = jnp.arange(slots, dtype=jnp.int32)[None, :] == image_of[:, None]
    tile_low = jnp.sum(jnp.where(member, starts[None, :], 0), axis=1)
    tile_high = jnp.sum(jnp.where(member, span_ends[None, :], 0), axis=1)
    return (tile_low, tile_high, tile_ids < tile_total)


def ring(step):
    return [(i, (i + step) % 4) for i in range(4)]


def norm_rows(values, gain):
    return values * lax.rsqrt(jnp.mean(values * values, axis=-1, keepdims=True) + 1e-05) * gain


CHUNKS = ((0, 512), (512, 1024), (1024, 2048), (2048, 3072), (3072, 4096))


def kv_kernel(
    tile_len, meta_ref, own_ref, other_ref, own_tail, other_tail, weight_ref, gain_ref, out_ref,
    tile_buf, weight_buf, acc_ref, tile_sem, tail_sem, weight_sem,
):
    core, own = meta_ref[0], meta_ref[1]
    whole = tile_len // 16 * 16 - HALF
    kv_width = weight_buf.shape[1]

    def weight_copy(k):
        low, high = CHUNKS[k]
        at = pl.ds(low, high - low)
        return pltpu.make_async_copy(weight_ref.at[at, pl.ds(0, kv_width)], weight_buf.at[at], weight_sem.at[k])

    def tile_copies(k, source, tail, lower):
        low, high = CHUNKS[k]
        at = pl.ds(low, high - low)
        if not lower:
            rows = pl.ds(0, HALF)
            return [pltpu.make_async_copy(source.at[rows, at], tile_buf.at[rows, at], tile_sem.at[k])]
        return [
            pltpu.make_async_copy(
                source.at[pl.ds(HALF, whole), at], tile_buf.at[pl.ds(0, whole), at], tile_sem.at[k]
            ),
            pltpu.make_async_copy(tail.at[:, at], tile_buf.at[pl.ds(whole, 16), at], tail_sem.at[k]),
        ]

    for k in range(len(CHUNKS)):
        weight_copy(k).start()
        for from_own, source, tail in ((1, own_ref, own_tail), (0, other_ref, other_tail)):
            for lower in (0, 1):

                @pl.when((own == from_own) & (core == lower))
                def _(k=k, source=source, tail=tail, lower=lower):
                    for copy in tile_copies(k, source, tail, lower):
                        copy.start()

    for k, (low, high) in enumerate(CHUNKS):
        weight_copy(k).wait()
        for lower in (0, 1):

            @pl.when(core == lower)
            def _(k=k, lower=lower):
                for copy in tile_copies(k, own_ref, own_tail, lower):
                    copy.wait()

        part = jnp.dot(tile_buf[:, low:high], weight_buf[low:high, :], preferred_element_type=jnp.float32)
        if k == 0:
            acc_ref[...] = part
        else:
            acc_ref[...] += part

    for y in range(4):
        held = tile_len - core * HALF - y * ROWS
        kept = lax.broadcasted_iota(jnp.int32, (ROWS, 128), 0) < held
        for h in range(4):
            at = slice(y * ROWS, (y + 1) * ROWS)
            keys = acc_ref[at, h * 128 : (h + 1) * 128]
            values = acc_ref[at, (h + 4) * 128 : (h + 5) * 128]
            if y == 3:
                keys, values = jnp.where(kept, keys, 0.0), jnp.where(kept, values, 0.0)
            out_ref[y * 4 + h, :, :128] = norm_rows(keys, gain_ref[...]).astype(jnp.bfloat16)
            out_ref[y * 4 + h, :, 128:] = values.astype(jnp.bfloat16)


def ragged_end(tile):
    whole = tile.shape[0] // 16 * 16
    return jnp.pad(tile[whole:], ((0, 16 - tile.shape[0] + whole), (0, 0)))


def project_kv(own, other, tails, weights, k_gain, core, use_own):
    tile_len, depth = own.shape
    width = 1024
    meta = jnp.stack([core, use_own]).astype(jnp.int32)
    chunks = len(CHUNKS)
    return pl.pallas_call(
        functools.partial(kv_kernel, tile_len),
        in_specs=[pl.BlockSpec(memory_space=pltpu.SMEM)]
        + [pl.BlockSpec(memory_space=pl.ANY)] * 5
        + [pl.BlockSpec(memory_space=pltpu.VMEM)],
        out_specs=pl.BlockSpec(memory_space=pltpu.VMEM),
        out_shape=jax.ShapeDtypeStruct((16, ROWS, 256), jnp.bfloat16),
        scratch_shapes=[
            pltpu.VMEM((HALF, depth), jnp.bfloat16),
            pltpu.VMEM((depth, width), jnp.bfloat16),
            pltpu.VMEM((HALF, width), jnp.float32),
            pltpu.SemaphoreType.DMA((chunks,)),
            pltpu.SemaphoreType.DMA((chunks,)),
            pltpu.SemaphoreType.DMA((chunks,)),
        ],
        compiler_params=pltpu.CompilerParams(vmem_limit_bytes=40 * 2**20),
        cost_estimate=pl.CostEstimate(
            flops=2 * HALF * depth * width, bytes_accessed=2 * (HALF + width) * depth, transcendentals=0
        ),
        name="kv_projection",
    )(meta, own, other, *tails, weights, k_gain)


def attend_kernel(pad, meta_ref, q_ref, *refs):
    part_refs, (out_ref, m_ref, l_ref, acc_ref) = refs[:-4], refs[-4:]
    tile = pl.program_id(0)
    blocks, rows, width = q_ref.shape
    heads = width // 128
    keys = PARTS * ROWS
    factor = LOG2E / 128**0.5
    pairs = heads // 2

    @pl.when(tile == 0)
    def _():
        m_ref[...] = jnp.full_like(m_ref, NONE)
        l_ref[...] = jnp.zeros_like(l_ref)
        acc_ref[...] = jnp.zeros_like(acc_ref)

    low, high = meta_ref[tile], meta_ref[4 + tile]
    some, every = False, True
    for b in range(blocks):
        first = meta_ref[8 + b]
        some = some | ((low < first + rows) & (high > first))
        every = every & (low <= first) & (high >= first + rows)

    def step(partial):
        held = []
        for own, before, after, low_tiles, high_tiles in (part_refs[:5], part_refs[5:]):
            opposite = jnp.where(tile < 2, low_tiles[0], high_tiles[0])
            held += [own[0], before[0], after[0], opposite]
        kv = jnp.concatenate(held, axis=0)
        row = lax.broadcasted_iota(jnp.int32, (keys, 128), 0)
        padding = (row >= meta_ref[8 + blocks]) & (row < meta_ref[8 + blocks] + pad)
        lane = lax.broadcasted_iota(jnp.int32, (keys, 128), 1) == 0
        bias = jnp.where(padding & lane, MASKED, 0.0).astype(jnp.bfloat16)
        key = jnp.concatenate([kv[:, :128], bias], axis=1)
        value = jnp.concatenate([kv[:, 128:], jnp.ones((keys, 128), jnp.bfloat16)], axis=1)
        one = (lax.broadcasted_iota(jnp.int32, (2 * rows, 128), 1) == 0).astype(jnp.bfloat16)

        def score(group):
            b, h = group // pairs, group % pairs * 2
            both = [q_ref[b, :, i * 128 : (i + 1) * 128] for i in (h, h + 1)]
            deep = jnp.concatenate([jnp.concatenate(both, axis=0), one], axis=1)
            return lax.dot_general(deep, key, (((1,), (1,)), ((), ())), preferred_element_type=jnp.float32)

        def soften(group, scores):
            if partial:
                at = meta_ref[8 + group // pairs] + lax.broadcasted_iota(jnp.int32, (2 * rows, 1), 0) % rows
                scores = jnp.where((at >= low) & (at < high), scores, MASKED)
            m_old = m_ref[group]
            m_new = jnp.maximum(m_old, jnp.max(scores, axis=1, keepdims=True))
            probs = jnp.exp2((scores - m_new) * factor)
            alpha = jnp.exp2((m_old - m_new) * factor)
            m_ref[group] = m_new
            summed = jnp.dot(probs.astype(jnp.bfloat16), value, preferred_element_type=jnp.float32)
            l_ref[group] = l_ref[group] * alpha + summed[:, 128:129]
            acc_ref[group] = acc_ref[group] * alpha + summed[:, :128]

        scores = score(0)
        for group in range(blocks * pairs):
            ahead = score(group + 1) if group + 1 < blocks * pairs else None
            soften(group, scores)
            scores = ahead

    pl.when(every)(lambda: step(False))
    pl.when(some & jnp.logical_not(every))(lambda: step(True))

    @pl.when(tile == pl.num_programs(0) - 1)
    def _():
        for b in range(blocks):
            for h in range(heads):
                group, at = b * pairs + h // 2, slice(h % 2 * rows, (h % 2 + 1) * rows)
                out_ref[b, :, h * 128 : (h + 1) * 128] = (
                    acc_ref[group, at] / jnp.maximum(l_ref[group, at], 1.0)
                ).astype(jnp.bfloat16)


def attend(query, parts, meta, pad):
    blocks, rows, width = query.shape
    tiles = parts[0].shape[0]
    groups = blocks * width // 256
    return pl.pallas_call(
        functools.partial(attend_kernel, pad),
        grid_spec=pltpu.PrefetchScalarGridSpec(
            num_scalar_prefetch=1,
            grid=(tiles,),
            in_specs=[
                pl.BlockSpec((blocks, rows, width), lambda j, meta: (0, 0, 0)),
            ]
            + (
                [pl.BlockSpec((1, ROWS, 256), lambda j, meta: (j, 0, 0))] * 3
                + [pl.BlockSpec((1, ROWS, 256), lambda j, meta: (jnp.minimum(j, 1), 0, 0))]
                + [pl.BlockSpec((1, ROWS, 256), lambda j, meta: (jnp.maximum(j - 2, 0), 0, 0))]
            )
            * 2,
            out_specs=pl.BlockSpec((blocks, rows, width), lambda j, meta: (0, 0, 0)),
            scratch_shapes=[
                pltpu.VMEM((groups, 2 * rows, 1), jnp.float32),
                pltpu.VMEM((groups, 2 * rows, 1), jnp.float32),
                pltpu.VMEM((groups, 2 * rows, 128), jnp.float32),
            ],
        ),
        out_shape=jax.ShapeDtypeStruct(query.shape, jnp.bfloat16),
        compiler_params=pltpu.CompilerParams(vmem_limit_bytes=40 * 2**20),
        cost_estimate=pl.CostEstimate(
            flops=8 * blocks * rows * width * tiles * PARTS * ROWS,
            bytes_accessed=512 * tiles * PARTS * ROWS,
            transcendentals=blocks * rows * width // 128 * tiles * PARTS * ROWS,
        ),
        name="attention",
    )(meta, query, *parts)


def query_kernel(text0, text1, text2, text3, weight_ref, gain_ref, out_ref, acc_ref):
    step = pl.program_id(0)
    text = jnp.concatenate([ref[...] for ref in (text0, text1, text2, text3)], axis=0)
    part = jnp.dot(text, weight_ref[...], preferred_element_type=jnp.float32)

    @pl.when(step == 0)
    def _():
        acc_ref[...] = part

    @pl.when(step > 0)
    def _():
        acc_ref[...] += part

    @pl.when(step == pl.num_programs(0) - 1)
    def _():
        for b in range(4):
            for h in range(acc_ref.shape[1] // 128):
                block = acc_ref[b * 128 : (b + 1) * 128, h * 128 : (h + 1) * 128]
                out_ref[b, :, h * 128 : (h + 1) * 128] = norm_rows(block, gain_ref[...]).astype(jnp.bfloat16)


def project_query(texts, weights, gain):
    rows, depth = texts[0].shape
    width = 512
    chunk = 1024
    last = weights.shape[1] // width - 1
    return pl.pallas_call(
        query_kernel,
        grid=(depth // chunk,),
        in_specs=[pl.BlockSpec((rows, chunk), lambda i: (0, i))] * 4
        + [pl.BlockSpec((chunk, width), lambda i: (i, last)), pl.BlockSpec((1, 128), lambda i: (0, 0))],
        out_specs=pl.BlockSpec((4, rows, width), lambda i: (0, 0, 0)),
        out_shape=jax.ShapeDtypeStruct((4, rows, width), jnp.bfloat16),
        scratch_shapes=[pltpu.VMEM((4 * rows, width), jnp.float32)],
        compiler_params=pltpu.CompilerParams(vmem_limit_bytes=32 * 2**20),
        cost_estimate=pl.CostEstimate(
            flops=8 * rows * depth * width, bytes_accessed=2 * (4 * rows + width) * depth, transcendentals=0
        ),
        name="query_projection",
    )(*texts, weights, gain)


def local(
    text,
    norm_gain,
    q_weight,
    k_weight,
    v_weight,
    q_gain,
    k_gain,
    vision,
    tiles_per_image,
    image_start,
    tile_owner,
):
    row_count = text.shape[0]
    head_dim = q_gain.shape[0]
    heads_kv = k_weight.shape[1] // head_dim
    tile_rows = vision[0]
    tile_len = tile_rows.shape[0]
    most_tiles = tile_owner.shape[1]
    length = row_count * lax.axis_size(SEQ)
    at_doc, at_y, at_x, at_core = (lax.axis_index(a) for a in ("z", "y", "x", "c"))

    group_width = q_weight.shape[1] // heads_kv
    q_share = lax.dynamic_slice_in_dim(q_weight, at_doc * group_width, group_width, 1)
    weights = lax.all_gather(jnp.concatenate([k_weight, v_weight, q_share], axis=1), SEQ, axis=0, tiled=True)
    other_rows = lax.ppermute(tile_rows, "c", [(0, 1), (1, 0)])
    text_wide = text.astype(jnp.float32)
    normed = norm_rows(text_wide, norm_gain).astype(jnp.bfloat16)
    around = [normed] + [
        lax.ppermute(normed, "z", ring(step)) for step in (1, 2, 3)
    ]
    tails = (ragged_end(tile_rows), ragged_end(other_rows))
    weights, other_rows, tails, *around = lax.optimization_barrier((weights, other_rows, tails, *around))

    totals = jnp.sum(tiles_per_image, axis=1)
    valid = jnp.arange(most_tiles, dtype=jnp.int32)[None, :] < totals[:, None]
    owned = jnp.any(
        (tile_owner[:, :, None] == jnp.arange(lax.axis_size(SEQ), dtype=jnp.int32)) & valid[:, :, None], axis=1
    )
    owned = owned.reshape(owned.shape[0], -1, 2)
    crowded = jnp.any(owned[:, :, 0] & owned[:, :, 1])
    picked = jnp.arange(tiles_per_image.shape[0], dtype=jnp.int32) == at_doc
    tile_counts = jnp.sum(jnp.where(picked[:, None], tiles_per_image, 0), axis=0)
    starts = jnp.sum(jnp.where(picked[:, None], image_start, 0), axis=0)
    owners = jnp.sum(jnp.where(picked[:, None], tile_owner, 0), axis=0)
    first_core = jnp.any(owned & picked[:, None, None], axis=0)[:, 0]
    tile_low, tile_high, tile_valid = tile_spans(tile_counts, starts, length, most_tiles)
    tile_low = jnp.where(tile_valid, tile_low, 2 * length)
    tile_high = jnp.where(tile_valid, tile_high, 0)

    chip_first = jnp.sum(
        jnp.where(jnp.arange(first_core.shape[0]) == at_y * 4 + at_x, first_core.astype(jnp.int32), 0)
    )
    source = 1 - chip_first
    gain_row = k_gain.reshape(1, head_dim)
    chip_of = owners // 2
    turn = jnp.where((owners % 2 == 1) & first_core[chip_of], 1, 0)

    def project(from_core):
        use_own = (at_core == from_core).astype(jnp.int32)
        return project_kv(tile_rows, other_rows, tails, weights, gain_row, at_core, use_own)

    pieces, weights = lax.optimization_barrier((project(source), weights))

    def spread(rounds):
        def run():
            if rounds == 1:
                sent = pieces[:, None]
            else:
                sent = jnp.stack([pieces, project(1)], axis=1)
            got = lax.all_to_all(sent, PLANE, 0, 0, tiled=True)
            query = project_query(around, weights, q_gain.reshape(1, head_dim))
            mine = [query[0]] + [lax.ppermute(query[k], "z", ring(-k)) for k in (1, 2, 3)]
            got, mine = lax.optimization_barrier((got, jnp.stack(mine)))
            at_turn = turn if rounds > 1 else jnp.zeros_like(turn)
            return jnp.stack([got[chip_of[j], at_turn[j]] for j in range(most_tiles)]), mine

        return run

    chosen, mine = lax.cond(crowded, spread(2), spread(1))

    after, before, swap = ring(1), ring(-1), [(0, 1), (1, 0)]
    from_before, from_after = lax.ppermute(chosen, "y", after), lax.ppermute(chosen, "y", before)
    half = most_tiles // 2
    opposite = [lax.ppermute(from_before[:half], "y", after), lax.ppermute(from_after[half:], "y", before)]
    parts = [chosen, from_before, from_after, *opposite]
    parts += [lax.ppermute(part, "c", swap) for part in parts]
    query = [mine[(at_x + s - at_doc) % 4] for s in range(4)]
    query = [query[0]] + [lax.ppermute(query[s], "x", ring(s)) for s in (1, 2, 3)]
    last_slot = jnp.array([1, 3, 2, 0], jnp.int32)[at_y]
    last_part = jnp.where(at_core == 1, last_slot, last_slot + 4)
    pad = 2 * HALF - tile_len
    pad_row = (last_part + 1) * ROWS - pad

    token_x = (at_x - jnp.arange(4, dtype=jnp.int32)) % 4
    blocks = ((at_y * 4 + token_x) * 2 + at_core) * row_count
    spans = jnp.concatenate([tile_low, tile_high])
    far = attend(jnp.stack(query[1:]), parts, jnp.concatenate([spans, blocks[1:], pad_row[None]]), pad)
    context = [lax.ppermute(far[k - 1], "x", ring(-k)) for k in (1, 2, 3)]
    near = attend(query[0][None], parts, jnp.concatenate([spans, blocks[:1], pad_row[None]]), pad)
    context = [near[0]] + context
    context = jnp.stack(context)
    return jnp.concatenate([context[(h - at_x) % 4] for h in range(heads_kv)], axis=1)


def solution(mesh):
    grid = Mesh(mesh.devices.reshape(4, 4, 4, 2), ("z", "y", "x", "c"))
    rows = ("z", "y", "x", "c")
    return jax.shard_map(
        local,
        mesh=grid,
        in_specs=(
            P(rows, None),
            P(),
            P(SEQ, None),
            P(SEQ, None),
            P(SEQ, None),
            P(),
            P(),
            P(rows, None, None),
            P(),
            P(),
            P(),
        ),
        out_specs=P(rows, None),
        check_vma=False,
    )
```

```python
import functools

import jax
import jax.numpy as jnp
from jax import lax
from jax.experimental import pallas as pl
from jax.experimental.pallas import tpu as pltpu
from jax.sharding import Mesh
from jax.sharding import PartitionSpec as P

SEQ = ("y", "x", "c")
PLANE = ("y", "x")
PARTS = 8
ROWS = 208
HALF = 4 * ROWS
NONE = -1e30
MASKED = -2e30
LOG2E = 1.4426950408889634


def tile_spans(tile_counts, starts, length, most_tiles):
    slots = tile_counts.shape[0]
    span_ends = jnp.concatenate([starts[1:], jnp.full((1,), length, jnp.int32)])
    offsets = jnp.cumsum(tile_counts) - tile_counts
    tile_total = jnp.sum(tile_counts)
    tile_ids = jnp.arange(most_tiles, dtype=jnp.int32)
    image_of = jnp.sum((offsets[None, :] <= tile_ids[:, None]).astype(jnp.int32), axis=1) - 1
    member = jnp.arange(slots, dtype=jnp.int32)[None, :] == image_of[:, None]
    tile_low = jnp.sum(jnp.where(member, starts[None, :], 0), axis=1)
    tile_high = jnp.sum(jnp.where(member, span_ends[None, :], 0), axis=1)
    return (tile_low, tile_high, tile_ids < tile_total)


def ring(step):
    return [(i, (i + step) % 4) for i in range(4)]


def norm_rows(values, gain):
    return values * lax.rsqrt(jnp.mean(values * values, axis=-1, keepdims=True) + 1e-05) * gain


CHUNKS = ((0, 512), (512, 1024), (1024, 2048), (2048, 3072), (3072, 4096))


def kv_kernel(
    tile_len, meta_ref, own_ref, other_ref, own_tail, other_tail, weight_ref, gain_ref, out_ref,
    tile_buf, weight_buf, acc_ref, tile_sem, tail_sem, weight_sem,
):
    core, own = meta_ref[0], meta_ref[1]
    whole = tile_len // 16 * 16 - HALF
    kv_width = weight_buf.shape[1]

    def weight_copy(k):
        low, high = CHUNKS[k]
        at = pl.ds(low, high - low)
        return pltpu.make_async_copy(weight_ref.at[at, pl.ds(0, kv_width)], weight_buf.at[at], weight_sem.at[k])

    def tile_copies(k, source, tail, lower):
        low, high = CHUNKS[k]
        at = pl.ds(low, high - low)
        if not lower:
            rows = pl.ds(0, HALF)
            return [pltpu.make_async_copy(source.at[rows, at], tile_buf.at[rows, at], tile_sem.at[k])]
        return [
            pltpu.make_async_copy(
                source.at[pl.ds(HALF, whole), at], tile_buf.at[pl.ds(0, whole), at], tile_sem.at[k]
            ),
            pltpu.make_async_copy(tail.at[:, at], tile_buf.at[pl.ds(whole, 16), at], tail_sem.at[k]),
        ]

    for k in range(len(CHUNKS)):
        weight_copy(k).start()
        for from_own, source, tail in ((1, own_ref, own_tail), (0, other_ref, other_tail)):
            for lower in (0, 1):

                @pl.when((own == from_own) & (core == lower))
                def _(k=k, source=source, tail=tail, lower=lower):
                    for copy in tile_copies(k, source, tail, lower):
                        copy.start()

    for k, (low, high) in enumerate(CHUNKS):
        weight_copy(k).wait()
        for lower in (0, 1):

            @pl.when(core == lower)
            def _(k=k, lower=lower):
                for copy in tile_copies(k, own_ref, own_tail, lower):
                    copy.wait()

        part = jnp.dot(tile_buf[:, low:high], weight_buf[low:high, :], preferred_element_type=jnp.float32)
        if k == 0:
            acc_ref[...] = part
        else:
            acc_ref[...] += part

    for y in range(4):
        held = tile_len - core * HALF - y * ROWS
        kept = lax.broadcasted_iota(jnp.int32, (ROWS, 128), 0) < held
        for h in range(4):
            at = slice(y * ROWS, (y + 1) * ROWS)
            keys = acc_ref[at, h * 128 : (h + 1) * 128]
            values = acc_ref[at, (h + 4) * 128 : (h + 5) * 128]
            if y == 3:
                keys, values = jnp.where(kept, keys, 0.0), jnp.where(kept, values, 0.0)
            out_ref[y * 4 + h, :, :128] = norm_rows(keys, gain_ref[...]).astype(jnp.bfloat16)
            out_ref[y * 4 + h, :, 128:] = values.astype(jnp.bfloat16)


def ragged_end(tile):
    whole = tile.shape[0] // 16 * 16
    return jnp.pad(tile[whole:], ((0, 16 - tile.shape[0] + whole), (0, 0)))


def project_kv(own, other, tails, weights, k_gain, core, use_own):
    tile_len, depth = own.shape
    width = 1024
    meta = jnp.stack([core, use_own]).astype(jnp.int32)
    chunks = len(CHUNKS)
    return pl.pallas_call(
        functools.partial(kv_kernel, tile_len),
        in_specs=[pl.BlockSpec(memory_space=pltpu.SMEM)]
        + [pl.BlockSpec(memory_space=pl.ANY)] * 5
        + [pl.BlockSpec(memory_space=pltpu.VMEM)],
        out_specs=pl.BlockSpec(memory_space=pltpu.VMEM),
        out_shape=jax.ShapeDtypeStruct((16, ROWS, 256), jnp.bfloat16),
        scratch_shapes=[
            pltpu.VMEM((HALF, depth), jnp.bfloat16),
            pltpu.VMEM((depth, width), jnp.bfloat16),
            pltpu.VMEM((HALF, width), jnp.float32),
            pltpu.SemaphoreType.DMA((chunks,)),
            pltpu.SemaphoreType.DMA((chunks,)),
            pltpu.SemaphoreType.DMA((chunks,)),
        ],
        compiler_params=pltpu.CompilerParams(vmem_limit_bytes=40 * 2**20),
        cost_estimate=pl.CostEstimate(
            flops=2 * HALF * depth * width, bytes_accessed=2 * (HALF + width) * depth, transcendentals=0
        ),
        name="kv_projection",
    )(meta, own, other, *tails, weights, k_gain)


def attend_kernel(pad, meta_ref, q_ref, *refs):
    part_refs, (out_ref, m_ref, l_ref, acc_ref) = refs[:-4], refs[-4:]
    tile = pl.program_id(0)
    blocks, rows, width = q_ref.shape
    heads = width // 128
    keys = PARTS * ROWS
    factor = LOG2E / 128**0.5
    pairs = heads // 2

    @pl.when(tile == 0)
    def _():
        m_ref[...] = jnp.full_like(m_ref, NONE)
        l_ref[...] = jnp.zeros_like(l_ref)
        acc_ref[...] = jnp.zeros_like(acc_ref)

    low, high = meta_ref[tile], meta_ref[4 + tile]
    some, every = False, True
    for b in range(blocks):
        first = meta_ref[8 + b]
        some = some | ((low < first + rows) & (high > first))
        every = every & (low <= first) & (high >= first + rows)

    def step(partial):
        held = []
        for own, before, after, low_tiles, high_tiles in (part_refs[:5], part_refs[5:]):
            opposite = jnp.where(tile < 2, low_tiles[0], high_tiles[0])
            held += [own[0], before[0], after[0], opposite]
        kv = jnp.concatenate(held, axis=0)
        row = lax.broadcasted_iota(jnp.int32, (keys, 128), 0)
        padding = (row >= meta_ref[8 + blocks]) & (row < meta_ref[8 + blocks] + pad)
        lane = lax.broadcasted_iota(jnp.int32, (keys, 128), 1) == 0
        bias = jnp.where(padding & lane, MASKED, 0.0).astype(jnp.bfloat16)
        key = jnp.concatenate([kv[:, :128], bias], axis=1)
        value = jnp.concatenate([kv[:, 128:], jnp.ones((keys, 128), jnp.bfloat16)], axis=1)
        one = (lax.broadcasted_iota(jnp.int32, (2 * rows, 128), 1) == 0).astype(jnp.bfloat16)

        def score(group):
            b, h = group // pairs, group % pairs * 2
            both = [q_ref[b, :, i * 128 : (i + 1) * 128] for i in (h, h + 1)]
            deep = jnp.concatenate([jnp.concatenate(both, axis=0), one], axis=1)
            return lax.dot_general(deep, key, (((1,), (1,)), ((), ())), preferred_element_type=jnp.float32)

        def soften(group, scores):
            if partial:
                at = meta_ref[8 + group // pairs] + lax.broadcasted_iota(jnp.int32, (2 * rows, 1), 0) % rows
                scores = jnp.where((at >= low) & (at < high), scores, MASKED)
            m_old = m_ref[group]
            m_new = jnp.maximum(m_old, jnp.max(scores, axis=1, keepdims=True))
            probs = jnp.exp2((scores - m_new) * factor)
            alpha = jnp.exp2((m_old - m_new) * factor)
            m_ref[group] = m_new
            summed = jnp.dot(probs.astype(jnp.bfloat16), value, preferred_element_type=jnp.float32)
            l_ref[group] = l_ref[group] * alpha + summed[:, 128:129]
            acc_ref[group] = acc_ref[group] * alpha + summed[:, :128]

        scores = score(0)
        for group in range(blocks * pairs):
            ahead = score(group + 1) if group + 1 < blocks * pairs else None
            soften(group, scores)
            scores = ahead

    pl.when(every)(lambda: step(False))
    pl.when(some & jnp.logical_not(every))(lambda: step(True))

    @pl.when(tile == pl.num_programs(0) - 1)
    def _():
        for b in range(blocks):
            for h in range(heads):
                group, at = b * pairs + h // 2, slice(h % 2 * rows, (h % 2 + 1) * rows)
                out_ref[b, :, h * 128 : (h + 1) * 128] = (
                    acc_ref[group, at] / jnp.maximum(l_ref[group, at], 1.0)
                ).astype(jnp.bfloat16)


def attend(query, parts, meta, pad):
    blocks, rows, width = query.shape
    tiles = parts[0].shape[0]
    groups = blocks * width // 256
    return pl.pallas_call(
        functools.partial(attend_kernel, pad),
        grid_spec=pltpu.PrefetchScalarGridSpec(
            num_scalar_prefetch=1,
            grid=(tiles,),
            in_specs=[
                pl.BlockSpec((blocks, rows, width), lambda j, meta: (0, 0, 0)),
            ]
            + (
                [pl.BlockSpec((1, ROWS, 256), lambda j, meta: (j, 0, 0))] * 3
                + [pl.BlockSpec((1, ROWS, 256), lambda j, meta: (jnp.minimum(j, 1), 0, 0))]
                + [pl.BlockSpec((1, ROWS, 256), lambda j, meta: (jnp.maximum(j - 2, 0), 0, 0))]
            )
            * 2,
            out_specs=pl.BlockSpec((blocks, rows, width), lambda j, meta: (0, 0, 0)),
            scratch_shapes=[
                pltpu.VMEM((groups, 2 * rows, 1), jnp.float32),
                pltpu.VMEM((groups, 2 * rows, 1), jnp.float32),
                pltpu.VMEM((groups, 2 * rows, 128), jnp.float32),
            ],
        ),
        out_shape=jax.ShapeDtypeStruct(query.shape, jnp.bfloat16),
        compiler_params=pltpu.CompilerParams(vmem_limit_bytes=40 * 2**20),
        cost_estimate=pl.CostEstimate(
            flops=8 * blocks * rows * width * tiles * PARTS * ROWS,
            bytes_accessed=512 * tiles * PARTS * ROWS,
            transcendentals=blocks * rows * width // 128 * tiles * PARTS * ROWS,
        ),
        name="attention",
    )(meta, query, *parts)


def query_kernel(text0, text1, text2, text3, weight_ref, gain_ref, out_ref, acc_ref):
    step = pl.program_id(0)
    text = jnp.concatenate([ref[...] for ref in (text0, text1, text2, text3)], axis=0)
    part = jnp.dot(text, weight_ref[...], preferred_element_type=jnp.float32)

    @pl.when(step == 0)
    def _():
        acc_ref[...] = part

    @pl.when(step > 0)
    def _():
        acc_ref[...] += part

    @pl.when(step == pl.num_programs(0) - 1)
    def _():
        for b in range(4):
            for h in range(acc_ref.shape[1] // 128):
                block = acc_ref[b * 128 : (b + 1) * 128, h * 128 : (h + 1) * 128]
                out_ref[b, :, h * 128 : (h + 1) * 128] = norm_rows(block, gain_ref[...]).astype(jnp.bfloat16)


def project_query(texts, weights, gain):
    rows, depth = texts[0].shape
    width = 512
    chunk = 1024
    last = weights.shape[1] // width - 1
    return pl.pallas_call(
        query_kernel,
        grid=(depth // chunk,),
        in_specs=[pl.BlockSpec((rows, chunk), lambda i: (0, i))] * 4
        + [pl.BlockSpec((chunk, width), lambda i: (i, last)), pl.BlockSpec((1, 128), lambda i: (0, 0))],
        out_specs=pl.BlockSpec((4, rows, width), lambda i: (0, 0, 0)),
        out_shape=jax.ShapeDtypeStruct((4, rows, width), jnp.bfloat16),
        scratch_shapes=[pltpu.VMEM((4 * rows, width), jnp.float32)],
        compiler_params=pltpu.CompilerParams(vmem_limit_bytes=32 * 2**20),
        cost_estimate=pl.CostEstimate(
            flops=8 * rows * depth * width, bytes_accessed=2 * (4 * rows + width) * depth, transcendentals=0
        ),
        name="query_projection",
    )(*texts, weights, gain)


def local(
    text,
    norm_gain,
    q_weight,
    k_weight,
    v_weight,
    q_gain,
    k_gain,
    vision,
    tiles_per_image,
    image_start,
    tile_owner,
):
    row_count = text.shape[0]
    head_dim = q_gain.shape[0]
    heads_kv = k_weight.shape[1] // head_dim
    tile_rows = vision[0]
    tile_len = tile_rows.shape[0]
    most_tiles = tile_owner.shape[1]
    length = row_count * lax.axis_size(SEQ)
    at_doc, at_y, at_x, at_core = (lax.axis_index(a) for a in ("z", "y", "x", "c"))

    group_width = q_weight.shape[1] // heads_kv
    q_share = lax.dynamic_slice_in_dim(q_weight, at_doc * group_width, group_width, 1)
    weights = lax.all_gather(jnp.concatenate([k_weight, v_weight, q_share], axis=1), SEQ, axis=0, tiled=True)
    other_rows = lax.ppermute(tile_rows, "c", [(0, 1), (1, 0)])
    text_wide = text.astype(jnp.float32)
    normed = norm_rows(text_wide, norm_gain).astype(jnp.bfloat16)
    around = [normed] + [
        lax.ppermute(normed, "z", ring(step)) for step in (1, 2, 3)
    ]
    tails = (ragged_end(tile_rows), ragged_end(other_rows))
    weights, other_rows, tails, *around = lax.optimization_barrier((weights, other_rows, tails, *around))

    totals = jnp.sum(tiles_per_image, axis=1)
    valid = jnp.arange(most_tiles, dtype=jnp.int32)[None, :] < totals[:, None]
    owned = jnp.any(
        (tile_owner[:, :, None] == jnp.arange(lax.axis_size(SEQ), dtype=jnp.int32)) & valid[:, :, None], axis=1
    )
    owned = owned.reshape(owned.shape[0], -1, 2)
    crowded = jnp.any(owned[:, :, 0] & owned[:, :, 1])
    picked = jnp.arange(tiles_per_image.shape[0], dtype=jnp.int32) == at_doc
    tile_counts = jnp.sum(jnp.where(picked[:, None], tiles_per_image, 0), axis=0)
    starts = jnp.sum(jnp.where(picked[:, None], image_start, 0), axis=0)
    owners = jnp.sum(jnp.where(picked[:, None], tile_owner, 0), axis=0)
    first_core = jnp.any(owned & picked[:, None, None], axis=0)[:, 0]
    tile_low, tile_high, tile_valid = tile_spans(tile_counts, starts, length, most_tiles)
    tile_low = jnp.where(tile_valid, tile_low, 2 * length)
    tile_high = jnp.where(tile_valid, tile_high, 0)

    chip_first = jnp.sum(
        jnp.where(jnp.arange(first_core.shape[0]) == at_y * 4 + at_x, first_core.astype(jnp.int32), 0)
    )
    source = 1 - chip_first
    gain_row = k_gain.reshape(1, head_dim)
    chip_of = owners // 2
    turn = jnp.where((owners % 2 == 1) & first_core[chip_of], 1, 0)

    def project(from_core):
        use_own = (at_core == from_core).astype(jnp.int32)
        return project_kv(tile_rows, other_rows, tails, weights, gain_row, at_core, use_own)

    pieces, weights = lax.optimization_barrier((project(source), weights))

    def send(sent):
        return lax.all_to_all(sent, PLANE, 0, 0, tiled=True)

    def pick(got):
        return jnp.stack([got[chip_of[j]] for j in range(most_tiles)])

    def ask():
        query = project_query(around, weights, q_gain.reshape(1, head_dim))
        return jnp.stack([query[0]] + [lax.ppermute(query[k], "z", ring(-k)) for k in (1, 2, 3)])

    def spread_one():
        got, mine = lax.optimization_barrier((send(pieces), ask()))
        return pick(got), mine

    def spread_two():
        got, second = lax.optimization_barrier((send(pieces), project(1)))
        later, mine = lax.optimization_barrier((send(second), ask()))
        return jnp.where((turn > 0)[:, None, None], pick(later), pick(got)), mine

    chosen, mine = lax.cond(crowded, spread_two, spread_one)

    after, before, swap = ring(1), ring(-1), [(0, 1), (1, 0)]
    from_before, from_after = lax.ppermute(chosen, "y", after), lax.ppermute(chosen, "y", before)
    half = most_tiles // 2
    opposite = [lax.ppermute(from_before[:half], "y", after), lax.ppermute(from_after[half:], "y", before)]
    parts = [chosen, from_before, from_after, *opposite]
    parts += [lax.ppermute(part, "c", swap) for part in parts]
    query = [mine[(at_x + s - at_doc) % 4] for s in range(4)]
    query = [query[0]] + [lax.ppermute(query[s], "x", ring(s)) for s in (1, 2, 3)]
    last_slot = jnp.array([1, 3, 2, 0], jnp.int32)[at_y]
    last_part = jnp.where(at_core == 1, last_slot, last_slot + 4)
    pad = 2 * HALF - tile_len
    pad_row = (last_part + 1) * ROWS - pad

    token_x = (at_x - jnp.arange(4, dtype=jnp.int32)) % 4
    blocks = ((at_y * 4 + token_x) * 2 + at_core) * row_count
    spans = jnp.concatenate([tile_low, tile_high])
    context = attend(jnp.stack(query), parts, jnp.concatenate([spans, blocks, pad_row[None]]), pad)
    context = [context[0]] + [lax.ppermute(context[k], "x", ring(-k)) for k in (1, 2, 3)]
    context = jnp.stack(context)
    return jnp.concatenate([context[(h - at_x) % 4] for h in range(heads_kv)], axis=1)


def solution(mesh):
    grid = Mesh(mesh.devices.reshape(4, 4, 4, 2), ("z", "y", "x", "c"))
    rows = ("z", "y", "x", "c")
    return jax.shard_map(
        local,
        mesh=grid,
        in_specs=(
            P(rows, None),
            P(),
            P(SEQ, None),
            P(SEQ, None),
            P(SEQ, None),
            P(),
            P(),
            P(rows, None, None),
            P(),
            P(),
            P(),
        ),
        out_specs=P(rows, None),
        check_vma=False,
    )
```

```python
import functools

import jax
import jax.numpy as jnp
from jax import lax
from jax.experimental import pallas as pl
from jax.experimental.pallas import tpu as pltpu
from jax.sharding import Mesh
from jax.sharding import PartitionSpec as P

SEQ = ("y", "x", "c")
PLANE = ("y", "x")
PARTS = 8
ROWS = 208
HALF = 4 * ROWS
NONE = -1e30
MASKED = -2e30
LOG2E = 1.4426950408889634


def tile_spans(tile_counts, starts, length, most_tiles):
    slots = tile_counts.shape[0]
    span_ends = jnp.concatenate([starts[1:], jnp.full((1,), length, jnp.int32)])
    offsets = jnp.cumsum(tile_counts) - tile_counts
    tile_total = jnp.sum(tile_counts)
    tile_ids = jnp.arange(most_tiles, dtype=jnp.int32)
    image_of = jnp.sum((offsets[None, :] <= tile_ids[:, None]).astype(jnp.int32), axis=1) - 1
    member = jnp.arange(slots, dtype=jnp.int32)[None, :] == image_of[:, None]
    tile_low = jnp.sum(jnp.where(member, starts[None, :], 0), axis=1)
    tile_high = jnp.sum(jnp.where(member, span_ends[None, :], 0), axis=1)
    return (tile_low, tile_high, tile_ids < tile_total)


def ring(step):
    return [(i, (i + step) % 4) for i in range(4)]


def norm_rows(values, gain):
    return values * lax.rsqrt(jnp.mean(values * values, axis=-1, keepdims=True) + 1e-05) * gain


CHUNKS = ((0, 512), (512, 1024), (1024, 2048), (2048, 3072), (3072, 4096))


def kv_kernel(
    tile_len, meta_ref, own_ref, other_ref, own_tail, other_tail, weight_ref, gain_ref, out_ref,
    tile_buf, weight_buf, acc_ref, tile_sem, tail_sem, weight_sem,
):
    core, own = meta_ref[0], meta_ref[1]
    whole = tile_len // 16 * 16 - HALF
    kv_width = weight_buf.shape[1]

    def weight_copy(k):
        low, high = CHUNKS[k]
        at = pl.ds(low, high - low)
        return pltpu.make_async_copy(weight_ref.at[at, pl.ds(0, kv_width)], weight_buf.at[at], weight_sem.at[k])

    def tile_copies(k, source, tail, lower):
        low, high = CHUNKS[k]
        at = pl.ds(low, high - low)
        if not lower:
            rows = pl.ds(0, HALF)
            return [pltpu.make_async_copy(source.at[rows, at], tile_buf.at[rows, at], tile_sem.at[k])]
        return [
            pltpu.make_async_copy(
                source.at[pl.ds(HALF, whole), at], tile_buf.at[pl.ds(0, whole), at], tile_sem.at[k]
            ),
            pltpu.make_async_copy(tail.at[:, at], tile_buf.at[pl.ds(whole, 16), at], tail_sem.at[k]),
        ]

    for k in range(len(CHUNKS)):
        weight_copy(k).start()
        for from_own, source, tail in ((1, own_ref, own_tail), (0, other_ref, other_tail)):
            for lower in (0, 1):

                @pl.when((own == from_own) & (core == lower))
                def _(k=k, source=source, tail=tail, lower=lower):
                    for copy in tile_copies(k, source, tail, lower):
                        copy.start()

    for k, (low, high) in enumerate(CHUNKS):
        weight_copy(k).wait()
        for lower in (0, 1):

            @pl.when(core == lower)
            def _(k=k, lower=lower):
                for copy in tile_copies(k, own_ref, own_tail, lower):
                    copy.wait()

        part = jnp.dot(tile_buf[:, low:high], weight_buf[low:high, :], preferred_element_type=jnp.float32)
        if k == 0:
            acc_ref[...] = part
        else:
            acc_ref[...] += part

    for y in range(4):
        held = tile_len - core * HALF - y * ROWS
        kept = lax.broadcasted_iota(jnp.int32, (ROWS, 128), 0) < held
        for h in range(4):
            at = slice(y * ROWS, (y + 1) * ROWS)
            keys = acc_ref[at, h * 128 : (h + 1) * 128]
            values = acc_ref[at, (h + 4) * 128 : (h + 5) * 128]
            if y == 3:
                keys, values = jnp.where(kept, keys, 0.0), jnp.where(kept, values, 0.0)
            out_ref[y * 4 + h, :, :128] = norm_rows(keys, gain_ref[...]).astype(jnp.bfloat16)
            out_ref[y * 4 + h, :, 128:] = values.astype(jnp.bfloat16)


def ragged_end(tile):
    whole = tile.shape[0] // 16 * 16
    return jnp.pad(tile[whole:], ((0, 16 - tile.shape[0] + whole), (0, 0)))


def project_kv(own, other, tails, weights, k_gain, core, use_own):
    tile_len, depth = own.shape
    width = 1024
    meta = jnp.stack([core, use_own]).astype(jnp.int32)
    chunks = len(CHUNKS)
    return pl.pallas_call(
        functools.partial(kv_kernel, tile_len),
        in_specs=[pl.BlockSpec(memory_space=pltpu.SMEM)]
        + [pl.BlockSpec(memory_space=pl.ANY)] * 5
        + [pl.BlockSpec(memory_space=pltpu.VMEM)],
        out_specs=pl.BlockSpec(memory_space=pltpu.VMEM),
        out_shape=jax.ShapeDtypeStruct((16, ROWS, 256), jnp.bfloat16),
        scratch_shapes=[
            pltpu.VMEM((HALF, depth), jnp.bfloat16),
            pltpu.VMEM((depth, width), jnp.bfloat16),
            pltpu.VMEM((HALF, width), jnp.float32),
            pltpu.SemaphoreType.DMA((chunks,)),
            pltpu.SemaphoreType.DMA((chunks,)),
            pltpu.SemaphoreType.DMA((chunks,)),
        ],
        compiler_params=pltpu.CompilerParams(vmem_limit_bytes=40 * 2**20),
        cost_estimate=pl.CostEstimate(
            flops=2 * HALF * depth * width, bytes_accessed=2 * (HALF + width) * depth, transcendentals=0
        ),
        name="kv_projection",
    )(meta, own, other, *tails, weights, k_gain)


def attend_kernel(pad, meta_ref, q_ref, *refs):
    part_refs, (out_ref, m_ref, l_ref, acc_ref) = refs[:-4], refs[-4:]
    tile = pl.program_id(0)
    blocks, rows, width = q_ref.shape
    heads = width // 128
    keys = PARTS * ROWS
    factor = LOG2E / 128**0.5
    pairs = heads // 2

    @pl.when(tile == 0)
    def _():
        m_ref[...] = jnp.full_like(m_ref, NONE)
        l_ref[...] = jnp.zeros_like(l_ref)
        acc_ref[...] = jnp.zeros_like(acc_ref)

    low, high = meta_ref[tile], meta_ref[4 + tile]
    some = False
    for b in range(blocks):
        first = meta_ref[8 + b]
        some = some | ((low < first + rows) & (high > first))

    @pl.when(some)
    def _():
        held = []
        for i in range(0, 2 * PARTS, 2):
            held.append(jnp.where(tile < 2, part_refs[i][0], part_refs[i + 1][0]))
        kv = jnp.concatenate(held, axis=0)
        row = lax.broadcasted_iota(jnp.int32, (keys, 128), 0)
        lane = lax.broadcasted_iota(jnp.int32, (keys, 128), 1)
        padding = (row >= meta_ref[8 + blocks]) & (row < meta_ref[8 + blocks] + pad)
        key_mask = jnp.where((lane == 0) & padding, MASKED, jnp.where(lane == 1, 1.0, 0.0))
        key = jnp.concatenate([kv[:, :128], key_mask.astype(jnp.bfloat16)], axis=1)
        value = jnp.concatenate([kv[:, 128:], jnp.ones((keys, 128), jnp.bfloat16)], axis=1)
        text_row = lax.broadcasted_iota(jnp.int32, (rows, 128), 0)
        text_lane = lax.broadcasted_iota(jnp.int32, (rows, 128), 1)

        def score(group):
            b, h = group // pairs, group % pairs * 2
            at = meta_ref[8 + b] + text_row
            outside = (at < low) | (at >= high)
            mask = jnp.where((text_lane == 1) & outside, MASKED, jnp.where(text_lane == 0, 1.0, 0.0))
            mask = mask.astype(jnp.bfloat16)
            both = [
                jnp.concatenate([q_ref[b, :, i * 128 : (i + 1) * 128], mask], axis=1) for i in (h, h + 1)
            ]
            return lax.dot_general(
                jnp.concatenate(both, axis=0), key, (((1,), (1,)), ((), ())), preferred_element_type=jnp.float32
            )

        def soften(group, scores):
            m_old = m_ref[group]
            m_new = jnp.maximum(m_old, jnp.max(scores, axis=1, keepdims=True))
            probs = jnp.exp2((scores - m_new) * factor)
            alpha = jnp.exp2((m_old - m_new) * factor)
            m_ref[group] = m_new
            summed = jnp.dot(probs.astype(jnp.bfloat16), value, preferred_element_type=jnp.float32)
            l_ref[group] = l_ref[group] * alpha + summed[:, 128:129]
            acc_ref[group] = acc_ref[group] * alpha + summed[:, :128]

        scores = score(0)
        for group in range(blocks * pairs):
            ahead = score(group + 1) if group + 1 < blocks * pairs else None
            soften(group, scores)
            scores = ahead

    @pl.when(tile == pl.num_programs(0) - 1)
    def _():
        for b in range(blocks):
            for h in range(heads):
                group, at = b * pairs + h // 2, slice(h % 2 * rows, (h % 2 + 1) * rows)
                out_ref[b, :, h * 128 : (h + 1) * 128] = (
                    acc_ref[group, at] / jnp.maximum(l_ref[group, at], 1.0)
                ).astype(jnp.bfloat16)


def attend(query, parts, meta, pad):
    blocks, rows, width = query.shape
    tiles = 2 * parts[0].shape[0]
    groups = blocks * width // 256
    return pl.pallas_call(
        functools.partial(attend_kernel, pad),
        grid_spec=pltpu.PrefetchScalarGridSpec(
            num_scalar_prefetch=1,
            grid=(tiles,),
            in_specs=[
                pl.BlockSpec((blocks, rows, width), lambda j, meta: (0, 0, 0)),
            ]
            + [
                pl.BlockSpec((1, ROWS, 256), lambda j, meta: (jnp.minimum(j, 1), 0, 0)),
                pl.BlockSpec((1, ROWS, 256), lambda j, meta: (jnp.maximum(j - 2, 0), 0, 0)),
            ]
            * PARTS,
            out_specs=pl.BlockSpec((blocks, rows, width), lambda j, meta: (0, 0, 0)),
            scratch_shapes=[
                pltpu.VMEM((groups, 2 * rows, 1), jnp.float32),
                pltpu.VMEM((groups, 2 * rows, 1), jnp.float32),
                pltpu.VMEM((groups, 2 * rows, 128), jnp.float32),
            ],
        ),
        out_shape=jax.ShapeDtypeStruct(query.shape, jnp.bfloat16),
        compiler_params=pltpu.CompilerParams(vmem_limit_bytes=40 * 2**20),
        cost_estimate=pl.CostEstimate(
            flops=8 * blocks * rows * width * tiles * PARTS * ROWS,
            bytes_accessed=512 * tiles * PARTS * ROWS,
            transcendentals=blocks * rows * width // 128 * tiles * PARTS * ROWS,
        ),
        name="attention",
    )(meta, query, *parts)


def query_kernel(text0, text1, text2, text3, weight_ref, gain_ref, out_ref, acc_ref):
    step = pl.program_id(0)
    text = jnp.concatenate([ref[...] for ref in (text0, text1, text2, text3)], axis=0)
    part = jnp.dot(text, weight_ref[...], preferred_element_type=jnp.float32)

    @pl.when(step == 0)
    def _():
        acc_ref[...] = part

    @pl.when(step > 0)
    def _():
        acc_ref[...] += part

    @pl.when(step == pl.num_programs(0) - 1)
    def _():
        for b in range(4):
            for h in range(acc_ref.shape[1] // 128):
                block = acc_ref[b * 128 : (b + 1) * 128, h * 128 : (h + 1) * 128]
                out_ref[b, :, h * 128 : (h + 1) * 128] = norm_rows(block, gain_ref[...]).astype(jnp.bfloat16)


def project_query(texts, weights, gain):
    rows, depth = texts[0].shape
    width = 512
    chunk = 1024
    last = weights.shape[1] // width - 1
    return pl.pallas_call(
        query_kernel,
        grid=(depth // chunk,),
        in_specs=[pl.BlockSpec((rows, chunk), lambda i: (0, i))] * 4
        + [pl.BlockSpec((chunk, width), lambda i: (i, last)), pl.BlockSpec((1, 128), lambda i: (0, 0))],
        out_specs=pl.BlockSpec((4, rows, width), lambda i: (0, 0, 0)),
        out_shape=jax.ShapeDtypeStruct((4, rows, width), jnp.bfloat16),
        scratch_shapes=[pltpu.VMEM((4 * rows, width), jnp.float32)],
        compiler_params=pltpu.CompilerParams(vmem_limit_bytes=32 * 2**20),
        cost_estimate=pl.CostEstimate(
            flops=8 * rows * depth * width, bytes_accessed=2 * (4 * rows + width) * depth, transcendentals=0
        ),
        name="query_projection",
    )(*texts, weights, gain)


def join_kernel(k_ref, v_ref, q_ref, out_ref, sems):
    width = k_ref.shape[1]
    start = pl.multiple_of(lax.axis_index("z") * width, 128)
    sources = (k_ref, v_ref, q_ref.at[:, pl.ds(start, width)])
    copies = [
        pltpu.make_async_copy(source, out_ref.at[:, pl.ds(i * width, width)], sems.at[i])
        for i, source in enumerate(sources)
    ]
    for copy in copies:
        copy.start()
    for copy in copies:
        copy.wait()


def join_columns(k_weight, v_weight, q_weight):
    rows, width = k_weight.shape
    return pl.pallas_call(
        join_kernel,
        in_specs=[pl.BlockSpec(memory_space=pl.ANY)] * 3,
        out_specs=pl.BlockSpec(memory_space=pl.ANY),
        out_shape=jax.ShapeDtypeStruct((rows, 3 * width), k_weight.dtype),
        scratch_shapes=[pltpu.SemaphoreType.DMA((3,))],
        name="join_columns",
    )(k_weight, v_weight, q_weight)


def local(
    text,
    norm_gain,
    q_weight,
    k_weight,
    v_weight,
    q_gain,
    k_gain,
    vision,
    tiles_per_image,
    image_start,
    tile_owner,
):
    row_count = text.shape[0]
    head_dim = q_gain.shape[0]
    heads_kv = k_weight.shape[1] // head_dim
    tile_rows = vision[0]
    tile_len = tile_rows.shape[0]
    most_tiles = tile_owner.shape[1]
    length = row_count * lax.axis_size(SEQ)
    at_doc, at_y, at_x, at_core = (lax.axis_index(a) for a in ("z", "y", "x", "c"))

    weights = lax.all_gather(join_columns(k_weight, v_weight, q_weight), SEQ, axis=0, tiled=True)
    other_rows = lax.ppermute(tile_rows, "c", [(0, 1), (1, 0)])
    text_wide = text.astype(jnp.float32)
    normed = norm_rows(text_wide, norm_gain).astype(jnp.bfloat16)
    around = [normed] + [
        lax.ppermute(normed, "z", ring(step)) for step in (1, 2, 3)
    ]
    tails = (ragged_end(tile_rows), ragged_end(other_rows))
    weights, other_rows, tails, *around = lax.optimization_barrier((weights, other_rows, tails, *around))

    totals = jnp.sum(tiles_per_image, axis=1)
    valid = jnp.arange(most_tiles, dtype=jnp.int32)[None, :] < totals[:, None]
    owned = jnp.any(
        (tile_owner[:, :, None] == jnp.arange(lax.axis_size(SEQ), dtype=jnp.int32)) & valid[:, :, None], axis=1
    )
    owned = owned.reshape(owned.shape[0], -1, 2)
    crowded = jnp.any(owned[:, :, 0] & owned[:, :, 1])
    picked = jnp.arange(tiles_per_image.shape[0], dtype=jnp.int32) == at_doc
    tile_counts = jnp.sum(jnp.where(picked[:, None], tiles_per_image, 0), axis=0)
    starts = jnp.sum(jnp.where(picked[:, None], image_start, 0), axis=0)
    owners = jnp.sum(jnp.where(picked[:, None], tile_owner, 0), axis=0)
    first_core = jnp.any(owned & picked[:, None, None], axis=0)[:, 0]
    tile_low, tile_high, tile_valid = tile_spans(tile_counts, starts, length, most_tiles)
    tile_low = jnp.where(tile_valid, tile_low, 2 * length)
    tile_high = jnp.where(tile_valid, tile_high, 0)

    chip_first = jnp.sum(
        jnp.where(jnp.arange(first_core.shape[0]) == at_y * 4 + at_x, first_core.astype(jnp.int32), 0)
    )
    source = 1 - chip_first
    gain_row = k_gain.reshape(1, head_dim)
    chip_of = owners // 2
    turn = jnp.where((owners % 2 == 1) & first_core[chip_of], 1, 0)

    def project(from_core):
        use_own = (at_core == from_core).astype(jnp.int32)
        return project_kv(tile_rows, other_rows, tails, weights, gain_row, at_core, use_own)

    pieces, weights = lax.optimization_barrier((project(source), weights))

    def send(sent):
        return lax.all_to_all(sent, PLANE, 0, 0, tiled=True)

    def pick(got):
        return [jnp.stack([got[chip_of[j]], got[chip_of[j + 1]]]) for j in range(0, most_tiles, 2)]

    def ask():
        query = project_query(around, weights, q_gain.reshape(1, head_dim))
        return jnp.stack([query[0]] + [lax.ppermute(query[k], "z", ring(-k)) for k in (1, 2, 3)])

    def spread_one():
        got, mine = lax.optimization_barrier((send(pieces), ask()))
        return *pick(got), mine

    def spread_two():
        got, second = lax.optimization_barrier((send(pieces), project(1)))
        later, mine = lax.optimization_barrier((send(second), ask()))
        is_later = (turn > 0)[:, None, None]
        both = [
            jnp.where(is_later[2 * i : 2 * i + 2], b, a) for i, (a, b) in enumerate(zip(pick(got), pick(later)))
        ]
        return *both, mine

    low_tiles, high_tiles, mine = lax.cond(crowded, spread_two, spread_one)

    before_low, after_high = lax.ppermute(low_tiles, "y", ring(1)), lax.ppermute(high_tiles, "y", ring(-1))
    before_high, after_low = lax.ppermute(high_tiles, "y", ring(1)), lax.ppermute(low_tiles, "y", ring(-1))
    far_low, far_high = lax.ppermute(before_low, "y", ring(1)), lax.ppermute(after_high, "y", ring(-1))
    parts = [low_tiles, high_tiles, before_low, before_high, after_low, after_high, far_low, far_high]
    parts += [lax.ppermute(part, "c", [(0, 1), (1, 0)]) for part in parts]
    query = [mine[(at_x + s - at_doc) % 4] for s in range(4)]
    query = [query[0]] + [lax.ppermute(query[s], "x", ring(s)) for s in (1, 2, 3)]
    last_slot = jnp.array([1, 3, 2, 0], jnp.int32)[at_y]
    last_part = jnp.where(at_core == 1, last_slot, last_slot + 4)
    pad = 2 * HALF - tile_len
    pad_row = (last_part + 1) * ROWS - pad

    token_x = (at_x - jnp.arange(4, dtype=jnp.int32)) % 4
    blocks = ((at_y * 4 + token_x) * 2 + at_core) * row_count
    spans = jnp.concatenate([tile_low, tile_high])
    context = attend(jnp.stack(query), parts, jnp.concatenate([spans, blocks, pad_row[None]]), pad)
    context = [context[0]] + [lax.ppermute(context[k], "x", ring(-k)) for k in (1, 2, 3)]
    context = jnp.stack(context)
    return jnp.concatenate([context[(h - at_x) % 4] for h in range(heads_kv)], axis=1)


def solution(mesh):
    grid = Mesh(mesh.devices.reshape(4, 4, 4, 2), ("z", "y", "x", "c"))
    rows = ("z", "y", "x", "c")
    return jax.shard_map(
        local,
        mesh=grid,
        in_specs=(
            P(rows, None),
            P(),
            P(SEQ, None),
            P(SEQ, None),
            P(SEQ, None),
            P(),
            P(),
            P(rows, None, None),
            P(),
            P(),
            P(),
        ),
        out_specs=P(rows, None),
        check_vma=False,
    )
```

```python
import functools

import jax
import jax.numpy as jnp
from jax import lax
from jax.experimental import pallas as pl
from jax.experimental.pallas import tpu as pltpu
from jax.sharding import Mesh
from jax.sharding import PartitionSpec as P

SEQ = ("y", "x", "c")
PLANE = ("y", "x")
PARTS = 8
ROWS = 208
HALF = 4 * ROWS
NONE = -1e30
MASKED = -2e30
LOG2E = 1.4426950408889634


def tile_spans(tile_counts, starts, length, most_tiles):
    slots = tile_counts.shape[0]
    span_ends = jnp.concatenate([starts[1:], jnp.full((1,), length, jnp.int32)])
    offsets = jnp.cumsum(tile_counts) - tile_counts
    tile_total = jnp.sum(tile_counts)
    tile_ids = jnp.arange(most_tiles, dtype=jnp.int32)
    image_of = jnp.sum((offsets[None, :] <= tile_ids[:, None]).astype(jnp.int32), axis=1) - 1
    member = jnp.arange(slots, dtype=jnp.int32)[None, :] == image_of[:, None]
    tile_low = jnp.sum(jnp.where(member, starts[None, :], 0), axis=1)
    tile_high = jnp.sum(jnp.where(member, span_ends[None, :], 0), axis=1)
    return (tile_low, tile_high, tile_ids < tile_total)


def ring(step):
    return [(i, (i + step) % 4) for i in range(4)]


def norm_rows(values, gain):
    return values * lax.rsqrt(jnp.mean(values * values, axis=-1, keepdims=True) + 1e-05) * gain


CHUNKS = ((0, 512), (512, 1024), (1024, 2048), (2048, 3072), (3072, 4096))


def kv_kernel(
    tile_len, meta_ref, own_ref, other_ref, own_tail, other_tail, weight_ref, gain_ref, out_ref,
    tile_buf, weight_buf, acc_ref, tile_sem, tail_sem, weight_sem,
):
    core, own = meta_ref[0], meta_ref[1]
    whole = tile_len // 16 * 16 - HALF
    kv_width = weight_buf.shape[1]

    def weight_copy(k):
        low, high = CHUNKS[k]
        at = pl.ds(low, high - low)
        return pltpu.make_async_copy(weight_ref.at[at, pl.ds(0, kv_width)], weight_buf.at[at], weight_sem.at[k])

    def tile_copies(k, source, tail, lower):
        low, high = CHUNKS[k]
        at = pl.ds(low, high - low)
        if not lower:
            rows = pl.ds(0, HALF)
            return [pltpu.make_async_copy(source.at[rows, at], tile_buf.at[rows, at], tile_sem.at[k])]
        return [
            pltpu.make_async_copy(
                source.at[pl.ds(HALF, whole), at], tile_buf.at[pl.ds(0, whole), at], tile_sem.at[k]
            ),
            pltpu.make_async_copy(tail.at[:, at], tile_buf.at[pl.ds(whole, 16), at], tail_sem.at[k]),
        ]

    for k in range(len(CHUNKS)):
        weight_copy(k).start()
        for from_own, source, tail in ((1, own_ref, own_tail), (0, other_ref, other_tail)):
            for lower in (0, 1):

                @pl.when((own == from_own) & (core == lower))
                def _(k=k, source=source, tail=tail, lower=lower):
                    for copy in tile_copies(k, source, tail, lower):
                        copy.start()

    for k, (low, high) in enumerate(CHUNKS):
        weight_copy(k).wait()
        for lower in (0, 1):

            @pl.when(core == lower)
            def _(k=k, lower=lower):
                for copy in tile_copies(k, own_ref, own_tail, lower):
                    copy.wait()

        part = jnp.dot(tile_buf[:, low:high], weight_buf[low:high, :], preferred_element_type=jnp.float32)
        if k == 0:
            acc_ref[...] = part
        else:
            acc_ref[...] += part

    for y in range(4):
        held = tile_len - core * HALF - y * ROWS
        kept = lax.broadcasted_iota(jnp.int32, (ROWS, 128), 0) < held
        for h in range(4):
            at = slice(y * ROWS, (y + 1) * ROWS)
            keys = acc_ref[at, h * 128 : (h + 1) * 128]
            values = acc_ref[at, (h + 4) * 128 : (h + 5) * 128]
            if y == 3:
                keys, values = jnp.where(kept, keys, 0.0), jnp.where(kept, values, 0.0)
            out_ref[y * 4 + h, :, :128] = norm_rows(keys, gain_ref[...]).astype(jnp.bfloat16)
            out_ref[y * 4 + h, :, 128:] = values.astype(jnp.bfloat16)


def ragged_end(tile):
    whole = tile.shape[0] // 16 * 16
    return jnp.pad(tile[whole:], ((0, 16 - tile.shape[0] + whole), (0, 0)))


def project_kv(own, other, tails, weights, k_gain, core, use_own):
    tile_len, depth = own.shape
    width = 1024
    meta = jnp.stack([core, use_own]).astype(jnp.int32)
    chunks = len(CHUNKS)
    return pl.pallas_call(
        functools.partial(kv_kernel, tile_len),
        in_specs=[pl.BlockSpec(memory_space=pltpu.SMEM)]
        + [pl.BlockSpec(memory_space=pl.ANY)] * 5
        + [pl.BlockSpec(memory_space=pltpu.VMEM)],
        out_specs=pl.BlockSpec(memory_space=pltpu.VMEM),
        out_shape=jax.ShapeDtypeStruct((16, ROWS, 256), jnp.bfloat16),
        scratch_shapes=[
            pltpu.VMEM((HALF, depth), jnp.bfloat16),
            pltpu.VMEM((depth, width), jnp.bfloat16),
            pltpu.VMEM((HALF, width), jnp.float32),
            pltpu.SemaphoreType.DMA((chunks,)),
            pltpu.SemaphoreType.DMA((chunks,)),
            pltpu.SemaphoreType.DMA((chunks,)),
        ],
        compiler_params=pltpu.CompilerParams(vmem_limit_bytes=40 * 2**20),
        cost_estimate=pl.CostEstimate(
            flops=2 * HALF * depth * width, bytes_accessed=2 * (HALF + width) * depth, transcendentals=0
        ),
        name="kv_projection",
    )(meta, own, other, *tails, weights, k_gain)


def attend_kernel(pad, meta_ref, q_ref, *refs):
    part_refs, (out_ref, m_ref, l_ref, acc_ref) = refs[:-4], refs[-4:]
    tile = pl.program_id(0)
    blocks, rows, width = q_ref.shape
    heads = width // 128
    keys = PARTS * ROWS
    factor = LOG2E / 128**0.5
    pairs = heads // 2

    @pl.when(tile == 0)
    def _():
        m_ref[...] = jnp.full_like(m_ref, NONE)
        l_ref[...] = jnp.zeros_like(l_ref)
        acc_ref[...] = jnp.zeros_like(acc_ref)

    low, high = meta_ref[tile], meta_ref[4 + tile]
    some = False
    for b in range(blocks):
        first = meta_ref[8 + b]
        some = some | ((low < first + rows) & (high > first))

    @pl.when(some)
    def _():
        held = []
        for own, before, after, low_tiles, high_tiles in (part_refs[:5], part_refs[5:]):
            held += [own[0], before[0], after[0], jnp.where(tile < 2, low_tiles[0], high_tiles[0])]
        kv = jnp.concatenate(held, axis=0)
        row = lax.broadcasted_iota(jnp.int32, (keys, 128), 0)
        lane = lax.broadcasted_iota(jnp.int32, (keys, 128), 1)
        padding = (row >= meta_ref[8 + blocks]) & (row < meta_ref[8 + blocks] + pad)
        key_mask = jnp.where((lane == 0) & padding, MASKED, jnp.where(lane == 1, 1.0, 0.0))
        key = jnp.concatenate([kv[:, :128], key_mask.astype(jnp.bfloat16)], axis=1)
        value = jnp.concatenate([kv[:, 128:], jnp.ones((keys, 128), jnp.bfloat16)], axis=1)
        text_row = lax.broadcasted_iota(jnp.int32, (rows, 128), 0)
        text_lane = lax.broadcasted_iota(jnp.int32, (rows, 128), 1)

        def score(group):
            b, h = group // pairs, group % pairs * 2
            at = meta_ref[8 + b] + text_row
            outside = (at < low) | (at >= high)
            mask = jnp.where((text_lane == 1) & outside, MASKED, jnp.where(text_lane == 0, 1.0, 0.0))
            mask = mask.astype(jnp.bfloat16)
            both = [
                jnp.concatenate([q_ref[b, :, i * 128 : (i + 1) * 128], mask], axis=1) for i in (h, h + 1)
            ]
            return lax.dot_general(
                jnp.concatenate(both, axis=0), key, (((1,), (1,)), ((), ())), preferred_element_type=jnp.float32
            )

        def soften(group, scores):
            m_old = m_ref[group]
            m_new = jnp.maximum(m_old, jnp.max(scores, axis=1, keepdims=True))
            probs = jnp.exp2((scores - m_new) * factor)
            alpha = jnp.exp2((m_old - m_new) * factor)
            m_ref[group] = m_new
            summed = jnp.dot(probs.astype(jnp.bfloat16), value, preferred_element_type=jnp.float32)
            l_ref[group] = l_ref[group] * alpha + summed[:, 128:129]
            acc_ref[group] = acc_ref[group] * alpha + summed[:, :128]

        scores = score(0)
        for group in range(blocks * pairs):
            ahead = score(group + 1) if group + 1 < blocks * pairs else None
            soften(group, scores)
            scores = ahead

    @pl.when(tile == pl.num_programs(0) - 1)
    def _():
        for b in range(blocks):
            for h in range(heads):
                group, at = b * pairs + h // 2, slice(h % 2 * rows, (h % 2 + 1) * rows)
                out_ref[b, :, h * 128 : (h + 1) * 128] = (
                    acc_ref[group, at] / jnp.maximum(l_ref[group, at], 1.0)
                ).astype(jnp.bfloat16)


def attend(query, parts, meta, pad):
    blocks, rows, width = query.shape
    tiles = parts[0].shape[0]
    groups = blocks * width // 256
    return pl.pallas_call(
        functools.partial(attend_kernel, pad),
        grid_spec=pltpu.PrefetchScalarGridSpec(
            num_scalar_prefetch=1,
            grid=(tiles,),
            in_specs=[
                pl.BlockSpec((blocks, rows, width), lambda j, meta: (0, 0, 0)),
            ]
            + (
                [pl.BlockSpec((1, ROWS, 256), lambda j, meta: (j, 0, 0))] * 3
                + [pl.BlockSpec((1, ROWS, 256), lambda j, meta: (jnp.minimum(j, 1), 0, 0))]
                + [pl.BlockSpec((1, ROWS, 256), lambda j, meta: (jnp.maximum(j - 2, 0), 0, 0))]
            )
            * 2,
            out_specs=pl.BlockSpec((blocks, rows, width), lambda j, meta: (0, 0, 0)),
            scratch_shapes=[
                pltpu.VMEM((groups, 2 * rows, 1), jnp.float32),
                pltpu.VMEM((groups, 2 * rows, 1), jnp.float32),
                pltpu.VMEM((groups, 2 * rows, 128), jnp.float32),
            ],
        ),
        out_shape=jax.ShapeDtypeStruct(query.shape, jnp.bfloat16),
        compiler_params=pltpu.CompilerParams(vmem_limit_bytes=40 * 2**20),
        cost_estimate=pl.CostEstimate(
            flops=8 * blocks * rows * width * tiles * PARTS * ROWS,
            bytes_accessed=512 * tiles * PARTS * ROWS,
            transcendentals=blocks * rows * width // 128 * tiles * PARTS * ROWS,
        ),
        name="attention",
    )(meta, query, *parts)


def query_kernel(text0, text1, text2, text3, weight_ref, gain_ref, out_ref, acc_ref):
    step = pl.program_id(0)
    text = jnp.concatenate([ref[...] for ref in (text0, text1, text2, text3)], axis=0)
    part = jnp.dot(text, weight_ref[...], preferred_element_type=jnp.float32)

    @pl.when(step == 0)
    def _():
        acc_ref[...] = part

    @pl.when(step > 0)
    def _():
        acc_ref[...] += part

    @pl.when(step == pl.num_programs(0) - 1)
    def _():
        for b in range(4):
            for h in range(acc_ref.shape[1] // 128):
                block = acc_ref[b * 128 : (b + 1) * 128, h * 128 : (h + 1) * 128]
                out_ref[b, :, h * 128 : (h + 1) * 128] = norm_rows(block, gain_ref[...]).astype(jnp.bfloat16)


def project_query(texts, weights, gain):
    rows, depth = texts[0].shape
    width = 512
    chunk = 1024
    last = weights.shape[1] // width - 1
    return pl.pallas_call(
        query_kernel,
        grid=(depth // chunk,),
        in_specs=[pl.BlockSpec((rows, chunk), lambda i: (0, i))] * 4
        + [pl.BlockSpec((chunk, width), lambda i: (i, last)), pl.BlockSpec((1, 128), lambda i: (0, 0))],
        out_specs=pl.BlockSpec((4, rows, width), lambda i: (0, 0, 0)),
        out_shape=jax.ShapeDtypeStruct((4, rows, width), jnp.bfloat16),
        scratch_shapes=[pltpu.VMEM((4 * rows, width), jnp.float32)],
        compiler_params=pltpu.CompilerParams(vmem_limit_bytes=32 * 2**20),
        cost_estimate=pl.CostEstimate(
            flops=8 * rows * depth * width, bytes_accessed=2 * (4 * rows + width) * depth, transcendentals=0
        ),
        name="query_projection",
    )(*texts, weights, gain)


def local(
    text,
    norm_gain,
    q_weight,
    k_weight,
    v_weight,
    q_gain,
    k_gain,
    vision,
    tiles_per_image,
    image_start,
    tile_owner,
):
    row_count = text.shape[0]
    head_dim = q_gain.shape[0]
    heads_kv = k_weight.shape[1] // head_dim
    tile_rows = vision[0]
    tile_len = tile_rows.shape[0]
    most_tiles = tile_owner.shape[1]
    length = row_count * lax.axis_size(SEQ)
    at_doc, at_y, at_x, at_core = (lax.axis_index(a) for a in ("z", "y", "x", "c"))

    group_width = q_weight.shape[1] // heads_kv
    q_share = lax.dynamic_slice_in_dim(q_weight, at_doc * group_width, group_width, 1)
    weights = lax.all_gather(jnp.concatenate([k_weight, v_weight, q_share], axis=1), SEQ, axis=0, tiled=True)
    other_rows = lax.ppermute(tile_rows, "c", [(0, 1), (1, 0)])
    text_wide = text.astype(jnp.float32)
    normed = norm_rows(text_wide, norm_gain).astype(jnp.bfloat16)
    around = [normed] + [
        lax.ppermute(normed, "z", ring(step)) for step in (1, 2, 3)
    ]
    tails = (ragged_end(tile_rows), ragged_end(other_rows))
    weights, other_rows, tails, *around = lax.optimization_barrier((weights, other_rows, tails, *around))

    totals = jnp.sum(tiles_per_image, axis=1)
    valid = jnp.arange(most_tiles, dtype=jnp.int32)[None, :] < totals[:, None]
    owned = jnp.any(
        (tile_owner[:, :, None] == jnp.arange(lax.axis_size(SEQ), dtype=jnp.int32)) & valid[:, :, None], axis=1
    )
    owned = owned.reshape(owned.shape[0], -1, 2)
    crowded = jnp.any(owned[:, :, 0] & owned[:, :, 1])
    picked = jnp.arange(tiles_per_image.shape[0], dtype=jnp.int32) == at_doc
    tile_counts = jnp.sum(jnp.where(picked[:, None], tiles_per_image, 0), axis=0)
    starts = jnp.sum(jnp.where(picked[:, None], image_start, 0), axis=0)
    owners = jnp.sum(jnp.where(picked[:, None], tile_owner, 0), axis=0)
    first_core = jnp.any(owned & picked[:, None, None], axis=0)[:, 0]
    tile_low, tile_high, tile_valid = tile_spans(tile_counts, starts, length, most_tiles)
    tile_low = jnp.where(tile_valid, tile_low, 2 * length)
    tile_high = jnp.where(tile_valid, tile_high, 0)

    chip_first = jnp.sum(
        jnp.where(jnp.arange(first_core.shape[0]) == at_y * 4 + at_x, first_core.astype(jnp.int32), 0)
    )
    source = 1 - chip_first
    gain_row = k_gain.reshape(1, head_dim)
    chip_of = owners // 2
    turn = jnp.where((owners % 2 == 1) & first_core[chip_of], 1, 0)

    def project(from_core):
        use_own = (at_core == from_core).astype(jnp.int32)
        return project_kv(tile_rows, other_rows, tails, weights, gain_row, at_core, use_own)

    pieces, weights = lax.optimization_barrier((project(source), weights))

    def send(sent):
        return lax.all_to_all(sent, PLANE, 0, 0, tiled=True)

    def pick(got):
        return jnp.stack([got[chip_of[j]] for j in range(most_tiles)])

    def ask():
        query = project_query(around, weights, q_gain.reshape(1, head_dim))
        return jnp.stack([query[0]] + [lax.ppermute(query[k], "z", ring(-k)) for k in (1, 2, 3)])

    def spread_one():
        got, mine = lax.optimization_barrier((send(pieces), ask()))
        return pick(got), mine

    def spread_two():
        got, second = lax.optimization_barrier((send(pieces), project(1)))
        later, mine = lax.optimization_barrier((send(second), ask()))
        return jnp.where((turn > 0)[:, None, None], pick(later), pick(got)), mine

    chosen, mine = lax.cond(crowded, spread_two, spread_one)

    before, after = lax.ppermute(chosen, "y", ring(1)), lax.ppermute(chosen, "y", ring(-1))
    half = most_tiles // 2
    opposite = [lax.ppermute(before[:half], "y", ring(1)), lax.ppermute(after[half:], "y", ring(-1))]
    parts = [chosen, before, after, *opposite]
    parts += [lax.ppermute(part, "c", [(0, 1), (1, 0)]) for part in parts]
    query = [mine[(at_x + s - at_doc) % 4] for s in range(4)]
    query = [query[0]] + [lax.ppermute(query[s], "x", ring(s)) for s in (1, 2, 3)]
    last_slot = jnp.array([1, 3, 2, 0], jnp.int32)[at_y]
    last_part = jnp.where(at_core == 1, last_slot, last_slot + 4)
    pad = 2 * HALF - tile_len
    pad_row = (last_part + 1) * ROWS - pad

    token_x = (at_x - jnp.arange(4, dtype=jnp.int32)) % 4
    blocks = ((at_y * 4 + token_x) * 2 + at_core) * row_count
    spans = jnp.concatenate([tile_low, tile_high])
    context = attend(jnp.stack(query), parts, jnp.concatenate([spans, blocks, pad_row[None]]), pad)
    context = [context[0]] + [lax.ppermute(context[k], "x", ring(-k)) for k in (1, 2, 3)]
    context = jnp.stack(context)
    return jnp.concatenate([context[(h - at_x) % 4] for h in range(heads_kv)], axis=1)


def solution(mesh):
    grid = Mesh(mesh.devices.reshape(4, 4, 4, 2), ("z", "y", "x", "c"))
    rows = ("z", "y", "x", "c")
    return jax.shard_map(
        local,
        mesh=grid,
        in_specs=(
            P(rows, None),
            P(),
            P(SEQ, None),
            P(SEQ, None),
            P(SEQ, None),
            P(),
            P(),
            P(rows, None, None),
            P(),
            P(),
            P(),
        ),
        out_specs=P(rows, None),
        check_vma=False,
    )
```

```python
import functools

import jax
import jax.numpy as jnp
from jax import lax
from jax.experimental import pallas as pl
from jax.experimental.pallas import tpu as pltpu
from jax.sharding import Mesh
from jax.sharding import PartitionSpec as P

SEQ = ("y", "x", "c")
PLANE = ("y", "x")
PARTS = 8
ROWS = 208
HALF = 4 * ROWS
NONE = -1e30
MASKED = -2e30
LOG2E = 1.4426950408889634


def tile_spans(tile_counts, starts, length, most_tiles):
    slots = tile_counts.shape[0]
    span_ends = jnp.concatenate([starts[1:], jnp.full((1,), length, jnp.int32)])
    offsets = jnp.cumsum(tile_counts) - tile_counts
    tile_total = jnp.sum(tile_counts)
    tile_ids = jnp.arange(most_tiles, dtype=jnp.int32)
    image_of = jnp.sum((offsets[None, :] <= tile_ids[:, None]).astype(jnp.int32), axis=1) - 1
    member = jnp.arange(slots, dtype=jnp.int32)[None, :] == image_of[:, None]
    tile_low = jnp.sum(jnp.where(member, starts[None, :], 0), axis=1)
    tile_high = jnp.sum(jnp.where(member, span_ends[None, :], 0), axis=1)
    return (tile_low, tile_high, tile_ids < tile_total)


def ring(step):
    return [(i, (i + step) % 4) for i in range(4)]


def norm_rows(values, gain):
    return values * lax.rsqrt(jnp.mean(values * values, axis=-1, keepdims=True) + 1e-05) * gain


AWAY = (0, -1, 1, 2)
CHUNKS = ((0, 2), (2, 4), (4, 8), (8, 12), (12, 16))
CHAIN = 5


def chip_at(y, x, place):
    return (y + AWAY[place // 4] + 4) % 4 * 4 + (x + AWAY[place % 4] + 4) % 4


def chain_piece(chain, far, near):
    if far < 3:
        return chain[far].at[near]
    return chain[3].at[near] if near < 2 else chain[4].at[near - 2]


def first_half(chain, place):
    return chain_piece(chain, place // 4, place % 4)


def second_half(chain, place):
    return chain_piece(chain, place % 4, place // 4)


def kv_kernel(tile_len, meta_ref, own_ref, other_ref, own_tail, other_tail, *refs):
    mine, swapped = refs[:CHAIN], refs[CHAIN : 2 * CHAIN]
    gain_ref, out_ref, tile_buf, weight_buf, acc_ref, tile_sem, tail_sem, first_sem, second_sem = refs[2 * CHAIN :]
    core, own, y_at, x_at = (meta_ref[i] for i in range(4))
    whole = tile_len // 16 * 16 - HALF
    split = mine[0].shape[2]
    rest = weight_buf.shape[1] - split

    def weight_copies(place, first, second):
        rows = pl.ds(place * 256, 256)
        return [
            pltpu.make_async_copy(
                first_half(first, place), weight_buf.at[rows, pl.ds(0, split)], first_sem.at[place]
            ),
            pltpu.make_async_copy(
                second_half(second, place).at[:, pl.ds(0, rest)],
                weight_buf.at[rows, pl.ds(split, rest)],
                second_sem.at[place],
            ),
        ]

    def tile_copies(place, source, tail, lower):
        at = pl.ds(pl.multiple_of(chip_at(y_at, x_at, place) * 256, 256), 256)
        to = pl.ds(place * 256, 256)
        if not lower:
            rows = pl.ds(0, HALF)
            return [pltpu.make_async_copy(source.at[rows, at], tile_buf.at[rows, to], tile_sem.at[place])]
        return [
            pltpu.make_async_copy(
                source.at[pl.ds(HALF, whole), at], tile_buf.at[pl.ds(0, whole), to], tile_sem.at[place]
            ),
            pltpu.make_async_copy(tail.at[:, at], tile_buf.at[pl.ds(whole, 16), to], tail_sem.at[place]),
        ]

    for low, high in CHUNKS:
        for lower, first, second in ((0, mine, swapped), (1, swapped, mine)):

            @pl.when(core == lower)
            def _(low=low, high=high, first=first, second=second):
                for place in range(low, high):
                    for copy in weight_copies(place, first, second):
                        copy.start()

            for from_own, source, tail in ((1, own_ref, own_tail), (0, other_ref, other_tail)):

                @pl.when((own == from_own) & (core == lower))
                def _(low=low, high=high, source=source, tail=tail, lower=lower):
                    for place in range(low, high):
                        for copy in tile_copies(place, source, tail, lower):
                            copy.start()

    for low, high in CHUNKS:
        for lower in (0, 1):

            @pl.when(core == lower)
            def _(low=low, high=high, lower=lower):
                for place in range(low, high):
                    for copy in weight_copies(place, mine, swapped) + tile_copies(place, own_ref, own_tail, lower):
                        copy.wait()

        at = slice(low * 256, high * 256)
        part = jnp.dot(tile_buf[:, at], weight_buf[at, :], preferred_element_type=jnp.float32)
        if low == 0:
            acc_ref[...] = part
        else:
            acc_ref[...] += part

    for y in range(4):
        held = tile_len - core * HALF - y * ROWS
        kept = lax.broadcasted_iota(jnp.int32, (ROWS, 128), 0) < held
        for h in range(4):
            at = slice(y * ROWS, (y + 1) * ROWS)
            keys = acc_ref[at, h * 128 : (h + 1) * 128]
            values = acc_ref[at, (h + 4) * 128 : (h + 5) * 128]
            if y == 3:
                keys, values = jnp.where(kept, keys, 0.0), jnp.where(kept, values, 0.0)
            out_ref[y * 4 + h, :, :128] = norm_rows(keys, gain_ref[...]).astype(jnp.bfloat16)
            out_ref[y * 4 + h, :, 128:] = values.astype(jnp.bfloat16)


def ragged_end(tile):
    whole = tile.shape[0] // 16 * 16
    return jnp.pad(tile[whole:], ((0, 16 - tile.shape[0] + whole), (0, 0)))


def project_kv(own, other, tails, chains, k_gain, meta):
    tile_len, depth = own.shape
    width = 1024
    return pl.pallas_call(
        functools.partial(kv_kernel, tile_len),
        in_specs=[pl.BlockSpec(memory_space=pltpu.SMEM)]
        + [pl.BlockSpec(memory_space=pl.ANY)] * (4 + 2 * CHAIN)
        + [pl.BlockSpec(memory_space=pltpu.VMEM)],
        out_specs=pl.BlockSpec(memory_space=pltpu.VMEM),
        out_shape=jax.ShapeDtypeStruct((16, ROWS, 256), jnp.bfloat16),
        scratch_shapes=[
            pltpu.VMEM((HALF, depth), jnp.bfloat16),
            pltpu.VMEM((depth, width), jnp.bfloat16),
            pltpu.VMEM((HALF, width), jnp.float32),
        ]
        + [pltpu.SemaphoreType.DMA((16,))] * 4,
        compiler_params=pltpu.CompilerParams(vmem_limit_bytes=32 * 2**20),
        cost_estimate=pl.CostEstimate(
            flops=2 * HALF * depth * width, bytes_accessed=2 * (HALF + width) * depth, transcendentals=0
        ),
        name="kv_projection",
    )(meta, own, other, *tails, *chains, k_gain)


def attend_kernel(pad, meta_ref, q_ref, *refs):
    part_refs, (out_ref, m_ref, l_ref, acc_ref) = refs[:-4], refs[-4:]
    tile = pl.program_id(0)
    blocks, rows, width = q_ref.shape
    heads = width // 128
    keys = PARTS * ROWS
    factor = LOG2E / 128**0.5
    pairs = heads // 2

    @pl.when(tile == 0)
    def _():
        m_ref[...] = jnp.full_like(m_ref, NONE)
        l_ref[...] = jnp.zeros_like(l_ref)
        acc_ref[...] = jnp.zeros_like(acc_ref)

    low, high = meta_ref[tile], meta_ref[4 + tile]
    some = False
    for b in range(blocks):
        first = meta_ref[8 + b]
        some = some | ((low < first + rows) & (high > first))

    @pl.when(some)
    def _():
        held = []
        for own, before, after, low_tiles, high_tiles in (part_refs[:5], part_refs[5:]):
            held += [own[0], before[0], after[0], jnp.where(tile < 2, low_tiles[0], high_tiles[0])]
        kv = jnp.concatenate(held, axis=0)
        row = lax.broadcasted_iota(jnp.int32, (keys, 128), 0)
        lane = lax.broadcasted_iota(jnp.int32, (keys, 128), 1)
        padding = (row >= meta_ref[8 + blocks]) & (row < meta_ref[8 + blocks] + pad)
        key_mask = jnp.where((lane == 0) & padding, MASKED, jnp.where(lane == 1, 1.0, 0.0))
        key = jnp.concatenate([kv[:, :128], key_mask.astype(jnp.bfloat16)], axis=1)
        value = jnp.concatenate([kv[:, 128:], jnp.ones((keys, 128), jnp.bfloat16)], axis=1)
        text_row = lax.broadcasted_iota(jnp.int32, (rows, 128), 0)
        text_lane = lax.broadcasted_iota(jnp.int32, (rows, 128), 1)

        def score(group):
            b, h = group // pairs, group % pairs * 2
            at = meta_ref[8 + b] + text_row
            outside = (at < low) | (at >= high)
            mask = jnp.where((text_lane == 1) & outside, MASKED, jnp.where(text_lane == 0, 1.0, 0.0))
            mask = mask.astype(jnp.bfloat16)
            both = [
                jnp.concatenate([q_ref[b, :, i * 128 : (i + 1) * 128], mask], axis=1) for i in (h, h + 1)
            ]
            return lax.dot_general(
                jnp.concatenate(both, axis=0), key, (((1,), (1,)), ((), ())), preferred_element_type=jnp.float32
            )

        def soften(group, scores):
            m_old = m_ref[group]
            m_new = jnp.maximum(m_old, jnp.max(scores, axis=1, keepdims=True))
            probs = jnp.exp2((scores - m_new) * factor)
            alpha = jnp.exp2((m_old - m_new) * factor)
            m_ref[group] = m_new
            summed = jnp.dot(probs.astype(jnp.bfloat16), value, preferred_element_type=jnp.float32)
            l_ref[group] = l_ref[group] * alpha + summed[:, 128:129]
            acc_ref[group] = acc_ref[group] * alpha + summed[:, :128]

        scores = score(0)
        for group in range(blocks * pairs):
            ahead = score(group + 1) if group + 1 < blocks * pairs else None
            soften(group, scores)
            scores = ahead

    @pl.when(tile == pl.num_programs(0) - 1)
    def _():
        for b in range(blocks):
            for h in range(heads):
                group, at = b * pairs + h // 2, slice(h % 2 * rows, (h % 2 + 1) * rows)
                out_ref[b, :, h * 128 : (h + 1) * 128] = (
                    acc_ref[group, at] / jnp.maximum(l_ref[group, at], 1.0)
                ).astype(jnp.bfloat16)


def attend(query, parts, meta, pad):
    blocks, rows, width = query.shape
    tiles = parts[0].shape[0]
    groups = blocks * width // 256
    return pl.pallas_call(
        functools.partial(attend_kernel, pad),
        grid_spec=pltpu.PrefetchScalarGridSpec(
            num_scalar_prefetch=1,
            grid=(tiles,),
            in_specs=[
                pl.BlockSpec((blocks, rows, width), lambda j, meta: (0, 0, 0)),
            ]
            + (
                [pl.BlockSpec((1, ROWS, 256), lambda j, meta: (j, 0, 0))] * 3
                + [pl.BlockSpec((1, ROWS, 256), lambda j, meta: (jnp.minimum(j, 1), 0, 0))]
                + [pl.BlockSpec((1, ROWS, 256), lambda j, meta: (jnp.maximum(j - 2, 0), 0, 0))]
            )
            * 2,
            out_specs=pl.BlockSpec((blocks, rows, width), lambda j, meta: (0, 0, 0)),
            scratch_shapes=[
                pltpu.VMEM((groups, 2 * rows, 1), jnp.float32),
                pltpu.VMEM((groups, 2 * rows, 1), jnp.float32),
                pltpu.VMEM((groups, 2 * rows, 128), jnp.float32),
            ],
        ),
        out_shape=jax.ShapeDtypeStruct(query.shape, jnp.bfloat16),
        compiler_params=pltpu.CompilerParams(vmem_limit_bytes=40 * 2**20),
        cost_estimate=pl.CostEstimate(
            flops=8 * blocks * rows * width * tiles * PARTS * ROWS,
            bytes_accessed=512 * tiles * PARTS * ROWS,
            transcendentals=blocks * rows * width // 128 * tiles * PARTS * ROWS,
        ),
        name="attention",
    )(meta, query, *parts)


def query_kernel(meta_ref, text0, text1, text2, text3, *refs):
    mine, swapped = refs[:CHAIN], refs[CHAIN : 2 * CHAIN]
    gain_ref, out_ref, weight_buf, acc_ref, sems = refs[2 * CHAIN :]
    core, y_at, x_at = meta_ref[0], meta_ref[2], meta_ref[3]
    width = weight_buf.shape[1]
    skip = mine[0].shape[2] - width

    def weight_copy(place, second):
        return pltpu.make_async_copy(
            second_half(second, place).at[:, pl.ds(skip, width)],
            weight_buf.at[pl.ds(place * 256, 256)],
            sems.at[place],
        )

    for lower, second in ((0, swapped), (1, mine)):

        @pl.when(core == lower)
        def _(second=second):
            for place in range(16):
                weight_copy(place, second).start()

    for low in range(0, 16, 4):
        columns = []
        for place in range(low, low + 4):
            weight_copy(place, mine).wait()
            at = pl.ds(pl.multiple_of(chip_at(y_at, x_at, place) * 256, 256), 256)
            columns.append(jnp.concatenate([ref[:, at] for ref in (text0, text1, text2, text3)], axis=0))
        part = jnp.dot(
            jnp.concatenate(columns, axis=1),
            weight_buf[low * 256 : (low + 4) * 256, :],
            preferred_element_type=jnp.float32,
        )
        if low == 0:
            acc_ref[...] = part
        else:
            acc_ref[...] += part

    for b in range(4):
        for h in range(width // 128):
            block = acc_ref[b * 128 : (b + 1) * 128, h * 128 : (h + 1) * 128]
            out_ref[b, :, h * 128 : (h + 1) * 128] = norm_rows(block, gain_ref[...]).astype(jnp.bfloat16)


def project_query(texts, chains, gain, meta):
    rows, depth = texts[0].shape
    width = 512
    return pl.pallas_call(
        query_kernel,
        in_specs=[pl.BlockSpec(memory_space=pltpu.SMEM)]
        + [pl.BlockSpec(memory_space=pltpu.VMEM)] * 4
        + [pl.BlockSpec(memory_space=pl.ANY)] * (2 * CHAIN)
        + [pl.BlockSpec(memory_space=pltpu.VMEM)],
        out_specs=pl.BlockSpec(memory_space=pltpu.VMEM),
        out_shape=jax.ShapeDtypeStruct((4, rows, width), jnp.bfloat16),
        scratch_shapes=[
            pltpu.VMEM((depth, width), jnp.bfloat16),
            pltpu.VMEM((4 * rows, width), jnp.float32),
            pltpu.SemaphoreType.DMA((16,)),
        ],
        compiler_params=pltpu.CompilerParams(vmem_limit_bytes=32 * 2**20),
        cost_estimate=pl.CostEstimate(
            flops=8 * rows * depth * width, bytes_accessed=2 * (4 * rows + width) * depth, transcendentals=0
        ),
        name="query_projection",
    )(meta, *texts, *chains, gain)


def gather_weights(k_weight, v_weight, q_share, core):
    cut = v_weight.shape[1] // 2
    halves = (
        jnp.concatenate([k_weight, v_weight[:, :cut]], axis=1),
        jnp.concatenate([v_weight[:, cut:], q_share], axis=1),
    )
    swap = [(0, 1), (1, 0)]
    kept = jnp.where(core == 0, halves[0], halves[1])
    got = lax.ppermute(jnp.where(core == 0, halves[1], halves[0]), "c", swap)
    chip = jnp.where(core == 0, jnp.concatenate([kept, got]), jnp.concatenate([got, kept]))

    def move(piece, step, turn):
        pairs = []
        for y in range(4):
            for x in range(4):
                for c in range(2):
                    to = (y, (x + step) % 4) if (c == 0) == (turn == 0) else ((y + step) % 4, x)
                    pairs.append(((y * 4 + x) * 2 + c, (to[0] * 4 + to[1]) * 2 + c))
        return lax.ppermute(piece, SEQ, pairs)

    line = jnp.stack([chip, move(chip, 1, 0), move(chip, -1, 0), move(chip, 2, 0)])
    before, after = move(line, 1, 1), move(line, -1, 1)
    chain = [line, before, after, move(before[:2], 1, 1), move(after[2:], -1, 1)]
    return chain + [lax.ppermute(piece, "c", swap) for piece in chain]


def local(
    text,
    norm_gain,
    q_weight,
    k_weight,
    v_weight,
    q_gain,
    k_gain,
    vision,
    tiles_per_image,
    image_start,
    tile_owner,
):
    row_count = text.shape[0]
    head_dim = q_gain.shape[0]
    heads_kv = k_weight.shape[1] // head_dim
    tile_rows = vision[0]
    tile_len = tile_rows.shape[0]
    most_tiles = tile_owner.shape[1]
    length = row_count * lax.axis_size(SEQ)
    at_doc, at_y, at_x, at_core = (lax.axis_index(a) for a in ("z", "y", "x", "c"))

    group_width = q_weight.shape[1] // heads_kv
    q_share = lax.dynamic_slice_in_dim(q_weight, at_doc * group_width, group_width, 1)
    chains = gather_weights(k_weight, v_weight, q_share, at_core)
    other_rows = lax.ppermute(tile_rows, "c", [(0, 1), (1, 0)])
    text_wide = text.astype(jnp.float32)
    normed = norm_rows(text_wide, norm_gain).astype(jnp.bfloat16)
    around = [normed] + [
        lax.ppermute(normed, "z", ring(step)) for step in (1, 2, 3)
    ]
    tails = (ragged_end(tile_rows), ragged_end(other_rows))
    chains, other_rows, tails, around = lax.optimization_barrier((chains, other_rows, tails, around))

    totals = jnp.sum(tiles_per_image, axis=1)
    valid = jnp.arange(most_tiles, dtype=jnp.int32)[None, :] < totals[:, None]
    owned = jnp.any(
        (tile_owner[:, :, None] == jnp.arange(lax.axis_size(SEQ), dtype=jnp.int32)) & valid[:, :, None], axis=1
    )
    owned = owned.reshape(owned.shape[0], -1, 2)
    crowded = jnp.any(owned[:, :, 0] & owned[:, :, 1])
    picked = jnp.arange(tiles_per_image.shape[0], dtype=jnp.int32) == at_doc
    tile_counts = jnp.sum(jnp.where(picked[:, None], tiles_per_image, 0), axis=0)
    starts = jnp.sum(jnp.where(picked[:, None], image_start, 0), axis=0)
    owners = jnp.sum(jnp.where(picked[:, None], tile_owner, 0), axis=0)
    first_core = jnp.any(owned & picked[:, None, None], axis=0)[:, 0]
    tile_low, tile_high, tile_valid = tile_spans(tile_counts, starts, length, most_tiles)
    tile_low = jnp.where(tile_valid, tile_low, 2 * length)
    tile_high = jnp.where(tile_valid, tile_high, 0)

    chip_first = jnp.sum(
        jnp.where(jnp.arange(first_core.shape[0]) == at_y * 4 + at_x, first_core.astype(jnp.int32), 0)
    )
    source = 1 - chip_first
    gain_row = k_gain.reshape(1, head_dim)
    chip_of = owners // 2
    turn = jnp.where((owners % 2 == 1) & first_core[chip_of], 1, 0)

    def project(from_core):
        use_own = (at_core == from_core).astype(jnp.int32)
        meta = jnp.stack([at_core, use_own, at_y, at_x]).astype(jnp.int32)
        return project_kv(tile_rows, other_rows, tails, chains, gain_row, meta)

    pieces, chains = lax.optimization_barrier((project(source), chains))

    def send(sent):
        return lax.all_to_all(sent, PLANE, 0, 0, tiled=True)

    def pick(got):
        return jnp.stack([got[chip_of[j]] for j in range(most_tiles)])

    def ask():
        meta = jnp.stack([at_core, at_core, at_y, at_x]).astype(jnp.int32)
        query = project_query(around, chains, q_gain.reshape(1, head_dim), meta)
        return jnp.stack([query[0]] + [lax.ppermute(query[k], "z", ring(-k)) for k in (1, 2, 3)])

    def spread_one():
        got, mine = lax.optimization_barrier((send(pieces), ask()))
        return pick(got), mine

    def spread_two():
        got, second = lax.optimization_barrier((send(pieces), project(1)))
        later, mine = lax.optimization_barrier((send(second), ask()))
        return jnp.where((turn > 0)[:, None, None], pick(later), pick(got)), mine

    chosen, mine = lax.cond(crowded, spread_two, spread_one)

    before, after = lax.ppermute(chosen, "y", ring(1)), lax.ppermute(chosen, "y", ring(-1))
    half = most_tiles // 2
    opposite = [lax.ppermute(before[:half], "y", ring(1)), lax.ppermute(after[half:], "y", ring(-1))]
    parts = [chosen, before, after, *opposite]
    parts += [lax.ppermute(part, "c", [(0, 1), (1, 0)]) for part in parts]
    query = [mine[(at_x + s - at_doc) % 4] for s in range(4)]
    query = [query[0]] + [lax.ppermute(query[s], "x", ring(s)) for s in (1, 2, 3)]
    last_slot = jnp.array([1, 3, 2, 0], jnp.int32)[at_y]
    last_part = jnp.where(at_core == 1, last_slot, last_slot + 4)
    pad = 2 * HALF - tile_len
    pad_row = (last_part + 1) * ROWS - pad

    token_x = (at_x - jnp.arange(4, dtype=jnp.int32)) % 4
    blocks = ((at_y * 4 + token_x) * 2 + at_core) * row_count
    spans = jnp.concatenate([tile_low, tile_high])
    context = attend(jnp.stack(query), parts, jnp.concatenate([spans, blocks, pad_row[None]]), pad)
    context = [context[0]] + [lax.ppermute(context[k], "x", ring(-k)) for k in (1, 2, 3)]
    context = jnp.stack(context)
    return jnp.concatenate([context[(h - at_x) % 4] for h in range(heads_kv)], axis=1)


def solution(mesh):
    grid = Mesh(mesh.devices.reshape(4, 4, 4, 2), ("z", "y", "x", "c"))
    rows = ("z", "y", "x", "c")
    return jax.shard_map(
        local,
        mesh=grid,
        in_specs=(
            P(rows, None),
            P(),
            P(SEQ, None),
            P(SEQ, None),
            P(SEQ, None),
            P(),
            P(),
            P(rows, None, None),
            P(),
            P(),
            P(),
        ),
        out_specs=P(rows, None),
        check_vma=False,
    )
```

```python
import functools

import jax
import jax.numpy as jnp
from jax import lax
from jax.experimental import pallas as pl
from jax.experimental.pallas import tpu as pltpu
from jax.sharding import Mesh
from jax.sharding import PartitionSpec as P

SEQ = ("y", "x", "c")
PLANE = ("y", "x")
PARTS = 8
ROWS = 208
HALF = 4 * ROWS
NONE = -1e30
MASKED = -2e30
LOG2E = 1.4426950408889634


def tile_spans(tile_counts, starts, length, most_tiles):
    slots = tile_counts.shape[0]
    span_ends = jnp.concatenate([starts[1:], jnp.full((1,), length, jnp.int32)])
    offsets = jnp.cumsum(tile_counts) - tile_counts
    tile_total = jnp.sum(tile_counts)
    tile_ids = jnp.arange(most_tiles, dtype=jnp.int32)
    image_of = jnp.sum((offsets[None, :] <= tile_ids[:, None]).astype(jnp.int32), axis=1) - 1
    member = jnp.arange(slots, dtype=jnp.int32)[None, :] == image_of[:, None]
    tile_low = jnp.sum(jnp.where(member, starts[None, :], 0), axis=1)
    tile_high = jnp.sum(jnp.where(member, span_ends[None, :], 0), axis=1)
    return (tile_low, tile_high, tile_ids < tile_total)


def ring(step):
    return [(i, (i + step) % 4) for i in range(4)]


def norm_rows(values, gain):
    return values * lax.rsqrt(jnp.mean(values * values, axis=-1, keepdims=True) + 1e-05) * gain


AWAY = (0, -1, 1, 2)
CHAIN = 5
FULL = ((0, 0, 4), (1, 4, 4), (2, 8, 4), (3, 12, 2), (4, 14, 2))


def away(at, slot):
    return (at + AWAY[slot] + 4) % 4


def slot_of(at, place):
    ahead = (place - at + 4) % 4
    return jnp.where(ahead == 0, 0, jnp.where(ahead == 3, 1, ahead + 1))


def kv_kernel(tile_len, meta_ref, own_ref, other_ref, own_tail, other_tail, *refs):
    mine, swapped = refs[:CHAIN], refs[CHAIN : 2 * CHAIN]
    (gain_ref, out_ref, tile_buf, first_buf, second_buf, acc_ref, tile_sem, tail_sem, first_sem, second_sem) = refs[
        2 * CHAIN :
    ]
    core, own, y_at, x_at = (meta_ref[i] for i in range(4))
    whole = tile_len // 16 * 16 - HALF
    split, rest = first_buf.shape[2], second_buf.shape[2]

    def first_copy(chain, i):
        array, start, count = FULL[i]
        return pltpu.make_async_copy(chain[array], first_buf.at[pl.ds(start, count)], first_sem.at[i])

    def second_copy(chain, i):
        array, start, count = FULL[i]
        return pltpu.make_async_copy(
            chain[array].at[:, :, pl.ds(0, rest)], second_buf.at[pl.ds(start, count)], second_sem.at[i]
        )

    def tile_copies(i, source, tail, lower):
        at = pl.ds(pl.multiple_of(away(y_at, i) * 1024, 1024), 1024)
        to = pl.ds(i * 1024, 1024)
        if not lower:
            rows = pl.ds(0, HALF)
            return [pltpu.make_async_copy(source.at[rows, at], tile_buf.at[rows, to], tile_sem.at[i])]
        return [
            pltpu.make_async_copy(
                source.at[pl.ds(HALF, whole), at], tile_buf.at[pl.ds(0, whole), to], tile_sem.at[i]
            ),
            pltpu.make_async_copy(tail.at[:, at], tile_buf.at[pl.ds(whole, 16), to], tail_sem.at[i]),
        ]

    def start_tile(i):
        for from_own, source, tail in ((1, own_ref, own_tail), (0, other_ref, other_tail)):
            for lower in (0, 1):

                @pl.when((own == from_own) & (core == lower))
                def _(source=source, tail=tail, lower=lower):
                    for copy in tile_copies(i, source, tail, lower):
                        copy.start()

    for lower, first, second in ((0, mine, swapped), (1, swapped, mine)):

        @pl.when(core == lower)
        def _(first=first, second=second):
            first_copy(first, 0).start()
            for i in range(CHAIN):
                second_copy(second, i).start()

    start_tile(0)
    for lower, first in ((0, mine), (1, swapped)):

        @pl.when(core == lower)
        def _(first=first):
            for i in range(1, CHAIN):
                first_copy(first, i).start()

    for i in range(1, 4):
        start_tile(i)

    for i in range(4):
        first_copy(mine, i).wait()
        if i == 0:
            for j in range(CHAIN):
                second_copy(mine, j).wait()
        if i == 3:
            first_copy(mine, 4).wait()
        for lower in (0, 1):

            @pl.when(core == lower)
            def _(i=i, lower=lower):
                for copy in tile_copies(i, own_ref, own_tail, lower):
                    copy.wait()

        slots = [slot_of(x_at, x) for x in range(4)]
        tile = tile_buf[:, i * 1024 : (i + 1) * 1024]
        one = jnp.concatenate([first_buf[4 * i + slot] for slot in slots], axis=0)
        two = jnp.concatenate([second_buf[4 * slot + i] for slot in slots], axis=0)
        part_one = jnp.dot(tile, one, preferred_element_type=jnp.float32)
        part_two = jnp.dot(tile, two, preferred_element_type=jnp.float32)
        if i == 0:
            acc_ref[:, :split] = part_one
            acc_ref[:, split:] = part_two
        else:
            acc_ref[:, :split] += part_one
            acc_ref[:, split:] += part_two

    for y in range(4):
        held = tile_len - core * HALF - y * ROWS
        kept = lax.broadcasted_iota(jnp.int32, (ROWS, 128), 0) < held
        for h in range(4):
            at = slice(y * ROWS, (y + 1) * ROWS)
            keys = acc_ref[at, h * 128 : (h + 1) * 128]
            values = acc_ref[at, (h + 4) * 128 : (h + 5) * 128]
            if y == 3:
                keys, values = jnp.where(kept, keys, 0.0), jnp.where(kept, values, 0.0)
            out_ref[y * 4 + h, :, :128] = norm_rows(keys, gain_ref[...]).astype(jnp.bfloat16)
            out_ref[y * 4 + h, :, 128:] = values.astype(jnp.bfloat16)


def ragged_end(tile):
    whole = tile.shape[0] // 16 * 16
    return jnp.pad(tile[whole:], ((0, 16 - tile.shape[0] + whole), (0, 0)))


def project_kv(own, other, tails, chains, k_gain, meta):
    tile_len, depth = own.shape
    width, split = 1024, chains[0].shape[2]
    return pl.pallas_call(
        functools.partial(kv_kernel, tile_len),
        in_specs=[pl.BlockSpec(memory_space=pltpu.SMEM)]
        + [pl.BlockSpec(memory_space=pl.ANY)] * (4 + 2 * CHAIN)
        + [pl.BlockSpec(memory_space=pltpu.VMEM)],
        out_specs=pl.BlockSpec(memory_space=pltpu.VMEM),
        out_shape=jax.ShapeDtypeStruct((16, ROWS, 256), jnp.bfloat16),
        scratch_shapes=[
            pltpu.VMEM((HALF, depth), jnp.bfloat16),
            pltpu.VMEM((16, 256, split), jnp.bfloat16),
            pltpu.VMEM((16, 256, width - split), jnp.bfloat16),
            pltpu.VMEM((HALF, width), jnp.float32),
        ]
        + [pltpu.SemaphoreType.DMA((4,))] * 2
        + [pltpu.SemaphoreType.DMA((CHAIN,))] * 2,
        compiler_params=pltpu.CompilerParams(vmem_limit_bytes=32 * 2**20),
        cost_estimate=pl.CostEstimate(
            flops=2 * HALF * depth * width, bytes_accessed=2 * (HALF + width) * depth, transcendentals=0
        ),
        name="kv_projection",
    )(meta, own, other, *tails, *chains, k_gain)


def attend_kernel(pad, meta_ref, q_ref, *refs):
    part_refs, (out_ref, m_ref, l_ref, acc_ref) = refs[:-4], refs[-4:]
    tile = pl.program_id(0)
    blocks, rows, width = q_ref.shape
    heads = width // 128
    keys = PARTS * ROWS
    factor = LOG2E / 128**0.5
    pairs = heads // 2

    @pl.when(tile == 0)
    def _():
        m_ref[...] = jnp.full_like(m_ref, NONE)
        l_ref[...] = jnp.zeros_like(l_ref)
        acc_ref[...] = jnp.zeros_like(acc_ref)

    low, high = meta_ref[tile], meta_ref[4 + tile]
    some = False
    for b in range(blocks):
        first = meta_ref[8 + b]
        some = some | ((low < first + rows) & (high > first))

    @pl.when(some)
    def _():
        held = []
        for own, before, after, low_tiles, high_tiles in (part_refs[:5], part_refs[5:]):
            held += [own[0], before[0], after[0], jnp.where(tile < 2, low_tiles[0], high_tiles[0])]
        kv = jnp.concatenate(held, axis=0)
        row = lax.broadcasted_iota(jnp.int32, (keys, 128), 0)
        lane = lax.broadcasted_iota(jnp.int32, (keys, 128), 1)
        padding = (row >= meta_ref[8 + blocks]) & (row < meta_ref[8 + blocks] + pad)
        key_mask = jnp.where((lane == 0) & padding, MASKED, jnp.where(lane == 1, 1.0, 0.0))
        key = jnp.concatenate([kv[:, :128], key_mask.astype(jnp.bfloat16)], axis=1)
        value = jnp.concatenate([kv[:, 128:], jnp.ones((keys, 128), jnp.bfloat16)], axis=1)
        text_row = lax.broadcasted_iota(jnp.int32, (rows, 128), 0)
        text_lane = lax.broadcasted_iota(jnp.int32, (rows, 128), 1)

        def score(group):
            b, h = group // pairs, group % pairs * 2
            at = meta_ref[8 + b] + text_row
            outside = (at < low) | (at >= high)
            mask = jnp.where((text_lane == 1) & outside, MASKED, jnp.where(text_lane == 0, 1.0, 0.0))
            mask = mask.astype(jnp.bfloat16)
            both = [
                jnp.concatenate([q_ref[b, :, i * 128 : (i + 1) * 128], mask], axis=1) for i in (h, h + 1)
            ]
            return lax.dot_general(
                jnp.concatenate(both, axis=0), key, (((1,), (1,)), ((), ())), preferred_element_type=jnp.float32
            )

        def soften(group, scores):
            m_old = m_ref[group]
            m_new = jnp.maximum(m_old, jnp.max(scores, axis=1, keepdims=True))
            probs = jnp.exp2((scores - m_new) * factor)
            alpha = jnp.exp2((m_old - m_new) * factor)
            m_ref[group] = m_new
            summed = jnp.dot(probs.astype(jnp.bfloat16), value, preferred_element_type=jnp.float32)
            l_ref[group] = l_ref[group] * alpha + summed[:, 128:129]
            acc_ref[group] = acc_ref[group] * alpha + summed[:, :128]

        scores = score(0)
        for group in range(blocks * pairs):
            ahead = score(group + 1) if group + 1 < blocks * pairs else None
            soften(group, scores)
            scores = ahead

    @pl.when(tile == pl.num_programs(0) - 1)
    def _():
        for b in range(blocks):
            for h in range(heads):
                group, at = b * pairs + h // 2, slice(h % 2 * rows, (h % 2 + 1) * rows)
                out_ref[b, :, h * 128 : (h + 1) * 128] = (
                    acc_ref[group, at] / jnp.maximum(l_ref[group, at], 1.0)
                ).astype(jnp.bfloat16)


def attend(query, parts, meta, pad):
    blocks, rows, width = query.shape
    tiles = parts[0].shape[0]
    groups = blocks * width // 256
    return pl.pallas_call(
        functools.partial(attend_kernel, pad),
        grid_spec=pltpu.PrefetchScalarGridSpec(
            num_scalar_prefetch=1,
            grid=(tiles,),
            in_specs=[
                pl.BlockSpec((blocks, rows, width), lambda j, meta: (0, 0, 0)),
            ]
            + (
                [pl.BlockSpec((1, ROWS, 256), lambda j, meta: (j, 0, 0))] * 3
                + [pl.BlockSpec((1, ROWS, 256), lambda j, meta: (jnp.minimum(j, 1), 0, 0))]
                + [pl.BlockSpec((1, ROWS, 256), lambda j, meta: (jnp.maximum(j - 2, 0), 0, 0))]
            )
            * 2,
            out_specs=pl.BlockSpec((blocks, rows, width), lambda j, meta: (0, 0, 0)),
            scratch_shapes=[
                pltpu.VMEM((groups, 2 * rows, 1), jnp.float32),
                pltpu.VMEM((groups, 2 * rows, 1), jnp.float32),
                pltpu.VMEM((groups, 2 * rows, 128), jnp.float32),
            ],
        ),
        out_shape=jax.ShapeDtypeStruct(query.shape, jnp.bfloat16),
        compiler_params=pltpu.CompilerParams(vmem_limit_bytes=40 * 2**20),
        cost_estimate=pl.CostEstimate(
            flops=8 * blocks * rows * width * tiles * PARTS * ROWS,
            bytes_accessed=512 * tiles * PARTS * ROWS,
            transcendentals=blocks * rows * width // 128 * tiles * PARTS * ROWS,
        ),
        name="attention",
    )(meta, query, *parts)


def query_kernel(meta_ref, *refs):
    text_refs, refs = refs[:8], refs[8:]
    mine, swapped = refs[:CHAIN], refs[CHAIN : 2 * CHAIN]
    gain_ref, out_ref, weight_buf, acc_ref, sems = refs[2 * CHAIN :]
    core, y_at, x_at = meta_ref[0], meta_ref[2], meta_ref[3]
    width = weight_buf.shape[2]
    skip = mine[0].shape[2] - width

    def weight_copy(chain, i):
        array, start, count = FULL[i]
        return pltpu.make_async_copy(
            chain[array].at[:, :, pl.ds(skip, width)], weight_buf.at[pl.ds(start, count)], sems.at[i]
        )

    for lower, second in ((0, swapped), (1, mine)):

        @pl.when(core == lower)
        def _(second=second):
            for i in range(CHAIN):
                weight_copy(second, i).start()

    for j in range(4):
        weight_copy(mine, j).wait()
        if j == 3:
            weight_copy(mine, 4).wait()
        columns = []
        for i in range(4):
            chip = away(y_at, i) * 4 + away(x_at, j)
            at = pl.ds(pl.multiple_of(chip * 256, 256), 256)
            columns.append(jnp.concatenate([ref[:, at] for ref in text_refs], axis=0))
        part = jnp.dot(
            jnp.concatenate(columns, axis=1),
            weight_buf[4 * j : 4 * j + 4].reshape(1024, width),
            preferred_element_type=jnp.float32,
        )
        if j == 0:
            acc_ref[...] = part
        else:
            acc_ref[...] += part

    for b in range(4):
        for h in range(width // 128):
            block = acc_ref[b * 128 : (b + 1) * 128, h * 128 : (h + 1) * 128]
            out_ref[b, :, h * 128 : (h + 1) * 128] = norm_rows(block, gain_ref[...]).astype(jnp.bfloat16)


def project_query(texts, chains, gain, meta):
    rows, depth = 2 * texts[0].shape[0], texts[0].shape[1]
    width = 512
    return pl.pallas_call(
        query_kernel,
        in_specs=[pl.BlockSpec(memory_space=pltpu.SMEM)]
        + [pl.BlockSpec(memory_space=pltpu.VMEM)] * 8
        + [pl.BlockSpec(memory_space=pl.ANY)] * (2 * CHAIN)
        + [pl.BlockSpec(memory_space=pltpu.VMEM)],
        out_specs=pl.BlockSpec(memory_space=pltpu.VMEM),
        out_shape=jax.ShapeDtypeStruct((4, rows, width), jnp.bfloat16),
        scratch_shapes=[
            pltpu.VMEM((16, 256, width), jnp.bfloat16),
            pltpu.VMEM((4 * rows, width), jnp.float32),
            pltpu.SemaphoreType.DMA((CHAIN,)),
        ],
        compiler_params=pltpu.CompilerParams(vmem_limit_bytes=32 * 2**20),
        cost_estimate=pl.CostEstimate(
            flops=8 * rows * depth * width, bytes_accessed=2 * (4 * rows + width) * depth, transcendentals=0
        ),
        name="query_projection",
    )(meta, *texts, *chains, gain)


def gather(k_weight, v_weight, q_share, tile_rows, normed, core):
    cut = v_weight.shape[1] // 2
    halves = (
        jnp.concatenate([k_weight, v_weight[:, :cut]], axis=1),
        jnp.concatenate([v_weight[:, cut:], q_share], axis=1),
    )
    swap = [(0, 1), (1, 0)]
    kept = jnp.where(core == 0, halves[0], halves[1])
    got = lax.ppermute(jnp.where(core == 0, halves[1], halves[0]), "c", swap)
    got, tile_rows = lax.optimization_barrier((got, tile_rows))
    other_rows = lax.ppermute(tile_rows, "c", swap)
    chip = jnp.where(core == 0, jnp.concatenate([kept, got]), jnp.concatenate([got, kept]))

    def move(piece, step, turn):
        pairs = []
        for y in range(4):
            for x in range(4):
                for c in range(2):
                    to = (y, (x + step) % 4) if (c == 0) == (turn == 0) else ((y + step) % 4, x)
                    pairs.append(((y * 4 + x) * 2 + c, (to[0] * 4 + to[1]) * 2 + c))
        return lax.ppermute(piece, SEQ, pairs)

    def climb(piece, step):
        return lax.ppermute(piece, "z", ring(step))

    half = normed.shape[0] // 2
    upper, lower = normed[:half], normed[half:]
    texts = [upper, lower, climb(upper, 1), None, None, None, climb(upper, -1), None]
    line = jnp.stack([chip, move(chip, 1, 0), move(chip, -1, 0), move(chip, 2, 0)])
    line, texts[2], texts[6], lower = lax.optimization_barrier((line, texts[2], texts[6], lower))
    before, after = move(line, 1, 1), move(line, -1, 1)
    texts[3], texts[7] = climb(lower, 1), climb(lower, -1)
    before, after, texts[3], texts[7] = lax.optimization_barrier((before, after, texts[3], texts[7]))
    chain = [line, before, after, move(before[:2], 1, 1), move(after[2:], -1, 1)]
    texts[4], texts[5] = climb(texts[2], 1), climb(texts[7], -1)
    chain += [lax.ppermute(piece, "c", swap) for piece in chain]
    return chain, other_rows, texts


def local(
    text,
    norm_gain,
    q_weight,
    k_weight,
    v_weight,
    q_gain,
    k_gain,
    vision,
    tiles_per_image,
    image_start,
    tile_owner,
):
    row_count = text.shape[0]
    head_dim = q_gain.shape[0]
    heads_kv = k_weight.shape[1] // head_dim
    tile_rows = vision[0]
    tile_len = tile_rows.shape[0]
    most_tiles = tile_owner.shape[1]
    length = row_count * lax.axis_size(SEQ)
    at_doc, at_y, at_x, at_core = (lax.axis_index(a) for a in ("z", "y", "x", "c"))

    group_width = q_weight.shape[1] // heads_kv
    q_share = lax.dynamic_slice_in_dim(q_weight, at_doc * group_width, group_width, 1)
    text_wide = text.astype(jnp.float32)
    normed = norm_rows(text_wide, norm_gain).astype(jnp.bfloat16)
    chains, other_rows, texts = gather(k_weight, v_weight, q_share, tile_rows, normed, at_core)
    tails = (ragged_end(tile_rows), ragged_end(other_rows))
    chains, other_rows, tails = lax.optimization_barrier((chains, other_rows, tails))

    totals = jnp.sum(tiles_per_image, axis=1)
    valid = jnp.arange(most_tiles, dtype=jnp.int32)[None, :] < totals[:, None]
    owned = jnp.any(
        (tile_owner[:, :, None] == jnp.arange(lax.axis_size(SEQ), dtype=jnp.int32)) & valid[:, :, None], axis=1
    )
    owned = owned.reshape(owned.shape[0], -1, 2)
    crowded = jnp.any(owned[:, :, 0] & owned[:, :, 1])
    picked = jnp.arange(tiles_per_image.shape[0], dtype=jnp.int32) == at_doc
    tile_counts = jnp.sum(jnp.where(picked[:, None], tiles_per_image, 0), axis=0)
    starts = jnp.sum(jnp.where(picked[:, None], image_start, 0), axis=0)
    owners = jnp.sum(jnp.where(picked[:, None], tile_owner, 0), axis=0)
    first_core = jnp.any(owned & picked[:, None, None], axis=0)[:, 0]
    tile_low, tile_high, tile_valid = tile_spans(tile_counts, starts, length, most_tiles)
    tile_low = jnp.where(tile_valid, tile_low, 2 * length)
    tile_high = jnp.where(tile_valid, tile_high, 0)

    chip_first = jnp.sum(
        jnp.where(jnp.arange(first_core.shape[0]) == at_y * 4 + at_x, first_core.astype(jnp.int32), 0)
    )
    source = 1 - chip_first
    gain_row = k_gain.reshape(1, head_dim)
    chip_of = owners // 2
    turn = jnp.where((owners % 2 == 1) & first_core[chip_of], 1, 0)

    def project(from_core):
        use_own = (at_core == from_core).astype(jnp.int32)
        meta = jnp.stack([at_core, use_own, at_y, at_x]).astype(jnp.int32)
        return project_kv(tile_rows, other_rows, tails, chains, gain_row, meta)

    pieces, chains, texts = lax.optimization_barrier((project(source), chains, texts))

    def send(sent):
        return lax.all_to_all(sent, PLANE, 0, 0, tiled=True)

    def pick(got):
        return jnp.stack([got[chip_of[j]] for j in range(most_tiles)])

    def ask():
        meta = jnp.stack([at_core, at_core, at_y, at_x]).astype(jnp.int32)
        query = project_query(texts, chains, q_gain.reshape(1, head_dim), meta)
        return jnp.stack([query[0]] + [lax.ppermute(query[k], "z", ring(-k)) for k in (1, 2, 3)])

    def spread_one():
        got, mine = lax.optimization_barrier((send(pieces), ask()))
        return pick(got), mine

    def spread_two():
        got, second = lax.optimization_barrier((send(pieces), project(1)))
        later, mine = lax.optimization_barrier((send(second), ask()))
        return jnp.where((turn > 0)[:, None, None], pick(later), pick(got)), mine

    chosen, mine = lax.cond(crowded, spread_two, spread_one)

    before, after = lax.ppermute(chosen, "y", ring(1)), lax.ppermute(chosen, "y", ring(-1))
    half = most_tiles // 2
    opposite = [lax.ppermute(before[:half], "y", ring(1)), lax.ppermute(after[half:], "y", ring(-1))]
    parts = [chosen, before, after, *opposite]
    parts += [lax.ppermute(part, "c", [(0, 1), (1, 0)]) for part in parts]
    query = [mine[(at_x + s - at_doc) % 4] for s in range(4)]
    query = [query[0]] + [lax.ppermute(query[s], "x", ring(s)) for s in (1, 2, 3)]
    last_slot = jnp.array([1, 3, 2, 0], jnp.int32)[at_y]
    last_part = jnp.where(at_core == 1, last_slot, last_slot + 4)
    pad = 2 * HALF - tile_len
    pad_row = (last_part + 1) * ROWS - pad

    token_x = (at_x - jnp.arange(4, dtype=jnp.int32)) % 4
    blocks = ((at_y * 4 + token_x) * 2 + at_core) * row_count
    spans = jnp.concatenate([tile_low, tile_high])
    context = attend(jnp.stack(query), parts, jnp.concatenate([spans, blocks, pad_row[None]]), pad)
    context = [context[0]] + [lax.ppermute(context[k], "x", ring(-k)) for k in (1, 2, 3)]
    context = jnp.stack(context)
    return jnp.concatenate([context[(h - at_x) % 4] for h in range(heads_kv)], axis=1)


def solution(mesh):
    grid = Mesh(mesh.devices.reshape(4, 4, 4, 2), ("z", "y", "x", "c"))
    rows = ("z", "y", "x", "c")
    return jax.shard_map(
        local,
        mesh=grid,
        in_specs=(
            P(rows, None),
            P(),
            P(SEQ, None),
            P(SEQ, None),
            P(SEQ, None),
            P(),
            P(),
            P(rows, None, None),
            P(),
            P(),
            P(),
        ),
        out_specs=P(rows, None),
        check_vma=False,
    )
```

```python
import functools

import jax
import jax.numpy as jnp
from jax import lax
from jax.experimental import pallas as pl
from jax.experimental.pallas import tpu as pltpu
from jax.sharding import Mesh
from jax.sharding import PartitionSpec as P

SEQ = ("y", "x", "c")
PLANE = ("y", "x")
PARTS = 8
ROWS = 208
HALF = 4 * ROWS
NONE = -1e30
MASKED = -2e30
LOG2E = 1.4426950408889634


def tile_spans(tile_counts, starts, length, most_tiles):
    slots = tile_counts.shape[0]
    span_ends = jnp.concatenate([starts[1:], jnp.full((1,), length, jnp.int32)])
    offsets = jnp.cumsum(tile_counts) - tile_counts
    tile_total = jnp.sum(tile_counts)
    tile_ids = jnp.arange(most_tiles, dtype=jnp.int32)
    image_of = jnp.sum((offsets[None, :] <= tile_ids[:, None]).astype(jnp.int32), axis=1) - 1
    member = jnp.arange(slots, dtype=jnp.int32)[None, :] == image_of[:, None]
    tile_low = jnp.sum(jnp.where(member, starts[None, :], 0), axis=1)
    tile_high = jnp.sum(jnp.where(member, span_ends[None, :], 0), axis=1)
    return (tile_low, tile_high, tile_ids < tile_total)


def ring(step):
    return [(i, (i + step) % 4) for i in range(4)]


def norm_rows(values, gain):
    return values * lax.rsqrt(jnp.mean(values * values, axis=-1, keepdims=True) + 1e-05) * gain


AWAY = (0, -1, 1, 2)
CHAIN = 8


def away(at, slot):
    return (at + AWAY[slot] + 4) % 4


def slot_of(at, place):
    ahead = (place - at + 4) % 4
    return jnp.where(ahead == 0, 0, jnp.where(ahead == 3, 1, ahead + 1))


def kv_kernel(tile_len, meta_ref, own_ref, other_ref, own_tail, other_tail, *refs):
    mine, swapped = refs[:CHAIN], refs[CHAIN : 2 * CHAIN]
    (gain_ref, out_ref, tile_buf, first_buf, second_buf, acc_ref, tile_sem, tail_sem, first_sem, second_sem) = refs[
        2 * CHAIN :
    ]
    core, own, y_at, x_at = (meta_ref[i] for i in range(4))
    whole = tile_len // 16 * 16 - HALF
    split, rest = first_buf.shape[2], second_buf.shape[2]

    def first_copy(chain, i):
        return pltpu.make_async_copy(chain[i], first_buf.at[pl.ds(2 * i, 2)], first_sem.at[i])

    def second_copy(chain, i):
        return pltpu.make_async_copy(
            chain[i].at[:, :, pl.ds(0, rest)], second_buf.at[pl.ds(2 * i, 2)], second_sem.at[i]
        )

    def tile_copies(i, source, tail, lower):
        at = pl.ds(pl.multiple_of(away(y_at, i) * 1024, 1024), 1024)
        to = pl.ds(i * 1024, 1024)
        if not lower:
            rows = pl.ds(0, HALF)
            return [pltpu.make_async_copy(source.at[rows, at], tile_buf.at[rows, to], tile_sem.at[i])]
        return [
            pltpu.make_async_copy(
                source.at[pl.ds(HALF, whole), at], tile_buf.at[pl.ds(0, whole), to], tile_sem.at[i]
            ),
            pltpu.make_async_copy(tail.at[:, at], tile_buf.at[pl.ds(whole, 16), to], tail_sem.at[i]),
        ]

    def start_tile(i):
        for from_own, source, tail in ((1, own_ref, own_tail), (0, other_ref, other_tail)):
            for lower in (0, 1):

                @pl.when((own == from_own) & (core == lower))
                def _(source=source, tail=tail, lower=lower):
                    for copy in tile_copies(i, source, tail, lower):
                        copy.start()

    for lower, first, second in ((0, mine, swapped), (1, swapped, mine)):

        @pl.when(core == lower)
        def _(first=first, second=second):
            for i in range(2):
                first_copy(first, i).start()
            for i in range(CHAIN):
                second_copy(second, i).start()

    start_tile(0)
    for lower, first in ((0, mine), (1, swapped)):

        @pl.when(core == lower)
        def _(first=first):
            for i in range(2, CHAIN):
                first_copy(first, i).start()

    for i in range(1, 4):
        start_tile(i)

    for i in range(4):
        first_copy(mine, 2 * i).wait()
        first_copy(mine, 2 * i + 1).wait()
        if i == 0:
            for j in range(CHAIN):
                second_copy(mine, j).wait()
        for lower in (0, 1):

            @pl.when(core == lower)
            def _(i=i, lower=lower):
                for copy in tile_copies(i, own_ref, own_tail, lower):
                    copy.wait()

        slots = [slot_of(x_at, x) for x in range(4)]
        tile = tile_buf[:, i * 1024 : (i + 1) * 1024]
        one = jnp.concatenate([first_buf[4 * i + slot] for slot in slots], axis=0)
        two = jnp.concatenate([second_buf[4 * slot + i] for slot in slots], axis=0)
        part_one = jnp.dot(tile, one, preferred_element_type=jnp.float32)
        part_two = jnp.dot(tile, two, preferred_element_type=jnp.float32)
        if i == 0:
            acc_ref[:, :split] = part_one
            acc_ref[:, split:] = part_two
        else:
            acc_ref[:, :split] += part_one
            acc_ref[:, split:] += part_two

    for y in range(4):
        held = tile_len - core * HALF - y * ROWS
        kept = lax.broadcasted_iota(jnp.int32, (ROWS, 128), 0) < held
        for h in range(4):
            at = slice(y * ROWS, (y + 1) * ROWS)
            keys = acc_ref[at, h * 128 : (h + 1) * 128]
            values = acc_ref[at, (h + 4) * 128 : (h + 5) * 128]
            if y == 3:
                keys, values = jnp.where(kept, keys, 0.0), jnp.where(kept, values, 0.0)
            out_ref[y * 4 + h, :, :128] = norm_rows(keys, gain_ref[...]).astype(jnp.bfloat16)
            out_ref[y * 4 + h, :, 128:] = values.astype(jnp.bfloat16)


def ragged_end(tile):
    whole = tile.shape[0] // 16 * 16
    return jnp.pad(tile[whole:], ((0, 16 - tile.shape[0] + whole), (0, 0)))


def project_kv(own, other, tails, chains, k_gain, meta):
    tile_len, depth = own.shape
    width, split = 1024, chains[0].shape[2]
    return pl.pallas_call(
        functools.partial(kv_kernel, tile_len),
        in_specs=[pl.BlockSpec(memory_space=pltpu.SMEM)]
        + [pl.BlockSpec(memory_space=pl.ANY)] * (4 + 2 * CHAIN)
        + [pl.BlockSpec(memory_space=pltpu.VMEM)],
        out_specs=pl.BlockSpec(memory_space=pltpu.VMEM),
        out_shape=jax.ShapeDtypeStruct((16, ROWS, 256), jnp.bfloat16),
        scratch_shapes=[
            pltpu.VMEM((HALF, depth), jnp.bfloat16),
            pltpu.VMEM((16, 256, split), jnp.bfloat16),
            pltpu.VMEM((16, 256, width - split), jnp.bfloat16),
            pltpu.VMEM((HALF, width), jnp.float32),
        ]
        + [pltpu.SemaphoreType.DMA((4,))] * 2
        + [pltpu.SemaphoreType.DMA((CHAIN,))] * 2,
        compiler_params=pltpu.CompilerParams(vmem_limit_bytes=52 * 2**20),
        cost_estimate=pl.CostEstimate(
            flops=2 * HALF * depth * width, bytes_accessed=2 * (HALF + width) * depth, transcendentals=0
        ),
        name="kv_projection",
    )(meta, own, other, *tails, *chains, k_gain)


def attend_kernel(pad, meta_ref, q_ref, *refs):
    part_refs, (out_ref, m_ref, l_ref, acc_ref) = refs[:-4], refs[-4:]
    tile = pl.program_id(0)
    blocks, rows, width = q_ref.shape
    heads = width // 128
    keys = PARTS * ROWS
    factor = LOG2E / 128**0.5
    pairs = heads // 2

    @pl.when(tile == 0)
    def _():
        m_ref[...] = jnp.full_like(m_ref, NONE)
        l_ref[...] = jnp.zeros_like(l_ref)
        acc_ref[...] = jnp.zeros_like(acc_ref)

    low, high = meta_ref[tile], meta_ref[4 + tile]
    some = False
    for b in range(blocks):
        first = meta_ref[8 + b]
        some = some | ((low < first + rows) & (high > first))

    @pl.when(some)
    def _():
        held = []
        for own, before, after, low_tiles, high_tiles in (part_refs[:5], part_refs[5:]):
            held += [own[0], before[0], after[0], jnp.where(tile < 2, low_tiles[0], high_tiles[0])]
        kv = jnp.concatenate(held, axis=0)
        row = lax.broadcasted_iota(jnp.int32, (keys, 128), 0)
        lane = lax.broadcasted_iota(jnp.int32, (keys, 128), 1)
        padding = (row >= meta_ref[8 + blocks]) & (row < meta_ref[8 + blocks] + pad)
        key_mask = jnp.where((lane == 0) & padding, MASKED, jnp.where(lane == 1, 1.0, 0.0))
        key = jnp.concatenate([kv[:, :128], key_mask.astype(jnp.bfloat16)], axis=1)
        value = jnp.concatenate([kv[:, 128:], jnp.ones((keys, 128), jnp.bfloat16)], axis=1)
        text_row = lax.broadcasted_iota(jnp.int32, (rows, 128), 0)
        text_lane = lax.broadcasted_iota(jnp.int32, (rows, 128), 1)

        def score(group):
            b, h = group // pairs, group % pairs * 2
            at = meta_ref[8 + b] + text_row
            outside = (at < low) | (at >= high)
            mask = jnp.where((text_lane == 1) & outside, MASKED, jnp.where(text_lane == 0, 1.0, 0.0))
            mask = mask.astype(jnp.bfloat16)
            both = [
                jnp.concatenate([q_ref[b, :, i * 128 : (i + 1) * 128], mask], axis=1) for i in (h, h + 1)
            ]
            return lax.dot_general(
                jnp.concatenate(both, axis=0), key, (((1,), (1,)), ((), ())), preferred_element_type=jnp.float32
            )

        def soften(group, scores):
            m_old = m_ref[group]
            m_new = jnp.maximum(m_old, jnp.max(scores, axis=1, keepdims=True))
            probs = jnp.exp2((scores - m_new) * factor)
            alpha = jnp.exp2((m_old - m_new) * factor)
            m_ref[group] = m_new
            summed = jnp.dot(probs.astype(jnp.bfloat16), value, preferred_element_type=jnp.float32)
            l_ref[group] = l_ref[group] * alpha + summed[:, 128:129]
            acc_ref[group] = acc_ref[group] * alpha + summed[:, :128]

        scores = score(0)
        for group in range(blocks * pairs):
            ahead = score(group + 1) if group + 1 < blocks * pairs else None
            soften(group, scores)
            scores = ahead

    @pl.when(tile == pl.num_programs(0) - 1)
    def _():
        for b in range(blocks):
            for h in range(heads):
                group, at = b * pairs + h // 2, slice(h % 2 * rows, (h % 2 + 1) * rows)
                out_ref[b, :, h * 128 : (h + 1) * 128] = (
                    acc_ref[group, at] / jnp.maximum(l_ref[group, at], 1.0)
                ).astype(jnp.bfloat16)


def attend(query, parts, meta, pad):
    blocks, rows, width = query.shape
    tiles = parts[0].shape[0]
    groups = blocks * width // 256
    return pl.pallas_call(
        functools.partial(attend_kernel, pad),
        grid_spec=pltpu.PrefetchScalarGridSpec(
            num_scalar_prefetch=1,
            grid=(tiles,),
            in_specs=[
                pl.BlockSpec((blocks, rows, width), lambda j, meta: (0, 0, 0)),
            ]
            + (
                [pl.BlockSpec((1, ROWS, 256), lambda j, meta: (j, 0, 0))] * 3
                + [pl.BlockSpec((1, ROWS, 256), lambda j, meta: (jnp.minimum(j, 1), 0, 0))]
                + [pl.BlockSpec((1, ROWS, 256), lambda j, meta: (jnp.maximum(j - 2, 0), 0, 0))]
            )
            * 2,
            out_specs=pl.BlockSpec((blocks, rows, width), lambda j, meta: (0, 0, 0)),
            scratch_shapes=[
                pltpu.VMEM((groups, 2 * rows, 1), jnp.float32),
                pltpu.VMEM((groups, 2 * rows, 1), jnp.float32),
                pltpu.VMEM((groups, 2 * rows, 128), jnp.float32),
            ],
        ),
        out_shape=jax.ShapeDtypeStruct(query.shape, jnp.bfloat16),
        compiler_params=pltpu.CompilerParams(vmem_limit_bytes=48 * 2**20),
        cost_estimate=pl.CostEstimate(
            flops=8 * blocks * rows * width * tiles * PARTS * ROWS,
            bytes_accessed=512 * tiles * PARTS * ROWS,
            transcendentals=blocks * rows * width // 128 * tiles * PARTS * ROWS,
        ),
        name="attention",
    )(meta, query, *parts)


def query_kernel(meta_ref, *refs):
    text_refs, refs = refs[:8], refs[8:]
    mine, swapped = refs[:CHAIN], refs[CHAIN : 2 * CHAIN]
    gain_ref, out_ref, weight_buf, acc_ref, sems = refs[2 * CHAIN :]
    core, y_at, x_at = meta_ref[0], meta_ref[2], meta_ref[3]
    width = weight_buf.shape[2]
    skip = mine[0].shape[2] - width

    def weight_copy(chain, i):
        return pltpu.make_async_copy(
            chain[i].at[:, :, pl.ds(skip, width)], weight_buf.at[pl.ds(2 * i, 2)], sems.at[i]
        )

    for lower, second in ((0, swapped), (1, mine)):

        @pl.when(core == lower)
        def _(second=second):
            for i in range(CHAIN):
                weight_copy(second, i).start()

    for j in range(4):
        weight_copy(mine, 2 * j).wait()
        weight_copy(mine, 2 * j + 1).wait()
        columns = []
        for i in range(4):
            chip = away(y_at, i) * 4 + away(x_at, j)
            at = pl.ds(pl.multiple_of(chip * 256, 256), 256)
            columns.append(jnp.concatenate([ref[:, at] for ref in text_refs], axis=0))
        part = jnp.dot(
            jnp.concatenate(columns, axis=1),
            weight_buf[4 * j : 4 * j + 4].reshape(1024, width),
            preferred_element_type=jnp.float32,
        )
        if j == 0:
            acc_ref[...] = part
        else:
            acc_ref[...] += part

    for b in range(4):
        for h in range(width // 128):
            block = acc_ref[b * 128 : (b + 1) * 128, h * 128 : (h + 1) * 128]
            out_ref[b, :, h * 128 : (h + 1) * 128] = norm_rows(block, gain_ref[...]).astype(jnp.bfloat16)


def project_query(texts, chains, gain, meta):
    rows, depth = 2 * texts[0].shape[0], texts[0].shape[1]
    width = 512
    return pl.pallas_call(
        query_kernel,
        in_specs=[pl.BlockSpec(memory_space=pltpu.SMEM)]
        + [pl.BlockSpec(memory_space=pltpu.VMEM)] * 8
        + [pl.BlockSpec(memory_space=pl.ANY)] * (2 * CHAIN)
        + [pl.BlockSpec(memory_space=pltpu.VMEM)],
        out_specs=pl.BlockSpec(memory_space=pltpu.VMEM),
        out_shape=jax.ShapeDtypeStruct((4, rows, width), jnp.bfloat16),
        scratch_shapes=[
            pltpu.VMEM((16, 256, width), jnp.bfloat16),
            pltpu.VMEM((4 * rows, width), jnp.float32),
            pltpu.SemaphoreType.DMA((CHAIN,)),
        ],
        compiler_params=pltpu.CompilerParams(vmem_limit_bytes=32 * 2**20),
        cost_estimate=pl.CostEstimate(
            flops=8 * rows * depth * width, bytes_accessed=2 * (4 * rows + width) * depth, transcendentals=0
        ),
        name="query_projection",
    )(meta, *texts, *chains, gain)


def gather(k_weight, v_weight, q_share, tile_rows, normed, core):
    cut = v_weight.shape[1] // 2
    halves = (
        jnp.concatenate([k_weight, v_weight[:, :cut]], axis=1),
        jnp.concatenate([v_weight[:, cut:], q_share], axis=1),
    )
    swap = [(0, 1), (1, 0)]
    kept = jnp.where(core == 0, halves[0], halves[1])
    got = lax.ppermute(jnp.where(core == 0, halves[1], halves[0]), "c", swap)
    got, tile_rows = lax.optimization_barrier((got, tile_rows))
    other_rows = lax.ppermute(tile_rows, "c", swap)
    chip = jnp.where(core == 0, jnp.concatenate([kept, got]), jnp.concatenate([got, kept]))

    def move(piece, step, turn):
        pairs = []
        for y in range(4):
            for x in range(4):
                for c in range(2):
                    to = (y, (x + step) % 4) if (c == 0) == (turn == 0) else ((y + step) % 4, x)
                    pairs.append(((y * 4 + x) * 2 + c, (to[0] * 4 + to[1]) * 2 + c))
        return lax.ppermute(piece, SEQ, pairs)

    def climb(piece, step):
        return lax.ppermute(piece, "z", ring(step))

    half = normed.shape[0] // 2
    upper, lower = normed[:half], normed[half:]
    texts = [upper, lower, climb(upper, 1), None, None, None, climb(upper, -1), None]
    near = jnp.stack([chip, move(chip, 1, 0)])
    far = jnp.stack([move(chip, -1, 0), move(chip, 2, 0)])
    near, far = lax.optimization_barrier((near, far))
    before = [move(near, 1, 1), move(far, 1, 1)]
    after = [move(near, -1, 1), move(far, -1, 1)]
    before, after, texts, lower = lax.optimization_barrier((before, after, texts, lower))
    texts[3], texts[7] = climb(lower, 1), climb(lower, -1)
    opposite = [move(before[0], 1, 1), move(after[1], -1, 1)]
    opposite, texts = lax.optimization_barrier((opposite, texts))
    chain = [near, far, *before, *after, *opposite]
    texts[4], texts[5] = climb(texts[2], 1), climb(texts[7], -1)
    chain += [lax.ppermute(piece, "c", swap) for piece in chain]
    return chain, other_rows, texts


def local(
    text,
    norm_gain,
    q_weight,
    k_weight,
    v_weight,
    q_gain,
    k_gain,
    vision,
    tiles_per_image,
    image_start,
    tile_owner,
):
    row_count = text.shape[0]
    head_dim = q_gain.shape[0]
    heads_kv = k_weight.shape[1] // head_dim
    tile_rows = vision[0]
    tile_len = tile_rows.shape[0]
    most_tiles = tile_owner.shape[1]
    length = row_count * lax.axis_size(SEQ)
    at_doc, at_y, at_x, at_core = (lax.axis_index(a) for a in ("z", "y", "x", "c"))

    group_width = q_weight.shape[1] // heads_kv
    q_share = lax.dynamic_slice_in_dim(q_weight, at_doc * group_width, group_width, 1)
    text_wide = text.astype(jnp.float32)
    normed = norm_rows(text_wide, norm_gain).astype(jnp.bfloat16)
    chains, other_rows, texts = gather(k_weight, v_weight, q_share, tile_rows, normed, at_core)
    tails = (ragged_end(tile_rows), ragged_end(other_rows))
    chains, other_rows, tails = lax.optimization_barrier((chains, other_rows, tails))

    totals = jnp.sum(tiles_per_image, axis=1)
    valid = jnp.arange(most_tiles, dtype=jnp.int32)[None, :] < totals[:, None]
    owned = jnp.any(
        (tile_owner[:, :, None] == jnp.arange(lax.axis_size(SEQ), dtype=jnp.int32)) & valid[:, :, None], axis=1
    )
    owned = owned.reshape(owned.shape[0], -1, 2)
    crowded = jnp.any(owned[:, :, 0] & owned[:, :, 1])
    picked = jnp.arange(tiles_per_image.shape[0], dtype=jnp.int32) == at_doc
    tile_counts = jnp.sum(jnp.where(picked[:, None], tiles_per_image, 0), axis=0)
    starts = jnp.sum(jnp.where(picked[:, None], image_start, 0), axis=0)
    owners = jnp.sum(jnp.where(picked[:, None], tile_owner, 0), axis=0)
    first_core = jnp.any(owned & picked[:, None, None], axis=0)[:, 0]
    tile_low, tile_high, tile_valid = tile_spans(tile_counts, starts, length, most_tiles)
    tile_low = jnp.where(tile_valid, tile_low, 2 * length)
    tile_high = jnp.where(tile_valid, tile_high, 0)

    chip_first = jnp.sum(
        jnp.where(jnp.arange(first_core.shape[0]) == at_y * 4 + at_x, first_core.astype(jnp.int32), 0)
    )
    source = 1 - chip_first
    gain_row = k_gain.reshape(1, head_dim)
    chip_of = owners // 2
    turn = jnp.where((owners % 2 == 1) & first_core[chip_of], 1, 0)

    def project(from_core):
        use_own = (at_core == from_core).astype(jnp.int32)
        meta = jnp.stack([at_core, use_own, at_y, at_x]).astype(jnp.int32)
        return project_kv(tile_rows, other_rows, tails, chains, gain_row, meta)

    pieces, chains, texts = lax.optimization_barrier((project(source), chains, texts))

    def send(sent):
        return lax.all_to_all(sent, PLANE, 0, 0, tiled=True)

    def pick(got):
        return jnp.stack([got[chip_of[j]] for j in range(most_tiles)])

    def ask():
        meta = jnp.stack([at_core, at_core, at_y, at_x]).astype(jnp.int32)
        query = project_query(texts, chains, q_gain.reshape(1, head_dim), meta)
        return jnp.stack([query[0]] + [lax.ppermute(query[k], "z", ring(-k)) for k in (1, 2, 3)])

    def spread_one():
        got, mine = lax.optimization_barrier((send(pieces), ask()))
        return pick(got), mine

    def spread_two():
        got, second = lax.optimization_barrier((send(pieces), project(1)))
        later, mine = lax.optimization_barrier((send(second), ask()))
        return jnp.where((turn > 0)[:, None, None], pick(later), pick(got)), mine

    chosen, mine = lax.cond(crowded, spread_two, spread_one)

    before, after = lax.ppermute(chosen, "y", ring(1)), lax.ppermute(chosen, "y", ring(-1))
    half = most_tiles // 2
    opposite = [lax.ppermute(before[:half], "y", ring(1)), lax.ppermute(after[half:], "y", ring(-1))]
    parts = [chosen, before, after, *opposite]
    parts += [lax.ppermute(part, "c", [(0, 1), (1, 0)]) for part in parts]
    query = [mine[(at_x + s - at_doc) % 4] for s in range(4)]
    query = [query[0]] + [lax.ppermute(query[s], "x", ring(s)) for s in (1, 2, 3)]
    last_slot = jnp.array([1, 3, 2, 0], jnp.int32)[at_y]
    last_part = jnp.where(at_core == 1, last_slot, last_slot + 4)
    pad = 2 * HALF - tile_len
    pad_row = (last_part + 1) * ROWS - pad

    token_x = (at_x - jnp.arange(4, dtype=jnp.int32)) % 4
    blocks = ((at_y * 4 + token_x) * 2 + at_core) * row_count
    spans = jnp.concatenate([tile_low, tile_high])
    context = attend(jnp.stack(query), parts, jnp.concatenate([spans, blocks, pad_row[None]]), pad)
    context = [context[0]] + [lax.ppermute(context[k], "x", ring(-k)) for k in (1, 2, 3)]
    context = jnp.stack(context)
    return jnp.concatenate([context[(h - at_x) % 4] for h in range(heads_kv)], axis=1)


def solution(mesh):
    grid = Mesh(mesh.devices.reshape(4, 4, 4, 2), ("z", "y", "x", "c"))
    rows = ("z", "y", "x", "c")
    return jax.shard_map(
        local,
        mesh=grid,
        in_specs=(
            P(rows, None),
            P(),
            P(SEQ, None),
            P(SEQ, None),
            P(SEQ, None),
            P(),
            P(),
            P(rows, None, None),
            P(),
            P(),
            P(),
        ),
        out_specs=P(rows, None),
        check_vma=False,
    )
```

```python
import functools

import jax
import jax.numpy as jnp
from jax import lax
from jax.experimental import pallas as pl
from jax.experimental.pallas import tpu as pltpu
from jax.sharding import Mesh
from jax.sharding import PartitionSpec as P

SEQ = ("y", "x", "c")
PLANE = ("y", "x")
PARTS = 8
ROWS = 208
HALF = 4 * ROWS
NONE = -1e30
MASKED = -2e30
LOG2E = 1.4426950408889634


def tile_spans(tile_counts, starts, length, most_tiles):
    slots = tile_counts.shape[0]
    span_ends = jnp.concatenate([starts[1:], jnp.full((1,), length, jnp.int32)])
    offsets = jnp.cumsum(tile_counts) - tile_counts
    tile_total = jnp.sum(tile_counts)
    tile_ids = jnp.arange(most_tiles, dtype=jnp.int32)
    image_of = jnp.sum((offsets[None, :] <= tile_ids[:, None]).astype(jnp.int32), axis=1) - 1
    member = jnp.arange(slots, dtype=jnp.int32)[None, :] == image_of[:, None]
    tile_low = jnp.sum(jnp.where(member, starts[None, :], 0), axis=1)
    tile_high = jnp.sum(jnp.where(member, span_ends[None, :], 0), axis=1)
    return (tile_low, tile_high, tile_ids < tile_total)


def ring(step):
    return [(i, (i + step) % 4) for i in range(4)]


def norm_rows(values, gain):
    return values * lax.rsqrt(jnp.mean(values * values, axis=-1, keepdims=True) + 1e-05) * gain


AWAY = (0, -1, 1, 2)
CHAIN = 8


def away(at, slot):
    return (at + AWAY[slot] + 4) % 4


def slot_of(at, place):
    ahead = (place - at + 4) % 4
    return jnp.where(ahead == 0, 0, jnp.where(ahead == 3, 1, ahead + 1))


def kv_kernel(tile_len, meta_ref, own_ref, other_ref, own_tail, other_tail, *refs):
    mine, swapped = refs[:CHAIN], refs[CHAIN : 2 * CHAIN]
    (gain_ref, out_ref, tile_buf, first_buf, second_buf, acc_ref, tile_sem, tail_sem, first_sem, second_sem) = refs[
        2 * CHAIN :
    ]
    core, own, y_at, x_at = (meta_ref[i] for i in range(4))
    whole = tile_len // 16 * 16 - HALF
    split, rest = first_buf.shape[2], second_buf.shape[2]

    def first_copy(chain, i):
        return pltpu.make_async_copy(chain[i], first_buf.at[pl.ds(2 * i, 2)], first_sem.at[i])

    def second_copy(chain, i):
        return pltpu.make_async_copy(
            chain[i].at[:, :, pl.ds(0, rest)], second_buf.at[pl.ds(2 * i, 2)], second_sem.at[i]
        )

    def tile_copies(i, source, tail, lower):
        at = pl.ds(pl.multiple_of(away(y_at, i) * 1024, 1024), 1024)
        to = pl.ds(i * 1024, 1024)
        if not lower:
            rows = pl.ds(0, HALF)
            return [pltpu.make_async_copy(source.at[rows, at], tile_buf.at[rows, to], tile_sem.at[i])]
        return [
            pltpu.make_async_copy(
                source.at[pl.ds(HALF, whole), at], tile_buf.at[pl.ds(0, whole), to], tile_sem.at[i]
            ),
            pltpu.make_async_copy(tail.at[:, at], tile_buf.at[pl.ds(whole, 16), to], tail_sem.at[i]),
        ]

    def start_tile(i):
        for from_own, source, tail in ((1, own_ref, own_tail), (0, other_ref, other_tail)):
            for lower in (0, 1):

                @pl.when((own == from_own) & (core == lower))
                def _(source=source, tail=tail, lower=lower):
                    for copy in tile_copies(i, source, tail, lower):
                        copy.start()

    for lower, first, second in ((0, mine, swapped), (1, swapped, mine)):

        @pl.when(core == lower)
        def _(first=first, second=second):
            for i in range(2):
                first_copy(first, i).start()
            for i in range(CHAIN):
                second_copy(second, i).start()

    start_tile(0)
    for lower, first in ((0, mine), (1, swapped)):

        @pl.when(core == lower)
        def _(first=first):
            for i in range(2, CHAIN):
                first_copy(first, i).start()

    for i in range(1, 4):
        start_tile(i)

    for i in range(4):
        first_copy(mine, 2 * i).wait()
        first_copy(mine, 2 * i + 1).wait()
        if i == 0:
            for j in range(CHAIN):
                second_copy(mine, j).wait()
        for lower in (0, 1):

            @pl.when(core == lower)
            def _(i=i, lower=lower):
                for copy in tile_copies(i, own_ref, own_tail, lower):
                    copy.wait()

        slots = [slot_of(x_at, x) for x in range(4)]
        tile = tile_buf[:, i * 1024 : (i + 1) * 1024]
        one = jnp.concatenate([first_buf[4 * i + slot] for slot in slots], axis=0)
        two = jnp.concatenate([second_buf[4 * slot + i] for slot in slots], axis=0)
        part_one = jnp.dot(tile, one, preferred_element_type=jnp.float32)
        part_two = jnp.dot(tile, two, preferred_element_type=jnp.float32)
        if i == 0:
            acc_ref[:, :split] = part_one
            acc_ref[:, split:] = part_two
        else:
            acc_ref[:, :split] += part_one
            acc_ref[:, split:] += part_two

    for y in range(4):
        held = tile_len - core * HALF - y * ROWS
        kept = lax.broadcasted_iota(jnp.int32, (ROWS, 128), 0) < held
        for h in range(4):
            at = slice(y * ROWS, (y + 1) * ROWS)
            keys = acc_ref[at, h * 128 : (h + 1) * 128]
            values = acc_ref[at, (h + 4) * 128 : (h + 5) * 128]
            if y == 3:
                keys, values = jnp.where(kept, keys, 0.0), jnp.where(kept, values, 0.0)
            out_ref[y * 4 + h, :, :128] = norm_rows(keys, gain_ref[...]).astype(jnp.bfloat16)
            out_ref[y * 4 + h, :, 128:] = values.astype(jnp.bfloat16)


def ragged_end(tile):
    whole = tile.shape[0] // 16 * 16
    return jnp.pad(tile[whole:], ((0, 16 - tile.shape[0] + whole), (0, 0)))


def project_kv(own, other, tails, chains, k_gain, meta):
    tile_len, depth = own.shape
    width, split = 1024, chains[0].shape[2]
    return pl.pallas_call(
        functools.partial(kv_kernel, tile_len),
        in_specs=[pl.BlockSpec(memory_space=pltpu.SMEM)]
        + [pl.BlockSpec(memory_space=pl.ANY)] * (4 + 2 * CHAIN)
        + [pl.BlockSpec(memory_space=pltpu.VMEM)],
        out_specs=pl.BlockSpec(memory_space=pltpu.VMEM),
        out_shape=jax.ShapeDtypeStruct((16, ROWS, 256), jnp.bfloat16),
        scratch_shapes=[
            pltpu.VMEM((HALF, depth), jnp.bfloat16),
            pltpu.VMEM((16, 256, split), jnp.bfloat16),
            pltpu.VMEM((16, 256, width - split), jnp.bfloat16),
            pltpu.VMEM((HALF, width), jnp.float32),
        ]
        + [pltpu.SemaphoreType.DMA((4,))] * 2
        + [pltpu.SemaphoreType.DMA((CHAIN,))] * 2,
        compiler_params=pltpu.CompilerParams(vmem_limit_bytes=52 * 2**20),
        cost_estimate=pl.CostEstimate(
            flops=2 * HALF * depth * width, bytes_accessed=2 * (HALF + width) * depth, transcendentals=0
        ),
        name="kv_projection",
    )(meta, own, other, *tails, *chains, k_gain)


def attend_kernel(pad, meta_ref, q_ref, *refs):
    part_refs, (out_ref, m_ref, l_ref, acc_ref) = refs[:-4], refs[-4:]
    tile = pl.program_id(0)
    blocks, rows, width = q_ref.shape
    heads = width // 128
    keys = PARTS * ROWS
    factor = LOG2E / 128**0.5
    pairs = heads // 2

    @pl.when(tile == 0)
    def _():
        m_ref[...] = jnp.full_like(m_ref, NONE)
        l_ref[...] = jnp.zeros_like(l_ref)
        acc_ref[...] = jnp.zeros_like(acc_ref)

    low, high = meta_ref[tile], meta_ref[4 + tile]
    some = False
    for b in range(blocks):
        first = meta_ref[8 + b]
        some = some | ((low < first + rows) & (high > first))

    @pl.when(some)
    def _():
        held = []
        for own, before, after, low_tiles, high_tiles in (part_refs[:5], part_refs[5:]):
            held += [own[0], before[0], after[0], jnp.where(tile < 2, low_tiles[0], high_tiles[0])]
        kv = jnp.concatenate(held, axis=0)
        row = lax.broadcasted_iota(jnp.int32, (keys, 128), 0)
        lane = lax.broadcasted_iota(jnp.int32, (keys, 128), 1)
        padding = (row >= meta_ref[8 + blocks]) & (row < meta_ref[8 + blocks] + pad)
        key_mask = jnp.where((lane == 0) & padding, MASKED, jnp.where(lane == 1, 1.0, 0.0))
        key = jnp.concatenate([kv[:, :128], key_mask.astype(jnp.bfloat16)], axis=1)
        value = jnp.concatenate([kv[:, 128:], jnp.ones((keys, 128), jnp.bfloat16)], axis=1)
        text_row = lax.broadcasted_iota(jnp.int32, (rows, 128), 0)
        text_lane = lax.broadcasted_iota(jnp.int32, (rows, 128), 1)

        def score(group):
            b, h = group // pairs, group % pairs * 2
            at = meta_ref[8 + b] + text_row
            outside = (at < low) | (at >= high)
            mask = jnp.where((text_lane == 1) & outside, MASKED, jnp.where(text_lane == 0, 1.0, 0.0))
            mask = mask.astype(jnp.bfloat16)
            both = [
                jnp.concatenate([q_ref[b, :, i * 128 : (i + 1) * 128], mask], axis=1) for i in (h, h + 1)
            ]
            return lax.dot_general(
                jnp.concatenate(both, axis=0), key, (((1,), (1,)), ((), ())), preferred_element_type=jnp.float32
            )

        def soften(group, scores):
            m_old = m_ref[group]
            m_new = jnp.maximum(m_old, jnp.max(scores, axis=1, keepdims=True))
            probs = jnp.exp2((scores - m_new) * factor)
            alpha = jnp.exp2((m_old - m_new) * factor)
            m_ref[group] = m_new
            summed = jnp.dot(probs.astype(jnp.bfloat16), value, preferred_element_type=jnp.float32)
            l_ref[group] = l_ref[group] * alpha + summed[:, 128:129]
            acc_ref[group] = acc_ref[group] * alpha + summed[:, :128]

        scores = score(0)
        for group in range(blocks * pairs):
            ahead = score(group + 1) if group + 1 < blocks * pairs else None
            soften(group, scores)
            scores = ahead

    @pl.when(tile == pl.num_programs(0) - 1)
    def _():
        for b in range(blocks):
            for h in range(heads):
                group, at = b * pairs + h // 2, slice(h % 2 * rows, (h % 2 + 1) * rows)
                out_ref[b, :, h * 128 : (h + 1) * 128] = (
                    acc_ref[group, at] / jnp.maximum(l_ref[group, at], 1.0)
                ).astype(jnp.bfloat16)


def attend(query, parts, meta, pad):
    blocks, rows, width = query.shape
    tiles = parts[0].shape[0]
    groups = blocks * width // 256
    return pl.pallas_call(
        functools.partial(attend_kernel, pad),
        grid_spec=pltpu.PrefetchScalarGridSpec(
            num_scalar_prefetch=1,
            grid=(tiles,),
            in_specs=[
                pl.BlockSpec((blocks, rows, width), lambda j, meta: (0, 0, 0)),
            ]
            + (
                [pl.BlockSpec((1, ROWS, 256), lambda j, meta: (j, 0, 0))] * 3
                + [pl.BlockSpec((1, ROWS, 256), lambda j, meta: (jnp.minimum(j, 1), 0, 0))]
                + [pl.BlockSpec((1, ROWS, 256), lambda j, meta: (jnp.maximum(j - 2, 0), 0, 0))]
            )
            * 2,
            out_specs=pl.BlockSpec((blocks, rows, width), lambda j, meta: (0, 0, 0)),
            scratch_shapes=[
                pltpu.VMEM((groups, 2 * rows, 1), jnp.float32),
                pltpu.VMEM((groups, 2 * rows, 1), jnp.float32),
                pltpu.VMEM((groups, 2 * rows, 128), jnp.float32),
            ],
        ),
        out_shape=jax.ShapeDtypeStruct(query.shape, jnp.bfloat16),
        compiler_params=pltpu.CompilerParams(vmem_limit_bytes=48 * 2**20),
        cost_estimate=pl.CostEstimate(
            flops=8 * blocks * rows * width * tiles * PARTS * ROWS,
            bytes_accessed=512 * tiles * PARTS * ROWS,
            transcendentals=blocks * rows * width // 128 * tiles * PARTS * ROWS,
        ),
        name="attention",
    )(meta, query, *parts)


def query_kernel(meta_ref, *refs):
    text_refs, refs = refs[:5], refs[5:]
    mine, swapped = refs[:CHAIN], refs[CHAIN : 2 * CHAIN]
    gain_ref, out_ref, weight_buf, acc_ref, sems = refs[2 * CHAIN :]
    core, y_at, x_at = meta_ref[0], meta_ref[2], meta_ref[3]
    width = weight_buf.shape[2]
    skip = mine[0].shape[2] - width

    def weight_copy(chain, i):
        return pltpu.make_async_copy(
            chain[i].at[:, :, pl.ds(skip, width)], weight_buf.at[pl.ds(2 * i, 2)], sems.at[i]
        )

    for lower, second in ((0, swapped), (1, mine)):

        @pl.when(core == lower)
        def _(second=second):
            for i in range(CHAIN):
                weight_copy(second, i).start()

    for j in range(4):
        weight_copy(mine, 2 * j).wait()
        weight_copy(mine, 2 * j + 1).wait()
        columns = []
        for i in range(4):
            chip = away(y_at, i) * 4 + away(x_at, j)
            at = pl.ds(pl.multiple_of(chip * 256, 256), 256)
            columns.append(jnp.concatenate([ref[:, at] for ref in text_refs], axis=0))
        part = jnp.dot(
            jnp.concatenate(columns, axis=1),
            weight_buf[4 * j : 4 * j + 4].reshape(1024, width),
            preferred_element_type=jnp.float32,
        )
        if j == 0:
            acc_ref[...] = part
        else:
            acc_ref[...] += part

    for b in range(4):
        for h in range(width // 128):
            block = acc_ref[b * 128 : (b + 1) * 128, h * 128 : (h + 1) * 128]
            out_ref[b, :, h * 128 : (h + 1) * 128] = norm_rows(block, gain_ref[...]).astype(jnp.bfloat16)


def project_query(texts, chains, gain, meta):
    rows, depth = texts[0].shape
    width = 512
    return pl.pallas_call(
        query_kernel,
        in_specs=[pl.BlockSpec(memory_space=pltpu.SMEM)]
        + [pl.BlockSpec(memory_space=pltpu.VMEM)] * 5
        + [pl.BlockSpec(memory_space=pl.ANY)] * (2 * CHAIN)
        + [pl.BlockSpec(memory_space=pltpu.VMEM)],
        out_specs=pl.BlockSpec(memory_space=pltpu.VMEM),
        out_shape=jax.ShapeDtypeStruct((4, rows, width), jnp.bfloat16),
        scratch_shapes=[
            pltpu.VMEM((16, 256, width), jnp.bfloat16),
            pltpu.VMEM((4 * rows, width), jnp.float32),
            pltpu.SemaphoreType.DMA((CHAIN,)),
        ],
        compiler_params=pltpu.CompilerParams(vmem_limit_bytes=32 * 2**20),
        cost_estimate=pl.CostEstimate(
            flops=8 * rows * depth * width, bytes_accessed=2 * (4 * rows + width) * depth, transcendentals=0
        ),
        name="query_projection",
    )(meta, *texts, *chains, gain)


def gather(k_weight, v_weight, q_share, tile_rows, normed, core):
    cut = v_weight.shape[1] // 2
    halves = (
        jnp.concatenate([k_weight, v_weight[:, :cut]], axis=1),
        jnp.concatenate([v_weight[:, cut:], q_share], axis=1),
    )
    swap = [(0, 1), (1, 0)]
    kept = jnp.where(core == 0, halves[0], halves[1])
    got = lax.ppermute(jnp.where(core == 0, halves[1], halves[0]), "c", swap)
    got, tile_rows = lax.optimization_barrier((got, tile_rows))
    other_rows = lax.ppermute(tile_rows, "c", swap)
    chip = jnp.where(core == 0, jnp.concatenate([kept, got]), jnp.concatenate([got, kept]))

    def move(piece, step, turn):
        pairs = []
        for y in range(4):
            for x in range(4):
                for c in range(2):
                    to = (y, (x + step) % 4) if (c == 0) == (turn == 0) else ((y + step) % 4, x)
                    pairs.append(((y * 4 + x) * 2 + c, (to[0] * 4 + to[1]) * 2 + c))
        return lax.ppermute(piece, SEQ, pairs)

    texts = [normed, lax.ppermute(normed, "z", ring(1)), lax.ppermute(normed, "z", ring(-1))]
    near = jnp.stack([chip, move(chip, 1, 0)])
    far = jnp.stack([move(chip, -1, 0), move(chip, 2, 0)])
    near, far = lax.optimization_barrier((near, far))
    before = [move(near, 1, 1), move(far, 1, 1)]
    after = [move(near, -1, 1), move(far, -1, 1)]
    before, after, texts = lax.optimization_barrier((before, after, texts))
    opposite = [move(before[0], 1, 1), move(after[1], -1, 1)]
    chain = [near, far, *before, *after, *opposite]
    chain += [lax.ppermute(piece, "c", swap) for piece in chain]
    return chain, other_rows, texts


def local(
    text,
    norm_gain,
    q_weight,
    k_weight,
    v_weight,
    q_gain,
    k_gain,
    vision,
    tiles_per_image,
    image_start,
    tile_owner,
):
    row_count = text.shape[0]
    head_dim = q_gain.shape[0]
    heads_kv = k_weight.shape[1] // head_dim
    tile_rows = vision[0]
    tile_len = tile_rows.shape[0]
    most_tiles = tile_owner.shape[1]
    length = row_count * lax.axis_size(SEQ)
    at_doc, at_y, at_x, at_core = (lax.axis_index(a) for a in ("z", "y", "x", "c"))

    group_width = q_weight.shape[1] // heads_kv
    q_share = lax.dynamic_slice_in_dim(q_weight, at_doc * group_width, group_width, 1)
    text_wide = text.astype(jnp.float32)
    normed = norm_rows(text_wide, norm_gain).astype(jnp.bfloat16)
    chains, other_rows, texts = gather(k_weight, v_weight, q_share, tile_rows, normed, at_core)
    tails = (ragged_end(tile_rows), ragged_end(other_rows))
    chains, other_rows, tails = lax.optimization_barrier((chains, other_rows, tails))

    totals = jnp.sum(tiles_per_image, axis=1)
    valid = jnp.arange(most_tiles, dtype=jnp.int32)[None, :] < totals[:, None]
    owned = jnp.any(
        (tile_owner[:, :, None] == jnp.arange(lax.axis_size(SEQ), dtype=jnp.int32)) & valid[:, :, None], axis=1
    )
    owned = owned.reshape(owned.shape[0], -1, 2)
    crowded = jnp.any(owned[:, :, 0] & owned[:, :, 1])
    picked = jnp.arange(tiles_per_image.shape[0], dtype=jnp.int32) == at_doc
    tile_counts = jnp.sum(jnp.where(picked[:, None], tiles_per_image, 0), axis=0)
    starts = jnp.sum(jnp.where(picked[:, None], image_start, 0), axis=0)
    owners = jnp.sum(jnp.where(picked[:, None], tile_owner, 0), axis=0)
    first_core = jnp.any(owned & picked[:, None, None], axis=0)[:, 0]
    tile_low, tile_high, tile_valid = tile_spans(tile_counts, starts, length, most_tiles)
    tile_low = jnp.where(tile_valid, tile_low, 2 * length)
    tile_high = jnp.where(tile_valid, tile_high, 0)

    chip_first = jnp.sum(
        jnp.where(jnp.arange(first_core.shape[0]) == at_y * 4 + at_x, first_core.astype(jnp.int32), 0)
    )
    source = 1 - chip_first
    gain_row = k_gain.reshape(1, head_dim)
    chip_of = owners // 2
    turn = jnp.where((owners % 2 == 1) & first_core[chip_of], 1, 0)

    def project(from_core):
        use_own = (at_core == from_core).astype(jnp.int32)
        meta = jnp.stack([at_core, use_own, at_y, at_x]).astype(jnp.int32)
        return project_kv(tile_rows, other_rows, tails, chains, gain_row, meta)

    pieces, chains, texts = lax.optimization_barrier((project(source), chains, texts))

    def send(sent):
        return lax.all_to_all(sent, PLANE, 0, 0, tiled=True)

    def pick(got):
        return jnp.stack([got[chip_of[j]] for j in range(most_tiles)])

    def ask():
        meta = jnp.stack([at_core, at_core, at_y, at_x]).astype(jnp.int32)
        own, below, above = texts
        half = row_count // 2
        opposite = [lax.ppermute(below[:half], "z", ring(1)), lax.ppermute(above[half:], "z", ring(-1))]
        query = project_query([own, below, *opposite, above], chains, q_gain.reshape(1, head_dim), meta)
        return jnp.stack([query[0]] + [lax.ppermute(query[k], "z", ring(-k)) for k in (1, 2, 3)])

    def spread_one():
        got, mine = lax.optimization_barrier((send(pieces), ask()))
        return pick(got), mine

    def spread_two():
        got, second = lax.optimization_barrier((send(pieces), project(1)))
        later, mine = lax.optimization_barrier((send(second), ask()))
        return jnp.where((turn > 0)[:, None, None], pick(later), pick(got)), mine

    chosen, mine = lax.cond(crowded, spread_two, spread_one)

    before, after = lax.ppermute(chosen, "y", ring(1)), lax.ppermute(chosen, "y", ring(-1))
    half = most_tiles // 2
    opposite = [lax.ppermute(before[:half], "y", ring(1)), lax.ppermute(after[half:], "y", ring(-1))]
    parts = [chosen, before, after, *opposite]
    parts += [lax.ppermute(part, "c", [(0, 1), (1, 0)]) for part in parts]
    query = [mine[(at_x + s - at_doc) % 4] for s in range(4)]
    query = [query[0]] + [lax.ppermute(query[s], "x", ring(s)) for s in (1, 2, 3)]
    last_slot = jnp.array([1, 3, 2, 0], jnp.int32)[at_y]
    last_part = jnp.where(at_core == 1, last_slot, last_slot + 4)
    pad = 2 * HALF - tile_len
    pad_row = (last_part + 1) * ROWS - pad

    token_x = (at_x - jnp.arange(4, dtype=jnp.int32)) % 4
    blocks = ((at_y * 4 + token_x) * 2 + at_core) * row_count
    spans = jnp.concatenate([tile_low, tile_high])
    context = attend(jnp.stack(query), parts, jnp.concatenate([spans, blocks, pad_row[None]]), pad)
    context = [context[0]] + [lax.ppermute(context[k], "x", ring(-k)) for k in (1, 2, 3)]
    context = jnp.stack(context)
    return jnp.concatenate([context[(h - at_x) % 4] for h in range(heads_kv)], axis=1)


def solution(mesh):
    grid = Mesh(mesh.devices.reshape(4, 4, 4, 2), ("z", "y", "x", "c"))
    rows = ("z", "y", "x", "c")
    return jax.shard_map(
        local,
        mesh=grid,
        in_specs=(
            P(rows, None),
            P(),
            P(SEQ, None),
            P(SEQ, None),
            P(SEQ, None),
            P(),
            P(),
            P(rows, None, None),
            P(),
            P(),
            P(),
        ),
        out_specs=P(rows, None),
        check_vma=False,
    )
```

```python
import functools

import jax
import jax.numpy as jnp
from jax import lax
from jax.experimental import pallas as pl
from jax.experimental.pallas import tpu as pltpu
from jax.sharding import Mesh
from jax.sharding import PartitionSpec as P

SEQ = ("y", "x", "c")
PLANE = ("y", "x")
PARTS = 8
ROWS = 208
HALF = 4 * ROWS
NONE = -1e30
MASKED = -2e30
LOG2E = 1.4426950408889634


def tile_spans(tile_counts, starts, length, most_tiles):
    slots = tile_counts.shape[0]
    span_ends = jnp.concatenate([starts[1:], jnp.full((1,), length, jnp.int32)])
    offsets = jnp.cumsum(tile_counts) - tile_counts
    tile_total = jnp.sum(tile_counts)
    tile_ids = jnp.arange(most_tiles, dtype=jnp.int32)
    image_of = jnp.sum((offsets[None, :] <= tile_ids[:, None]).astype(jnp.int32), axis=1) - 1
    member = jnp.arange(slots, dtype=jnp.int32)[None, :] == image_of[:, None]
    tile_low = jnp.sum(jnp.where(member, starts[None, :], 0), axis=1)
    tile_high = jnp.sum(jnp.where(member, span_ends[None, :], 0), axis=1)
    return (tile_low, tile_high, tile_ids < tile_total)


def ring(step):
    return [(i, (i + step) % 4) for i in range(4)]


def norm_rows(values, gain):
    return values * lax.rsqrt(jnp.mean(values * values, axis=-1, keepdims=True) + 1e-05) * gain


AWAY = (0, -1, 1, 2)
CHAIN = 8


def away(at, slot):
    step = AWAY[slot] if isinstance(slot, int) else 0
    return (at + step + 4) % 4


def slot_of(at, place):
    ahead = (place - at + 4) % 4
    return jnp.where(ahead == 0, 0, jnp.where(ahead == 3, 1, ahead + 1))


def kv_kernel(tile_len, meta_ref, own_ref, other_ref, own_tail, other_tail, *refs):
    mine, swapped = refs[:CHAIN], refs[CHAIN : 2 * CHAIN]
    (gain_ref, out_ref, tile_buf, first_buf, second_buf, acc_ref, tile_sem, tail_sem, first_sem, second_sem) = refs[
        2 * CHAIN :
    ]
    core, own, y_at, x_at = (meta_ref[i] for i in range(4))
    whole = tile_len // 16 * 16 - HALF
    split, rest = first_buf.shape[2], second_buf.shape[2]

    def first_copy(chain, i):
        source = chain[i] if isinstance(i, int) else chain[0]
        return pltpu.make_async_copy(source, first_buf.at[pl.ds(2 * i, 2)], first_sem.at[i])

    def second_copy(chain, i):
        return pltpu.make_async_copy(
            chain[i].at[:, :, pl.ds(0, rest)], second_buf.at[pl.ds(2 * i, 2)], second_sem.at[i]
        )

    def tile_copies(i, source, tail, lower):
        at = pl.ds(pl.multiple_of(away(y_at, i) * 1024, 1024), 1024)
        to = pl.ds(pl.multiple_of(i * 1024, 1024), 1024)
        if not lower:
            rows = pl.ds(0, HALF)
            return [pltpu.make_async_copy(source.at[rows, at], tile_buf.at[rows, to], tile_sem.at[i])]
        return [
            pltpu.make_async_copy(
                source.at[pl.ds(HALF, whole), at], tile_buf.at[pl.ds(0, whole), to], tile_sem.at[i]
            ),
            pltpu.make_async_copy(tail.at[:, at], tile_buf.at[pl.ds(whole, 16), to], tail_sem.at[i]),
        ]

    def start_tile(i):
        for from_own, source, tail in ((1, own_ref, own_tail), (0, other_ref, other_tail)):
            for lower in (0, 1):

                @pl.when((own == from_own) & (core == lower))
                def _(source=source, tail=tail, lower=lower):
                    for copy in tile_copies(i, source, tail, lower):
                        copy.start()

    for lower, first, second in ((0, mine, swapped), (1, swapped, mine)):

        @pl.when(core == lower)
        def _(first=first, second=second):
            for i in range(2):
                first_copy(first, i).start()
            for i in range(CHAIN):
                second_copy(second, i).start()

    start_tile(0)
    for lower, first in ((0, mine), (1, swapped)):

        @pl.when(core == lower)
        def _(first=first):
            for i in range(2, CHAIN):
                first_copy(first, i).start()

    for i in range(1, 4):
        start_tile(i)

    acc_ref[...] = jnp.zeros_like(acc_ref)
    for j in range(CHAIN):
        second_copy(mine, j).wait()
    slots = [slot_of(x_at, x) for x in range(4)]

    def add(i, carry):
        first_copy(mine, 2 * i).wait()
        first_copy(mine, 2 * i + 1).wait()
        for lower in (0, 1):

            @pl.when(core == lower)
            def _(lower=lower):
                for copy in tile_copies(i, own_ref, own_tail, lower):
                    copy.wait()

        tile = tile_buf[:, pl.ds(pl.multiple_of(i * 1024, 1024), 1024)]
        one = jnp.concatenate([first_buf[4 * i + slot] for slot in slots], axis=0)
        two = jnp.concatenate([second_buf[4 * slot + i] for slot in slots], axis=0)
        acc_ref[:, :split] += jnp.dot(tile, one, preferred_element_type=jnp.float32)
        acc_ref[:, split:] += jnp.dot(tile, two, preferred_element_type=jnp.float32)
        return carry

    lax.fori_loop(0, 4, add, 0)

    for y in range(4):
        held = tile_len - core * HALF - y * ROWS
        kept = lax.broadcasted_iota(jnp.int32, (ROWS, 128), 0) < held
        for h in range(4):
            at = slice(y * ROWS, (y + 1) * ROWS)
            keys = acc_ref[at, h * 128 : (h + 1) * 128]
            values = acc_ref[at, (h + 4) * 128 : (h + 5) * 128]
            if y == 3:
                keys, values = jnp.where(kept, keys, 0.0), jnp.where(kept, values, 0.0)
            out_ref[y * 4 + h, :, :128] = norm_rows(keys, gain_ref[...]).astype(jnp.bfloat16)
            out_ref[y * 4 + h, :, 128:] = values.astype(jnp.bfloat16)


def ragged_end(tile):
    whole = tile.shape[0] // 16 * 16
    return jnp.pad(tile[whole:], ((0, 16 - tile.shape[0] + whole), (0, 0)))


def project_kv(own, other, tails, chains, k_gain, meta):
    tile_len, depth = own.shape
    width, split = 1024, chains[0].shape[2]
    return pl.pallas_call(
        functools.partial(kv_kernel, tile_len),
        in_specs=[pl.BlockSpec(memory_space=pltpu.SMEM)]
        + [pl.BlockSpec(memory_space=pl.ANY)] * (4 + 2 * CHAIN)
        + [pl.BlockSpec(memory_space=pltpu.VMEM)],
        out_specs=pl.BlockSpec(memory_space=pltpu.VMEM),
        out_shape=jax.ShapeDtypeStruct((16, ROWS, 256), jnp.bfloat16),
        scratch_shapes=[
            pltpu.VMEM((HALF, depth), jnp.bfloat16),
            pltpu.VMEM((16, 256, split), jnp.bfloat16),
            pltpu.VMEM((16, 256, width - split), jnp.bfloat16),
            pltpu.VMEM((HALF, width), jnp.float32),
        ]
        + [pltpu.SemaphoreType.DMA((4,))] * 2
        + [pltpu.SemaphoreType.DMA((CHAIN,))] * 2,
        compiler_params=pltpu.CompilerParams(vmem_limit_bytes=52 * 2**20),
        cost_estimate=pl.CostEstimate(
            flops=2 * HALF * depth * width, bytes_accessed=2 * (HALF + width) * depth, transcendentals=0
        ),
        name="kv_projection",
    )(meta, own, other, *tails, *chains, k_gain)


def attend_kernel(pad, meta_ref, q_ref, *refs):
    part_refs, (out_ref, m_ref, l_ref, acc_ref) = refs[:-4], refs[-4:]
    tile = pl.program_id(0)
    blocks, rows, width = q_ref.shape
    heads = width // 128
    keys = PARTS * ROWS
    factor = LOG2E / 128**0.5
    pairs = heads // 2

    @pl.when(tile == 0)
    def _():
        m_ref[...] = jnp.full_like(m_ref, NONE)
        l_ref[...] = jnp.zeros_like(l_ref)
        acc_ref[...] = jnp.zeros_like(acc_ref)

    low, high = meta_ref[tile], meta_ref[4 + tile]
    some = False
    for b in range(blocks):
        first = meta_ref[8 + b]
        some = some | ((low < first + rows) & (high > first))

    @pl.when(some)
    def _():
        held = []
        for own, before, after, low_tiles, high_tiles in (part_refs[:5], part_refs[5:]):
            held += [own[0], before[0], after[0], jnp.where(tile < 2, low_tiles[0], high_tiles[0])]
        kv = jnp.concatenate(held, axis=0)
        row = lax.broadcasted_iota(jnp.int32, (keys, 128), 0)
        lane = lax.broadcasted_iota(jnp.int32, (keys, 128), 1)
        padding = (row >= meta_ref[8 + blocks]) & (row < meta_ref[8 + blocks] + pad)
        key_mask = jnp.where((lane == 0) & padding, MASKED, jnp.where(lane == 1, 1.0, 0.0))
        key = jnp.concatenate([kv[:, :128], key_mask.astype(jnp.bfloat16)], axis=1)
        value = jnp.concatenate([kv[:, 128:], jnp.ones((keys, 128), jnp.bfloat16)], axis=1)
        text_row = lax.broadcasted_iota(jnp.int32, (rows, 128), 0)
        text_lane = lax.broadcasted_iota(jnp.int32, (rows, 128), 1)

        def score(group):
            b, h = group // pairs, group % pairs * 2
            at = meta_ref[8 + b] + text_row
            outside = (at < low) | (at >= high)
            mask = jnp.where((text_lane == 1) & outside, MASKED, jnp.where(text_lane == 0, 1.0, 0.0))
            mask = mask.astype(jnp.bfloat16)
            both = [
                jnp.concatenate([q_ref[b, :, i * 128 : (i + 1) * 128], mask], axis=1) for i in (h, h + 1)
            ]
            return lax.dot_general(
                jnp.concatenate(both, axis=0), key, (((1,), (1,)), ((), ())), preferred_element_type=jnp.float32
            )

        def soften(group, scores):
            m_old = m_ref[group]
            m_new = jnp.maximum(m_old, jnp.max(scores, axis=1, keepdims=True))
            probs = jnp.exp2((scores - m_new) * factor)
            alpha = jnp.exp2((m_old - m_new) * factor)
            m_ref[group] = m_new
            summed = jnp.dot(probs.astype(jnp.bfloat16), value, preferred_element_type=jnp.float32)
            l_ref[group] = l_ref[group] * alpha + summed[:, 128:129]
            acc_ref[group] = acc_ref[group] * alpha + summed[:, :128]

        scores = score(0)
        for group in range(blocks * pairs):
            ahead = score(group + 1) if group + 1 < blocks * pairs else None
            soften(group, scores)
            scores = ahead

    @pl.when(tile == pl.num_programs(0) - 1)
    def _():
        for b in range(blocks):
            for h in range(heads):
                group, at = b * pairs + h // 2, slice(h % 2 * rows, (h % 2 + 1) * rows)
                out_ref[b, :, h * 128 : (h + 1) * 128] = (
                    acc_ref[group, at] / jnp.maximum(l_ref[group, at], 1.0)
                ).astype(jnp.bfloat16)


def attend(query, parts, meta, pad):
    blocks, rows, width = query.shape
    tiles = parts[0].shape[0]
    groups = blocks * width // 256
    return pl.pallas_call(
        functools.partial(attend_kernel, pad),
        grid_spec=pltpu.PrefetchScalarGridSpec(
            num_scalar_prefetch=1,
            grid=(tiles,),
            in_specs=[
                pl.BlockSpec((blocks, rows, width), lambda j, meta: (0, 0, 0)),
            ]
            + (
                [pl.BlockSpec((1, ROWS, 256), lambda j, meta: (j, 0, 0))] * 3
                + [pl.BlockSpec((1, ROWS, 256), lambda j, meta: (jnp.minimum(j, 1), 0, 0))]
                + [pl.BlockSpec((1, ROWS, 256), lambda j, meta: (jnp.maximum(j - 2, 0), 0, 0))]
            )
            * 2,
            out_specs=pl.BlockSpec((blocks, rows, width), lambda j, meta: (0, 0, 0)),
            scratch_shapes=[
                pltpu.VMEM((groups, 2 * rows, 1), jnp.float32),
                pltpu.VMEM((groups, 2 * rows, 1), jnp.float32),
                pltpu.VMEM((groups, 2 * rows, 128), jnp.float32),
            ],
        ),
        out_shape=jax.ShapeDtypeStruct(query.shape, jnp.bfloat16),
        compiler_params=pltpu.CompilerParams(vmem_limit_bytes=48 * 2**20),
        cost_estimate=pl.CostEstimate(
            flops=8 * blocks * rows * width * tiles * PARTS * ROWS,
            bytes_accessed=512 * tiles * PARTS * ROWS,
            transcendentals=blocks * rows * width // 128 * tiles * PARTS * ROWS,
        ),
        name="attention",
    )(meta, query, *parts)


def query_kernel(meta_ref, *refs):
    text_refs, refs = refs[:5], refs[5:]
    mine, swapped = refs[:CHAIN], refs[CHAIN : 2 * CHAIN]
    gain_ref, out_ref, weight_buf, acc_ref, sems = refs[2 * CHAIN :]
    core, y_at, x_at = meta_ref[0], meta_ref[2], meta_ref[3]
    width = weight_buf.shape[2]
    skip = mine[0].shape[2] - width

    def weight_copy(chain, i):
        return pltpu.make_async_copy(
            chain[i].at[:, :, pl.ds(skip, width)], weight_buf.at[pl.ds(2 * i, 2)], sems.at[i]
        )

    for lower, second in ((0, swapped), (1, mine)):

        @pl.when(core == lower)
        def _(second=second):
            for i in range(CHAIN):
                weight_copy(second, i).start()

    for j in range(4):
        weight_copy(mine, 2 * j).wait()
        weight_copy(mine, 2 * j + 1).wait()
        columns = []
        for i in range(4):
            chip = away(y_at, i) * 4 + away(x_at, j)
            at = pl.ds(pl.multiple_of(chip * 256, 256), 256)
            columns.append(jnp.concatenate([ref[:, at] for ref in text_refs], axis=0))
        part = jnp.dot(
            jnp.concatenate(columns, axis=1),
            weight_buf[4 * j : 4 * j + 4].reshape(1024, width),
            preferred_element_type=jnp.float32,
        )
        if j == 0:
            acc_ref[...] = part
        else:
            acc_ref[...] += part

    for b in range(4):
        for h in range(width // 128):
            block = acc_ref[b * 128 : (b + 1) * 128, h * 128 : (h + 1) * 128]
            out_ref[b, :, h * 128 : (h + 1) * 128] = norm_rows(block, gain_ref[...]).astype(jnp.bfloat16)


def project_query(texts, chains, gain, meta):
    rows, depth = texts[0].shape
    width = 512
    return pl.pallas_call(
        query_kernel,
        in_specs=[pl.BlockSpec(memory_space=pltpu.SMEM)]
        + [pl.BlockSpec(memory_space=pltpu.VMEM)] * 5
        + [pl.BlockSpec(memory_space=pl.ANY)] * (2 * CHAIN)
        + [pl.BlockSpec(memory_space=pltpu.VMEM)],
        out_specs=pl.BlockSpec(memory_space=pltpu.VMEM),
        out_shape=jax.ShapeDtypeStruct((4, rows, width), jnp.bfloat16),
        scratch_shapes=[
            pltpu.VMEM((16, 256, width), jnp.bfloat16),
            pltpu.VMEM((4 * rows, width), jnp.float32),
            pltpu.SemaphoreType.DMA((CHAIN,)),
        ],
        compiler_params=pltpu.CompilerParams(vmem_limit_bytes=32 * 2**20),
        cost_estimate=pl.CostEstimate(
            flops=8 * rows * depth * width, bytes_accessed=2 * (4 * rows + width) * depth, transcendentals=0
        ),
        name="query_projection",
    )(meta, *texts, *chains, gain)


def gather(k_weight, v_weight, q_share, tile_rows, normed, core):
    cut = v_weight.shape[1] // 2
    halves = (
        jnp.concatenate([k_weight, v_weight[:, :cut]], axis=1),
        jnp.concatenate([v_weight[:, cut:], q_share], axis=1),
    )
    swap = [(0, 1), (1, 0)]
    kept = jnp.where(core == 0, halves[0], halves[1])
    got = lax.ppermute(jnp.where(core == 0, halves[1], halves[0]), "c", swap)
    got, tile_rows = lax.optimization_barrier((got, tile_rows))
    other_rows = lax.ppermute(tile_rows, "c", swap)
    chip = jnp.where(core == 0, jnp.concatenate([kept, got]), jnp.concatenate([got, kept]))

    def move(piece, step, turn):
        pairs = []
        for y in range(4):
            for x in range(4):
                for c in range(2):
                    to = (y, (x + step) % 4) if (c == 0) == (turn == 0) else ((y + step) % 4, x)
                    pairs.append(((y * 4 + x) * 2 + c, (to[0] * 4 + to[1]) * 2 + c))
        return lax.ppermute(piece, SEQ, pairs)

    texts = [normed, lax.ppermute(normed, "z", ring(1)), lax.ppermute(normed, "z", ring(-1))]
    near = jnp.stack([chip, move(chip, 1, 0)])
    far = jnp.stack([move(chip, -1, 0), move(chip, 2, 0)])
    near, far = lax.optimization_barrier((near, far))
    before = [move(near, 1, 1), move(far, 1, 1)]
    after = [move(near, -1, 1), move(far, -1, 1)]
    before, after = lax.optimization_barrier((before, after))
    opposite = [move(before[0], 1, 1), move(after[1], -1, 1)]
    opposite, texts = lax.optimization_barrier((opposite, texts))
    own, below, above = texts
    half = own.shape[0] // 2
    texts = [own, below, lax.ppermute(below[:half], "z", ring(1)), lax.ppermute(above[half:], "z", ring(-1)), above]
    chain = [near, far, *before, *after, *opposite]
    chain += [lax.ppermute(piece, "c", swap) for piece in chain]
    return chain, other_rows, texts


def local(
    text,
    norm_gain,
    q_weight,
    k_weight,
    v_weight,
    q_gain,
    k_gain,
    vision,
    tiles_per_image,
    image_start,
    tile_owner,
):
    row_count = text.shape[0]
    head_dim = q_gain.shape[0]
    heads_kv = k_weight.shape[1] // head_dim
    tile_rows = vision[0]
    tile_len = tile_rows.shape[0]
    most_tiles = tile_owner.shape[1]
    length = row_count * lax.axis_size(SEQ)
    at_doc, at_y, at_x, at_core = (lax.axis_index(a) for a in ("z", "y", "x", "c"))

    group_width = q_weight.shape[1] // heads_kv
    q_share = lax.dynamic_slice_in_dim(q_weight, at_doc * group_width, group_width, 1)
    text_wide = text.astype(jnp.float32)
    normed = norm_rows(text_wide, norm_gain).astype(jnp.bfloat16)
    chains, other_rows, texts = gather(k_weight, v_weight, q_share, tile_rows, normed, at_core)
    tails = (ragged_end(tile_rows), ragged_end(other_rows))
    chains, other_rows, tails = lax.optimization_barrier((chains, other_rows, tails))

    totals = jnp.sum(tiles_per_image, axis=1)
    valid = jnp.arange(most_tiles, dtype=jnp.int32)[None, :] < totals[:, None]
    owned = jnp.any(
        (tile_owner[:, :, None] == jnp.arange(lax.axis_size(SEQ), dtype=jnp.int32)) & valid[:, :, None], axis=1
    )
    owned = owned.reshape(owned.shape[0], -1, 2)
    crowded = jnp.any(owned[:, :, 0] & owned[:, :, 1])
    picked = jnp.arange(tiles_per_image.shape[0], dtype=jnp.int32) == at_doc
    tile_counts = jnp.sum(jnp.where(picked[:, None], tiles_per_image, 0), axis=0)
    starts = jnp.sum(jnp.where(picked[:, None], image_start, 0), axis=0)
    owners = jnp.sum(jnp.where(picked[:, None], tile_owner, 0), axis=0)
    first_core = jnp.any(owned & picked[:, None, None], axis=0)[:, 0]
    tile_low, tile_high, tile_valid = tile_spans(tile_counts, starts, length, most_tiles)
    tile_low = jnp.where(tile_valid, tile_low, 2 * length)
    tile_high = jnp.where(tile_valid, tile_high, 0)

    chip_first = jnp.sum(
        jnp.where(jnp.arange(first_core.shape[0]) == at_y * 4 + at_x, first_core.astype(jnp.int32), 0)
    )
    source = 1 - chip_first
    gain_row = k_gain.reshape(1, head_dim)
    chip_of = owners // 2
    turn = jnp.where((owners % 2 == 1) & first_core[chip_of], 1, 0)

    def project(from_core):
        use_own = (at_core == from_core).astype(jnp.int32)
        meta = jnp.stack([at_core, use_own, at_y, at_x]).astype(jnp.int32)
        return project_kv(tile_rows, other_rows, tails, chains, gain_row, meta)

    pieces, chains, texts = lax.optimization_barrier((project(source), chains, texts))

    def send(sent):
        return lax.all_to_all(sent, PLANE, 0, 0, tiled=True)

    def pick(got):
        return jnp.stack([got[chip_of[j]] for j in range(most_tiles)])

    def ask():
        meta = jnp.stack([at_core, at_core, at_y, at_x]).astype(jnp.int32)
        query = project_query(texts, chains, q_gain.reshape(1, head_dim), meta)
        return jnp.stack([query[0]] + [lax.ppermute(query[k], "z", ring(-k)) for k in (1, 2, 3)])

    def spread_one():
        got, mine = lax.optimization_barrier((send(pieces), ask()))
        return pick(got), mine

    def spread_two():
        got, second = lax.optimization_barrier((send(pieces), project(1)))
        later, mine = lax.optimization_barrier((send(second), ask()))
        return jnp.where((turn > 0)[:, None, None], pick(later), pick(got)), mine

    chosen, mine = lax.cond(crowded, spread_two, spread_one)

    before, after = lax.ppermute(chosen, "y", ring(1)), lax.ppermute(chosen, "y", ring(-1))
    half = most_tiles // 2
    opposite = [lax.ppermute(before[:half], "y", ring(1)), lax.ppermute(after[half:], "y", ring(-1))]
    parts = [chosen, before, after, *opposite]
    parts += [lax.ppermute(part, "c", [(0, 1), (1, 0)]) for part in parts]
    query = [mine[(at_x + s - at_doc) % 4] for s in range(4)]
    query = [query[0]] + [lax.ppermute(query[s], "x", ring(s)) for s in (1, 2, 3)]
    last_slot = jnp.array([1, 3, 2, 0], jnp.int32)[at_y]
    last_part = jnp.where(at_core == 1, last_slot, last_slot + 4)
    pad = 2 * HALF - tile_len
    pad_row = (last_part + 1) * ROWS - pad

    token_x = (at_x - jnp.arange(4, dtype=jnp.int32)) % 4
    blocks = ((at_y * 4 + token_x) * 2 + at_core) * row_count
    spans = jnp.concatenate([tile_low, tile_high])
    context = attend(jnp.stack(query), parts, jnp.concatenate([spans, blocks, pad_row[None]]), pad)
    context = [context[0]] + [lax.ppermute(context[k], "x", ring(-k)) for k in (1, 2, 3)]
    context = jnp.stack(context)
    return jnp.concatenate([context[(h - at_x) % 4] for h in range(heads_kv)], axis=1)


def solution(mesh):
    grid = Mesh(mesh.devices.reshape(4, 4, 4, 2), ("z", "y", "x", "c"))
    rows = ("z", "y", "x", "c")
    return jax.shard_map(
        local,
        mesh=grid,
        in_specs=(
            P(rows, None),
            P(),
            P(SEQ, None),
            P(SEQ, None),
            P(SEQ, None),
            P(),
            P(),
            P(rows, None, None),
            P(),
            P(),
            P(),
        ),
        out_specs=P(rows, None),
        check_vma=False,
    )
```

```python
import functools

import jax
import jax.numpy as jnp
from jax import lax
from jax.experimental import pallas as pl
from jax.experimental.pallas import tpu as pltpu
from jax.sharding import Mesh
from jax.sharding import PartitionSpec as P

SEQ = ("y", "x", "c")
PLANE = ("y", "x")
PARTS = 8
ROWS = 208
HALF = 4 * ROWS
NONE = -1e30
MASKED = -2e30
LOG2E = 1.4426950408889634


def tile_spans(tile_counts, starts, length, most_tiles):
    slots = tile_counts.shape[0]
    span_ends = jnp.concatenate([starts[1:], jnp.full((1,), length, jnp.int32)])
    offsets = jnp.cumsum(tile_counts) - tile_counts
    tile_total = jnp.sum(tile_counts)
    tile_ids = jnp.arange(most_tiles, dtype=jnp.int32)
    image_of = jnp.sum((offsets[None, :] <= tile_ids[:, None]).astype(jnp.int32), axis=1) - 1
    member = jnp.arange(slots, dtype=jnp.int32)[None, :] == image_of[:, None]
    tile_low = jnp.sum(jnp.where(member, starts[None, :], 0), axis=1)
    tile_high = jnp.sum(jnp.where(member, span_ends[None, :], 0), axis=1)
    return (tile_low, tile_high, tile_ids < tile_total)


def ring(step):
    return [(i, (i + step) % 4) for i in range(4)]


def norm_rows(values, gain):
    return values * lax.rsqrt(jnp.mean(values * values, axis=-1, keepdims=True) + 1e-05) * gain


AWAY = (0, -1, 1, 2)
CHAIN = 8


def away(at, slot):
    step = AWAY[slot] if isinstance(slot, int) else 0
    return (at + step + 4) % 4


def slot_of(at, place):
    ahead = (place - at + 4) % 4
    return jnp.where(ahead == 0, 0, jnp.where(ahead == 3, 1, ahead + 1))


def kv_kernel(tile_len, meta_ref, own_ref, other_ref, own_tail, other_tail, *refs):
    mine, swapped = refs[:CHAIN], refs[CHAIN : 2 * CHAIN]
    (gain_ref, out_ref, tile_buf, first_buf, second_buf, acc_ref, tile_sem, tail_sem, first_sem, second_sem) = refs[
        2 * CHAIN :
    ]
    core, own, y_at, x_at = (meta_ref[i] for i in range(4))
    whole = tile_len // 16 * 16 - HALF
    split, rest = first_buf.shape[2], second_buf.shape[2]

    def first_copy(chain, i):
        source = chain[i] if isinstance(i, int) else chain[0]
        return pltpu.make_async_copy(source, first_buf.at[pl.ds(2 * i, 2)], first_sem.at[i])

    def second_copy(chain, i):
        return pltpu.make_async_copy(
            chain[i].at[:, :, pl.ds(0, rest)], second_buf.at[pl.ds(2 * i, 2)], second_sem.at[i]
        )

    def tile_copies(i, source, tail, lower):
        at = pl.ds(pl.multiple_of(away(y_at, i) * 1024, 1024), 1024)
        to = pl.ds(pl.multiple_of(i * 1024, 1024), 1024)
        if not lower:
            rows = pl.ds(0, HALF)
            return [pltpu.make_async_copy(source.at[rows, at], tile_buf.at[rows, to], tile_sem.at[i])]
        return [
            pltpu.make_async_copy(
                source.at[pl.ds(HALF, whole), at], tile_buf.at[pl.ds(0, whole), to], tile_sem.at[i]
            ),
            pltpu.make_async_copy(tail.at[:, at], tile_buf.at[pl.ds(whole, 16), to], tail_sem.at[i]),
        ]

    def start_tile(i):
        for from_own, source, tail in ((1, own_ref, own_tail), (0, other_ref, other_tail)):
            for lower in (0, 1):

                @pl.when((own == from_own) & (core == lower))
                def _(source=source, tail=tail, lower=lower):
                    for copy in tile_copies(i, source, tail, lower):
                        copy.start()

    for lower, first, second in ((0, mine, swapped), (1, swapped, mine)):

        @pl.when(core == lower)
        def _(first=first, second=second):
            for i in range(2):
                first_copy(first, i).start()
            for i in range(CHAIN):
                second_copy(second, i).start()

    start_tile(0)
    for lower, first in ((0, mine), (1, swapped)):

        @pl.when(core == lower)
        def _(first=first):
            for i in range(2, CHAIN):
                first_copy(first, i).start()

    for i in range(1, 4):
        start_tile(i)

    acc_ref[...] = jnp.zeros_like(acc_ref)
    for j in range(CHAIN):
        second_copy(mine, j).wait()
    slots = [slot_of(x_at, x) for x in range(4)]

    def add(i, carry):
        first_copy(mine, 2 * i).wait()
        first_copy(mine, 2 * i + 1).wait()
        for lower in (0, 1):

            @pl.when(core == lower)
            def _(lower=lower):
                for copy in tile_copies(i, own_ref, own_tail, lower):
                    copy.wait()

        tile = tile_buf[:, pl.ds(pl.multiple_of(i * 1024, 1024), 1024)]
        one = jnp.concatenate([first_buf[4 * i + slot] for slot in slots], axis=0)
        two = jnp.concatenate([second_buf[4 * slot + i] for slot in slots], axis=0)
        acc_ref[:, :split] += jnp.dot(tile, one, preferred_element_type=jnp.float32)
        acc_ref[:, split:] += jnp.dot(tile, two, preferred_element_type=jnp.float32)
        return carry

    lax.fori_loop(0, 4, add, 0)

    for y in range(4):
        held = tile_len - core * HALF - y * ROWS
        kept = lax.broadcasted_iota(jnp.int32, (ROWS, 128), 0) < held
        for h in range(4):
            at = slice(y * ROWS, (y + 1) * ROWS)
            keys = acc_ref[at, h * 128 : (h + 1) * 128]
            values = acc_ref[at, (h + 4) * 128 : (h + 5) * 128]
            if y == 3:
                keys, values = jnp.where(kept, keys, 0.0), jnp.where(kept, values, 0.0)
            out_ref[y * 4 + h, :, :128] = norm_rows(keys, gain_ref[...]).astype(jnp.bfloat16)
            out_ref[y * 4 + h, :, 128:] = values.astype(jnp.bfloat16)


def ragged_end(tile):
    whole = tile.shape[0] // 16 * 16
    return jnp.pad(tile[whole:], ((0, 16 - tile.shape[0] + whole), (0, 0)))


def project_kv(own, other, tails, chains, k_gain, meta):
    tile_len, depth = own.shape
    width, split = 1024, chains[0].shape[2]
    return pl.pallas_call(
        functools.partial(kv_kernel, tile_len),
        in_specs=[pl.BlockSpec(memory_space=pltpu.SMEM)]
        + [pl.BlockSpec(memory_space=pl.ANY)] * (4 + 2 * CHAIN)
        + [pl.BlockSpec(memory_space=pltpu.VMEM)],
        out_specs=pl.BlockSpec(memory_space=pltpu.VMEM),
        out_shape=jax.ShapeDtypeStruct((16, ROWS, 256), jnp.bfloat16),
        scratch_shapes=[
            pltpu.VMEM((HALF, depth), jnp.bfloat16),
            pltpu.VMEM((16, 256, split), jnp.bfloat16),
            pltpu.VMEM((16, 256, width - split), jnp.bfloat16),
            pltpu.VMEM((HALF, width), jnp.float32),
        ]
        + [pltpu.SemaphoreType.DMA((4,))] * 2
        + [pltpu.SemaphoreType.DMA((CHAIN,))] * 2,
        compiler_params=pltpu.CompilerParams(vmem_limit_bytes=52 * 2**20),
        cost_estimate=pl.CostEstimate(
            flops=2 * HALF * depth * width, bytes_accessed=2 * (HALF + width) * depth, transcendentals=0
        ),
        name="kv_projection",
    )(meta, own, other, *tails, *chains, k_gain)


def attend_kernel(pad, meta_ref, q_ref, *refs):
    part_refs, (out_ref, m_ref, l_ref, acc_ref) = refs[:-4], refs[-4:]
    tile = pl.program_id(0)
    blocks, rows, width = q_ref.shape
    heads = width // 128
    keys = PARTS * ROWS
    factor = LOG2E / 128**0.5
    pairs = heads // 2

    @pl.when(tile == 0)
    def _():
        m_ref[...] = jnp.full_like(m_ref, NONE)
        l_ref[...] = jnp.zeros_like(l_ref)
        acc_ref[...] = jnp.zeros_like(acc_ref)

    low, high = meta_ref[tile], meta_ref[4 + tile]
    some = False
    for b in range(blocks):
        first = meta_ref[8 + b]
        some = some | ((low < first + rows) & (high > first))

    @pl.when(some)
    def _():
        held = []
        for own, before, after, low_tiles, high_tiles in (part_refs[:5], part_refs[5:]):
            held += [own[0], before[0], after[0], jnp.where(tile < 2, low_tiles[0], high_tiles[0])]
        kv = jnp.concatenate(held, axis=0)
        row = lax.broadcasted_iota(jnp.int32, (keys, 128), 0)
        lane = lax.broadcasted_iota(jnp.int32, (keys, 128), 1)
        padding = (row >= meta_ref[8 + blocks]) & (row < meta_ref[8 + blocks] + pad)
        key_mask = jnp.where((lane == 0) & padding, MASKED, jnp.where(lane == 1, 1.0, 0.0))
        key = jnp.concatenate([kv[:, :128], key_mask.astype(jnp.bfloat16)], axis=1)
        value = jnp.concatenate([kv[:, 128:], jnp.ones((keys, 128), jnp.bfloat16)], axis=1)
        text_row = lax.broadcasted_iota(jnp.int32, (rows, 128), 0)
        text_lane = lax.broadcasted_iota(jnp.int32, (rows, 128), 1)

        def score(group):
            b, h = group // pairs, group % pairs * 2
            at = meta_ref[8 + b] + text_row
            outside = (at < low) | (at >= high)
            mask = jnp.where((text_lane == 1) & outside, MASKED, jnp.where(text_lane == 0, 1.0, 0.0))
            mask = mask.astype(jnp.bfloat16)
            both = [
                jnp.concatenate([q_ref[b, :, i * 128 : (i + 1) * 128], mask], axis=1) for i in (h, h + 1)
            ]
            return lax.dot_general(
                jnp.concatenate(both, axis=0), key, (((1,), (1,)), ((), ())), preferred_element_type=jnp.float32
            )

        def soften(group, scores):
            m_old = m_ref[group]
            m_new = jnp.maximum(m_old, jnp.max(scores, axis=1, keepdims=True))
            probs = jnp.exp2((scores - m_new) * factor)
            alpha = jnp.exp2((m_old - m_new) * factor)
            m_ref[group] = m_new
            summed = jnp.dot(probs.astype(jnp.bfloat16), value, preferred_element_type=jnp.float32)
            l_ref[group] = l_ref[group] * alpha + summed[:, 128:129]
            acc_ref[group] = acc_ref[group] * alpha + summed[:, :128]

        scores = score(0)
        for group in range(blocks * pairs):
            ahead = score(group + 1) if group + 1 < blocks * pairs else None
            soften(group, scores)
            scores = ahead

    @pl.when(tile == pl.num_programs(0) - 1)
    def _():
        for b in range(blocks):
            for h in range(heads):
                group, at = b * pairs + h // 2, slice(h % 2 * rows, (h % 2 + 1) * rows)
                out_ref[b, :, h * 128 : (h + 1) * 128] = (
                    acc_ref[group, at] / jnp.maximum(l_ref[group, at], 1.0)
                ).astype(jnp.bfloat16)


def attend(query, parts, meta, pad):
    blocks, rows, width = query.shape
    tiles = parts[0].shape[0]
    groups = blocks * width // 256
    return pl.pallas_call(
        functools.partial(attend_kernel, pad),
        grid_spec=pltpu.PrefetchScalarGridSpec(
            num_scalar_prefetch=1,
            grid=(tiles,),
            in_specs=[
                pl.BlockSpec((blocks, rows, width), lambda j, meta: (0, 0, 0)),
            ]
            + (
                [pl.BlockSpec((1, ROWS, 256), lambda j, meta: (j, 0, 0))] * 3
                + [pl.BlockSpec((1, ROWS, 256), lambda j, meta: (jnp.minimum(j, 1), 0, 0))]
                + [pl.BlockSpec((1, ROWS, 256), lambda j, meta: (jnp.maximum(j - 2, 0), 0, 0))]
            )
            * 2,
            out_specs=pl.BlockSpec((blocks, rows, width), lambda j, meta: (0, 0, 0)),
            scratch_shapes=[
                pltpu.VMEM((groups, 2 * rows, 1), jnp.float32),
                pltpu.VMEM((groups, 2 * rows, 1), jnp.float32),
                pltpu.VMEM((groups, 2 * rows, 128), jnp.float32),
            ],
        ),
        out_shape=jax.ShapeDtypeStruct(query.shape, jnp.bfloat16),
        compiler_params=pltpu.CompilerParams(vmem_limit_bytes=48 * 2**20),
        cost_estimate=pl.CostEstimate(
            flops=8 * blocks * rows * width * tiles * PARTS * ROWS,
            bytes_accessed=512 * tiles * PARTS * ROWS,
            transcendentals=blocks * rows * width // 128 * tiles * PARTS * ROWS,
        ),
        name="attention",
    )(meta, query, *parts)


def query_kernel(meta_ref, *refs):
    text_refs, refs = refs[:7], refs[7:]
    mine, swapped = refs[:CHAIN], refs[CHAIN : 2 * CHAIN]
    gain_ref, out_ref, weight_buf, acc_ref, sems = refs[2 * CHAIN :]
    core, y_at, x_at = meta_ref[0], meta_ref[2], meta_ref[3]
    width = weight_buf.shape[2]
    skip = mine[0].shape[2] - width

    def weight_copy(chain, i):
        return pltpu.make_async_copy(
            chain[i].at[:, :, pl.ds(skip, width)], weight_buf.at[pl.ds(2 * i, 2)], sems.at[i]
        )

    for lower, second in ((0, swapped), (1, mine)):

        @pl.when(core == lower)
        def _(second=second):
            for i in range(CHAIN):
                weight_copy(second, i).start()

    for j in range(4):
        weight_copy(mine, 2 * j).wait()
        weight_copy(mine, 2 * j + 1).wait()
        columns = []
        for i in range(4):
            chip = away(y_at, i) * 4 + away(x_at, j)
            at = pl.ds(pl.multiple_of(chip * 256, 256), 256)
            columns.append(jnp.concatenate([ref[:, at] for ref in text_refs], axis=0))
        part = jnp.dot(
            jnp.concatenate(columns, axis=1),
            weight_buf[4 * j : 4 * j + 4].reshape(1024, width),
            preferred_element_type=jnp.float32,
        )
        if j == 0:
            acc_ref[...] = part
        else:
            acc_ref[...] += part

    for b in range(4):
        for h in range(width // 128):
            block = acc_ref[b * 128 : (b + 1) * 128, h * 128 : (h + 1) * 128]
            out_ref[b, :, h * 128 : (h + 1) * 128] = norm_rows(block, gain_ref[...]).astype(jnp.bfloat16)


def project_query(texts, chains, gain, meta):
    rows, depth = texts[0].shape
    width = 512
    return pl.pallas_call(
        query_kernel,
        in_specs=[pl.BlockSpec(memory_space=pltpu.SMEM)]
        + [pl.BlockSpec(memory_space=pltpu.VMEM)] * 7
        + [pl.BlockSpec(memory_space=pl.ANY)] * (2 * CHAIN)
        + [pl.BlockSpec(memory_space=pltpu.VMEM)],
        out_specs=pl.BlockSpec(memory_space=pltpu.VMEM),
        out_shape=jax.ShapeDtypeStruct((4, rows, width), jnp.bfloat16),
        scratch_shapes=[
            pltpu.VMEM((16, 256, width), jnp.bfloat16),
            pltpu.VMEM((4 * rows, width), jnp.float32),
            pltpu.SemaphoreType.DMA((CHAIN,)),
        ],
        compiler_params=pltpu.CompilerParams(vmem_limit_bytes=32 * 2**20),
        cost_estimate=pl.CostEstimate(
            flops=8 * rows * depth * width, bytes_accessed=2 * (4 * rows + width) * depth, transcendentals=0
        ),
        name="query_projection",
    )(meta, *texts, *chains, gain)


def gather(k_weight, v_weight, q_share, tile_rows, normed, core):
    cut = v_weight.shape[1] // 2
    halves = (
        jnp.concatenate([k_weight, v_weight[:, :cut]], axis=1),
        jnp.concatenate([v_weight[:, cut:], q_share], axis=1),
    )
    swap = [(0, 1), (1, 0)]
    kept = jnp.where(core == 0, halves[0], halves[1])
    got = lax.ppermute(jnp.where(core == 0, halves[1], halves[0]), "c", swap)
    got, tile_rows = lax.optimization_barrier((got, tile_rows))
    other_rows = lax.ppermute(tile_rows, "c", swap)
    chip = jnp.where(core == 0, jnp.concatenate([kept, got]), jnp.concatenate([got, kept]))

    def move(piece, step, turn):
        pairs = []
        for y in range(4):
            for x in range(4):
                for c in range(2):
                    to = (y, (x + step) % 4) if (c == 0) == (turn == 0) else ((y + step) % 4, x)
                    pairs.append(((y * 4 + x) * 2 + c, (to[0] * 4 + to[1]) * 2 + c))
        return lax.ppermute(piece, SEQ, pairs)

    half = normed.shape[0] // 2
    upper, lower = normed[:half], normed[half:]
    upper_in, upper_out = lax.ppermute(upper, "z", ring(1)), lax.ppermute(upper, "z", ring(-1))
    near = jnp.stack([chip, move(chip, 1, 0)])
    far = jnp.stack([move(chip, -1, 0), move(chip, 2, 0)])
    near, far = lax.optimization_barrier((near, far))
    before = [move(near, 1, 1), move(far, 1, 1)]
    after = [move(near, -1, 1), move(far, -1, 1)]
    before, after, upper_in, upper_out, lower = lax.optimization_barrier((before, after, upper_in, upper_out, lower))
    lower_in, lower_out = lax.ppermute(lower, "z", ring(1)), lax.ppermute(lower, "z", ring(-1))
    opposite = lax.optimization_barrier([move(before[0], 1, 1), move(after[1], -1, 1)])
    chain = [near, far, *before, *after, *opposite]
    chain += [lax.ppermute(piece, "c", swap) for piece in chain]
    return chain, other_rows, (upper_in, lower_in, upper_out, lower_out)


def local(
    text,
    norm_gain,
    q_weight,
    k_weight,
    v_weight,
    q_gain,
    k_gain,
    vision,
    tiles_per_image,
    image_start,
    tile_owner,
):
    row_count = text.shape[0]
    head_dim = q_gain.shape[0]
    heads_kv = k_weight.shape[1] // head_dim
    tile_rows = vision[0]
    tile_len = tile_rows.shape[0]
    most_tiles = tile_owner.shape[1]
    length = row_count * lax.axis_size(SEQ)
    at_doc, at_y, at_x, at_core = (lax.axis_index(a) for a in ("z", "y", "x", "c"))

    group_width = q_weight.shape[1] // heads_kv
    q_share = lax.dynamic_slice_in_dim(q_weight, at_doc * group_width, group_width, 1)
    text_wide = text.astype(jnp.float32)
    normed = norm_rows(text_wide, norm_gain).astype(jnp.bfloat16)
    chains, other_rows, texts = gather(k_weight, v_weight, q_share, tile_rows, normed, at_core)
    tails = (ragged_end(tile_rows), ragged_end(other_rows))
    chains, other_rows, tails, texts = lax.optimization_barrier((chains, other_rows, tails, texts))
    opposite = [lax.ppermute(texts[0], "z", ring(1)), lax.ppermute(texts[3], "z", ring(-1))]
    texts = [normed, *texts[:2], *opposite, *texts[2:]]

    totals = jnp.sum(tiles_per_image, axis=1)
    valid = jnp.arange(most_tiles, dtype=jnp.int32)[None, :] < totals[:, None]
    owned = jnp.any(
        (tile_owner[:, :, None] == jnp.arange(lax.axis_size(SEQ), dtype=jnp.int32)) & valid[:, :, None], axis=1
    )
    owned = owned.reshape(owned.shape[0], -1, 2)
    crowded = jnp.any(owned[:, :, 0] & owned[:, :, 1])
    picked = jnp.arange(tiles_per_image.shape[0], dtype=jnp.int32) == at_doc
    tile_counts = jnp.sum(jnp.where(picked[:, None], tiles_per_image, 0), axis=0)
    starts = jnp.sum(jnp.where(picked[:, None], image_start, 0), axis=0)
    owners = jnp.sum(jnp.where(picked[:, None], tile_owner, 0), axis=0)
    first_core = jnp.any(owned & picked[:, None, None], axis=0)[:, 0]
    tile_low, tile_high, tile_valid = tile_spans(tile_counts, starts, length, most_tiles)
    tile_low = jnp.where(tile_valid, tile_low, 2 * length)
    tile_high = jnp.where(tile_valid, tile_high, 0)

    chip_first = jnp.sum(
        jnp.where(jnp.arange(first_core.shape[0]) == at_y * 4 + at_x, first_core.astype(jnp.int32), 0)
    )
    source = 1 - chip_first
    gain_row = k_gain.reshape(1, head_dim)
    chip_of = owners // 2
    turn = jnp.where((owners % 2 == 1) & first_core[chip_of], 1, 0)

    def project(from_core):
        use_own = (at_core == from_core).astype(jnp.int32)
        meta = jnp.stack([at_core, use_own, at_y, at_x]).astype(jnp.int32)
        return project_kv(tile_rows, other_rows, tails, chains, gain_row, meta)

    pieces, chains, texts = lax.optimization_barrier((project(source), chains, texts))

    def send(sent):
        return lax.all_to_all(sent, PLANE, 0, 0, tiled=True)

    def pick(got):
        return jnp.stack([got[chip_of[j]] for j in range(most_tiles)])

    def ask():
        meta = jnp.stack([at_core, at_core, at_y, at_x]).astype(jnp.int32)
        query = project_query(texts, chains, q_gain.reshape(1, head_dim), meta)
        return jnp.stack([query[0]] + [lax.ppermute(query[k], "z", ring(-k)) for k in (1, 2, 3)])

    def spread_one():
        got, mine = lax.optimization_barrier((send(pieces), ask()))
        return pick(got), mine

    def spread_two():
        got, second = lax.optimization_barrier((send(pieces), project(1)))
        later, mine = lax.optimization_barrier((send(second), ask()))
        return jnp.where((turn > 0)[:, None, None], pick(later), pick(got)), mine

    chosen, mine = lax.cond(crowded, spread_two, spread_one)

    before, after = lax.ppermute(chosen, "y", ring(1)), lax.ppermute(chosen, "y", ring(-1))
    half = most_tiles // 2
    opposite = [lax.ppermute(before[:half], "y", ring(1)), lax.ppermute(after[half:], "y", ring(-1))]
    parts = [chosen, before, after, *opposite]
    parts += [lax.ppermute(part, "c", [(0, 1), (1, 0)]) for part in parts]
    query = [mine[(at_x + s - at_doc) % 4] for s in range(4)]
    query = [query[0]] + [lax.ppermute(query[s], "x", ring(s)) for s in (1, 2, 3)]
    last_slot = jnp.array([1, 3, 2, 0], jnp.int32)[at_y]
    last_part = jnp.where(at_core == 1, last_slot, last_slot + 4)
    pad = 2 * HALF - tile_len
    pad_row = (last_part + 1) * ROWS - pad

    token_x = (at_x - jnp.arange(4, dtype=jnp.int32)) % 4
    blocks = ((at_y * 4 + token_x) * 2 + at_core) * row_count
    spans = jnp.concatenate([tile_low, tile_high])
    context = attend(jnp.stack(query), parts, jnp.concatenate([spans, blocks, pad_row[None]]), pad)
    context = [context[0]] + [lax.ppermute(context[k], "x", ring(-k)) for k in (1, 2, 3)]
    context = jnp.stack(context)
    return jnp.concatenate([context[(h - at_x) % 4] for h in range(heads_kv)], axis=1)


def solution(mesh):
    grid = Mesh(mesh.devices.reshape(4, 4, 4, 2), ("z", "y", "x", "c"))
    rows = ("z", "y", "x", "c")
    return jax.shard_map(
        local,
        mesh=grid,
        in_specs=(
            P(rows, None),
            P(),
            P(SEQ, None),
            P(SEQ, None),
            P(SEQ, None),
            P(),
            P(),
            P(rows, None, None),
            P(),
            P(),
            P(),
        ),
        out_specs=P(rows, None),
        check_vma=False,
    )
```

```python
import functools

import jax
import jax.numpy as jnp
from jax import lax
from jax.experimental import pallas as pl
from jax.experimental.pallas import tpu as pltpu
from jax.sharding import Mesh
from jax.sharding import PartitionSpec as P

SEQ = ("y", "x", "c")
PLANE = ("y", "x")
PARTS = 8
ROWS = 208
HALF = 4 * ROWS
NONE = -1e30
MASKED = -2e30
LOG2E = 1.4426950408889634


def tile_spans(tile_counts, starts, length, most_tiles):
    slots = tile_counts.shape[0]
    span_ends = jnp.concatenate([starts[1:], jnp.full((1,), length, jnp.int32)])
    offsets = jnp.cumsum(tile_counts) - tile_counts
    tile_total = jnp.sum(tile_counts)
    tile_ids = jnp.arange(most_tiles, dtype=jnp.int32)
    image_of = jnp.sum((offsets[None, :] <= tile_ids[:, None]).astype(jnp.int32), axis=1) - 1
    member = jnp.arange(slots, dtype=jnp.int32)[None, :] == image_of[:, None]
    tile_low = jnp.sum(jnp.where(member, starts[None, :], 0), axis=1)
    tile_high = jnp.sum(jnp.where(member, span_ends[None, :], 0), axis=1)
    return (tile_low, tile_high, tile_ids < tile_total)


def ring(step):
    return [(i, (i + step) % 4) for i in range(4)]


def norm_rows(values, gain):
    return values * lax.rsqrt(jnp.mean(values * values, axis=-1, keepdims=True) + 1e-05) * gain


AWAY = (0, -1, 1, 2)
CHAIN = 8


def away(at, slot):
    step = AWAY[slot] if isinstance(slot, int) else 0
    return (at + step + 4) % 4


def slot_of(at, place):
    ahead = (place - at + 4) % 4
    return jnp.where(ahead == 0, 0, jnp.where(ahead == 3, 1, ahead + 1))


def kv_kernel(tile_len, meta_ref, own_ref, other_ref, own_tail, other_tail, *refs):
    mine, swapped = refs[:CHAIN], refs[CHAIN : 2 * CHAIN]
    (gain_ref, out_ref, tile_buf, first_buf, second_buf, acc_ref, tile_sem, tail_sem, first_sem, second_sem) = refs[
        2 * CHAIN :
    ]
    core, own, y_at, x_at = (meta_ref[i] for i in range(4))
    whole = tile_len // 16 * 16 - HALF
    split, rest = first_buf.shape[2], second_buf.shape[2]

    def first_copy(chain, i):
        source = chain[i] if isinstance(i, int) else chain[0]
        return pltpu.make_async_copy(source, first_buf.at[pl.ds(2 * i, 2)], first_sem.at[i])

    def second_copy(chain, i):
        return pltpu.make_async_copy(
            chain[i].at[:, :, pl.ds(0, rest)], second_buf.at[pl.ds(2 * i, 2)], second_sem.at[i]
        )

    def tile_copies(i, source, tail, lower):
        at = pl.ds(pl.multiple_of(away(y_at, i) * 1024, 1024), 1024)
        to = pl.ds(pl.multiple_of(i * 1024, 1024), 1024)
        if not lower:
            rows = pl.ds(0, HALF)
            return [pltpu.make_async_copy(source.at[rows, at], tile_buf.at[rows, to], tile_sem.at[i])]
        return [
            pltpu.make_async_copy(
                source.at[pl.ds(HALF, whole), at], tile_buf.at[pl.ds(0, whole), to], tile_sem.at[i]
            ),
            pltpu.make_async_copy(tail.at[:, at], tile_buf.at[pl.ds(whole, 16), to], tail_sem.at[i]),
        ]

    def start_tile(i):
        for from_own, source, tail in ((1, own_ref, own_tail), (0, other_ref, other_tail)):
            for lower in (0, 1):

                @pl.when((own == from_own) & (core == lower))
                def _(source=source, tail=tail, lower=lower):
                    for copy in tile_copies(i, source, tail, lower):
                        copy.start()

    for lower, first, second in ((0, mine, swapped), (1, swapped, mine)):

        @pl.when(core == lower)
        def _(first=first, second=second):
            for i in range(2):
                first_copy(first, i).start()
            for i in range(CHAIN):
                second_copy(second, i).start()

    start_tile(0)
    for lower, first in ((0, mine), (1, swapped)):

        @pl.when(core == lower)
        def _(first=first):
            for i in range(2, CHAIN):
                first_copy(first, i).start()

    for i in range(1, 4):
        start_tile(i)

    acc_ref[...] = jnp.zeros_like(acc_ref)
    for j in range(CHAIN):
        second_copy(mine, j).wait()
    slots = [slot_of(x_at, x) for x in range(4)]

    def add(i, carry):
        first_copy(mine, 2 * i).wait()
        first_copy(mine, 2 * i + 1).wait()
        for lower in (0, 1):

            @pl.when(core == lower)
            def _(lower=lower):
                for copy in tile_copies(i, own_ref, own_tail, lower):
                    copy.wait()

        tile = tile_buf[:, pl.ds(pl.multiple_of(i * 1024, 1024), 1024)]
        one = jnp.concatenate([first_buf[4 * i + slot] for slot in slots], axis=0)
        two = jnp.concatenate([second_buf[4 * slot + i] for slot in slots], axis=0)
        acc_ref[:, :split] += jnp.dot(tile, one, preferred_element_type=jnp.float32)
        acc_ref[:, split:] += jnp.dot(tile, two, preferred_element_type=jnp.float32)
        return carry

    lax.fori_loop(0, 4, add, 0)

    for y in range(4):
        held = tile_len - core * HALF - y * ROWS
        kept = lax.broadcasted_iota(jnp.int32, (ROWS, 128), 0) < held
        for h in range(4):
            at = slice(y * ROWS, (y + 1) * ROWS)
            keys = acc_ref[at, h * 128 : (h + 1) * 128]
            values = acc_ref[at, (h + 4) * 128 : (h + 5) * 128]
            if y == 3:
                keys, values = jnp.where(kept, keys, 0.0), jnp.where(kept, values, 0.0)
            out_ref[y * 4 + h, :, :128] = norm_rows(keys, gain_ref[...]).astype(jnp.bfloat16)
            out_ref[y * 4 + h, :, 128:] = values.astype(jnp.bfloat16)


def ragged_end(tile):
    whole = tile.shape[0] // 16 * 16
    return jnp.pad(tile[whole:], ((0, 16 - tile.shape[0] + whole), (0, 0)))


def project_kv(own, other, tails, chains, k_gain, meta):
    tile_len, depth = own.shape
    width, split = 1024, chains[0].shape[2]
    return pl.pallas_call(
        functools.partial(kv_kernel, tile_len),
        in_specs=[pl.BlockSpec(memory_space=pltpu.SMEM)]
        + [pl.BlockSpec(memory_space=pl.ANY)] * (4 + 2 * CHAIN)
        + [pl.BlockSpec(memory_space=pltpu.VMEM)],
        out_specs=pl.BlockSpec(memory_space=pltpu.VMEM),
        out_shape=jax.ShapeDtypeStruct((16, ROWS, 256), jnp.bfloat16),
        scratch_shapes=[
            pltpu.VMEM((HALF, depth), jnp.bfloat16),
            pltpu.VMEM((16, 256, split), jnp.bfloat16),
            pltpu.VMEM((16, 256, width - split), jnp.bfloat16),
            pltpu.VMEM((HALF, width), jnp.float32),
        ]
        + [pltpu.SemaphoreType.DMA((4,))] * 2
        + [pltpu.SemaphoreType.DMA((CHAIN,))] * 2,
        compiler_params=pltpu.CompilerParams(vmem_limit_bytes=52 * 2**20),
        cost_estimate=pl.CostEstimate(
            flops=2 * HALF * depth * width, bytes_accessed=2 * (HALF + width) * depth, transcendentals=0
        ),
        name="kv_projection",
    )(meta, own, other, *tails, *chains, k_gain)


def attend_kernel(pad, meta_ref, q_ref, *refs):
    part_refs, (out_ref, m_ref, l_ref, acc_ref) = refs[:-4], refs[-4:]
    tile = pl.program_id(0)
    blocks, rows, width = q_ref.shape
    heads = width // 128
    keys = PARTS * ROWS
    factor = LOG2E / 128**0.5
    pairs = heads // 2

    @pl.when(tile == 0)
    def _():
        m_ref[...] = jnp.full_like(m_ref, NONE)
        l_ref[...] = jnp.zeros_like(l_ref)
        acc_ref[...] = jnp.zeros_like(acc_ref)

    low, high = meta_ref[tile], meta_ref[4 + tile]
    some = False
    for b in range(blocks):
        first = meta_ref[8 + b]
        some = some | ((low < first + rows) & (high > first))

    @pl.when(some)
    def _():
        held = []
        for own, before, after, low_tiles, high_tiles in (part_refs[:5], part_refs[5:]):
            held += [own[0], before[0], after[0], jnp.where(tile < 2, low_tiles[0], high_tiles[0])]
        kv = jnp.concatenate(held, axis=0)
        row = lax.broadcasted_iota(jnp.int32, (keys, 128), 0)
        lane = lax.broadcasted_iota(jnp.int32, (keys, 128), 1)
        padding = (row >= meta_ref[8 + blocks]) & (row < meta_ref[8 + blocks] + pad)
        key_mask = jnp.where((lane == 0) & padding, MASKED, jnp.where(lane == 1, 1.0, 0.0))
        key = jnp.concatenate([kv[:, :128], key_mask.astype(jnp.bfloat16)], axis=1)
        value = jnp.concatenate([kv[:, 128:], jnp.ones((keys, 128), jnp.bfloat16)], axis=1)
        text_row = lax.broadcasted_iota(jnp.int32, (rows, 128), 0)
        text_lane = lax.broadcasted_iota(jnp.int32, (rows, 128), 1)

        def score(group):
            b, h = group // pairs, group % pairs * 2
            at = meta_ref[8 + b] + text_row
            outside = (at < low) | (at >= high)
            mask = jnp.where((text_lane == 1) & outside, MASKED, jnp.where(text_lane == 0, 1.0, 0.0))
            mask = mask.astype(jnp.bfloat16)
            both = [
                jnp.concatenate([q_ref[b, :, i * 128 : (i + 1) * 128], mask], axis=1) for i in (h, h + 1)
            ]
            return lax.dot_general(
                jnp.concatenate(both, axis=0), key, (((1,), (1,)), ((), ())), preferred_element_type=jnp.float32
            )

        def soften(group, scores):
            m_old = m_ref[group]
            m_new = jnp.maximum(m_old, jnp.max(scores, axis=1, keepdims=True))
            probs = jnp.exp2((scores - m_new) * factor)
            alpha = jnp.exp2((m_old - m_new) * factor)
            m_ref[group] = m_new
            summed = jnp.dot(probs.astype(jnp.bfloat16), value, preferred_element_type=jnp.float32)
            l_ref[group] = l_ref[group] * alpha + summed[:, 128:129]
            acc_ref[group] = acc_ref[group] * alpha + summed[:, :128]

        scores = score(0)
        for group in range(blocks * pairs):
            ahead = score(group + 1) if group + 1 < blocks * pairs else None
            soften(group, scores)
            scores = ahead

    @pl.when(tile == pl.num_programs(0) - 1)
    def _():
        for b in range(blocks):
            for h in range(heads):
                group, at = b * pairs + h // 2, slice(h % 2 * rows, (h % 2 + 1) * rows)
                out_ref[b, :, h * 128 : (h + 1) * 128] = (
                    acc_ref[group, at] / jnp.maximum(l_ref[group, at], 1.0)
                ).astype(jnp.bfloat16)


def attend(query, parts, meta, pad):
    blocks, rows, width = query.shape
    tiles = parts[0].shape[0]
    groups = blocks * width // 256
    return pl.pallas_call(
        functools.partial(attend_kernel, pad),
        grid_spec=pltpu.PrefetchScalarGridSpec(
            num_scalar_prefetch=1,
            grid=(tiles,),
            in_specs=[
                pl.BlockSpec((blocks, rows, width), lambda j, meta: (0, 0, 0)),
            ]
            + (
                [pl.BlockSpec((1, ROWS, 256), lambda j, meta: (j, 0, 0))] * 3
                + [pl.BlockSpec((1, ROWS, 256), lambda j, meta: (jnp.minimum(j, 1), 0, 0))]
                + [pl.BlockSpec((1, ROWS, 256), lambda j, meta: (jnp.maximum(j - 2, 0), 0, 0))]
            )
            * 2,
            out_specs=pl.BlockSpec((blocks, rows, width), lambda j, meta: (0, 0, 0)),
            scratch_shapes=[
                pltpu.VMEM((groups, 2 * rows, 1), jnp.float32),
                pltpu.VMEM((groups, 2 * rows, 1), jnp.float32),
                pltpu.VMEM((groups, 2 * rows, 128), jnp.float32),
            ],
        ),
        out_shape=jax.ShapeDtypeStruct(query.shape, jnp.bfloat16),
        compiler_params=pltpu.CompilerParams(vmem_limit_bytes=48 * 2**20),
        cost_estimate=pl.CostEstimate(
            flops=8 * blocks * rows * width * tiles * PARTS * ROWS,
            bytes_accessed=512 * tiles * PARTS * ROWS,
            transcendentals=blocks * rows * width // 128 * tiles * PARTS * ROWS,
        ),
        name="attention",
    )(meta, query, *parts)


def query_kernel(meta_ref, *refs):
    text_refs, refs = refs[:7], refs[7:]
    mine, swapped = refs[:CHAIN], refs[CHAIN : 2 * CHAIN]
    gain_ref, out_ref, weight_buf, acc_ref, sems = refs[2 * CHAIN :]
    core, y_at, x_at = meta_ref[0], meta_ref[2], meta_ref[3]
    width = weight_buf.shape[2]
    skip = mine[0].shape[2] - width

    def weight_copy(chain, i):
        return pltpu.make_async_copy(
            chain[i].at[:, :, pl.ds(skip, width)], weight_buf.at[pl.ds(2 * i, 2)], sems.at[i]
        )

    for lower, second in ((0, swapped), (1, mine)):

        @pl.when(core == lower)
        def _(second=second):
            for i in range(CHAIN):
                weight_copy(second, i).start()

    for j in range(4):
        weight_copy(mine, 2 * j).wait()
        weight_copy(mine, 2 * j + 1).wait()
        columns = []
        for i in range(4):
            chip = away(y_at, i) * 4 + away(x_at, j)
            at = pl.ds(pl.multiple_of(chip * 256, 256), 256)
            columns.append(jnp.concatenate([ref[:, at] for ref in text_refs], axis=0))
        part = jnp.dot(
            jnp.concatenate(columns, axis=1),
            weight_buf[4 * j : 4 * j + 4].reshape(1024, width),
            preferred_element_type=jnp.float32,
        )
        if j == 0:
            acc_ref[...] = part
        else:
            acc_ref[...] += part

    for b in range(4):
        for h in range(width // 128):
            block = acc_ref[b * 128 : (b + 1) * 128, h * 128 : (h + 1) * 128]
            out_ref[b, :, h * 128 : (h + 1) * 128] = norm_rows(block, gain_ref[...]).astype(jnp.bfloat16)


def project_query(texts, chains, gain, meta):
    rows, depth = texts[0].shape
    width = 512
    return pl.pallas_call(
        query_kernel,
        in_specs=[pl.BlockSpec(memory_space=pltpu.SMEM)]
        + [pl.BlockSpec(memory_space=pltpu.VMEM)] * 7
        + [pl.BlockSpec(memory_space=pl.ANY)] * (2 * CHAIN)
        + [pl.BlockSpec(memory_space=pltpu.VMEM)],
        out_specs=pl.BlockSpec(memory_space=pltpu.VMEM),
        out_shape=jax.ShapeDtypeStruct((4, rows, width), jnp.bfloat16),
        scratch_shapes=[
            pltpu.VMEM((16, 256, width), jnp.bfloat16),
            pltpu.VMEM((4 * rows, width), jnp.float32),
            pltpu.SemaphoreType.DMA((CHAIN,)),
        ],
        compiler_params=pltpu.CompilerParams(vmem_limit_bytes=32 * 2**20),
        cost_estimate=pl.CostEstimate(
            flops=8 * rows * depth * width, bytes_accessed=2 * (4 * rows + width) * depth, transcendentals=0
        ),
        name="query_projection",
    )(meta, *texts, *chains, gain)


def gather(k_weight, v_weight, q_share, tile_rows, normed, core):
    cut = v_weight.shape[1] // 2
    halves = (
        jnp.concatenate([k_weight, v_weight[:, :cut]], axis=1),
        jnp.concatenate([v_weight[:, cut:], q_share], axis=1),
    )
    swap = [(0, 1), (1, 0)]
    kept = jnp.where(core == 0, halves[0], halves[1])
    got = lax.ppermute(jnp.where(core == 0, halves[1], halves[0]), "c", swap)
    got, tile_rows = lax.optimization_barrier((got, tile_rows))
    other_rows = lax.ppermute(tile_rows, "c", swap)
    chip = jnp.where(core == 0, jnp.concatenate([kept, got]), jnp.concatenate([got, kept]))

    def move(piece, step, turn):
        pairs = []
        for y in range(4):
            for x in range(4):
                for c in range(2):
                    to = (y, (x + step) % 4) if (c == 0) == (turn == 0) else ((y + step) % 4, x)
                    pairs.append(((y * 4 + x) * 2 + c, (to[0] * 4 + to[1]) * 2 + c))
        return lax.ppermute(piece, SEQ, pairs)

    half = normed.shape[0] // 2
    upper, lower = normed[:half], normed[half:]
    upper_in, upper_out = lax.ppermute(upper, "z", ring(1)), lax.ppermute(upper, "z", ring(-1))
    near = jnp.stack([chip, move(chip, 1, 0)])
    far = jnp.stack([move(chip, -1, 0), move(chip, 2, 0)])
    near, far = lax.optimization_barrier((near, far))
    before = [move(near, 1, 1), move(far, 1, 1)]
    after = [move(near, -1, 1), move(far, -1, 1)]
    before, after, upper_in, upper_out, lower = lax.optimization_barrier((before, after, upper_in, upper_out, lower))
    lower_in, lower_out = lax.ppermute(lower, "z", ring(1)), lax.ppermute(lower, "z", ring(-1))
    opposite = lax.optimization_barrier([move(before[0], 1, 1), move(after[1], -1, 1)])
    chain = [near, far, *before, *after, *opposite]
    chain += [lax.ppermute(piece, "c", swap) for piece in chain]
    return chain, other_rows, (upper_in, lower_in, upper_out, lower_out)


def local(
    text,
    norm_gain,
    q_weight,
    k_weight,
    v_weight,
    q_gain,
    k_gain,
    vision,
    tiles_per_image,
    image_start,
    tile_owner,
):
    row_count = text.shape[0]
    head_dim = q_gain.shape[0]
    heads_kv = k_weight.shape[1] // head_dim
    tile_rows = vision[0]
    tile_len = tile_rows.shape[0]
    most_tiles = tile_owner.shape[1]
    length = row_count * lax.axis_size(SEQ)
    at_doc, at_y, at_x, at_core = (lax.axis_index(a) for a in ("z", "y", "x", "c"))

    group_width = q_weight.shape[1] // heads_kv
    q_share = lax.dynamic_slice_in_dim(q_weight, at_doc * group_width, group_width, 1)
    text_wide = text.astype(jnp.float32)
    normed = norm_rows(text_wide, norm_gain).astype(jnp.bfloat16)
    chains, other_rows, texts = gather(k_weight, v_weight, q_share, tile_rows, normed, at_core)
    tails = (ragged_end(tile_rows), ragged_end(other_rows))
    chains, other_rows, tails = lax.optimization_barrier((chains, other_rows, tails))

    totals = jnp.sum(tiles_per_image, axis=1)
    valid = jnp.arange(most_tiles, dtype=jnp.int32)[None, :] < totals[:, None]
    owned = jnp.any(
        (tile_owner[:, :, None] == jnp.arange(lax.axis_size(SEQ), dtype=jnp.int32)) & valid[:, :, None], axis=1
    )
    owned = owned.reshape(owned.shape[0], -1, 2)
    crowded = jnp.any(owned[:, :, 0] & owned[:, :, 1])
    picked = jnp.arange(tiles_per_image.shape[0], dtype=jnp.int32) == at_doc
    tile_counts = jnp.sum(jnp.where(picked[:, None], tiles_per_image, 0), axis=0)
    starts = jnp.sum(jnp.where(picked[:, None], image_start, 0), axis=0)
    owners = jnp.sum(jnp.where(picked[:, None], tile_owner, 0), axis=0)
    first_core = jnp.any(owned & picked[:, None, None], axis=0)[:, 0]
    tile_low, tile_high, tile_valid = tile_spans(tile_counts, starts, length, most_tiles)
    tile_low = jnp.where(tile_valid, tile_low, 2 * length)
    tile_high = jnp.where(tile_valid, tile_high, 0)

    chip_first = jnp.sum(
        jnp.where(jnp.arange(first_core.shape[0]) == at_y * 4 + at_x, first_core.astype(jnp.int32), 0)
    )
    source = 1 - chip_first
    gain_row = k_gain.reshape(1, head_dim)
    chip_of = owners // 2
    turn = jnp.where((owners % 2 == 1) & first_core[chip_of], 1, 0)

    def project(from_core):
        use_own = (at_core == from_core).astype(jnp.int32)
        meta = jnp.stack([at_core, use_own, at_y, at_x]).astype(jnp.int32)
        return project_kv(tile_rows, other_rows, tails, chains, gain_row, meta)

    pieces, chains, texts = lax.optimization_barrier((project(source), chains, texts))

    def send(sent):
        return lax.all_to_all(sent, PLANE, 0, 0, tiled=True)

    def pick(got):
        return jnp.stack([got[chip_of[j]] for j in range(most_tiles)])

    def ask():
        meta = jnp.stack([at_core, at_core, at_y, at_x]).astype(jnp.int32)
        opposite = [lax.ppermute(texts[0], "z", ring(1)), lax.ppermute(texts[3], "z", ring(-1))]
        query = project_query([normed, *texts[:2], *opposite, *texts[2:]], chains, q_gain.reshape(1, head_dim), meta)
        return jnp.stack([query[0]] + [lax.ppermute(query[k], "z", ring(-k)) for k in (1, 2, 3)])

    def spread_one():
        got, mine = lax.optimization_barrier((send(pieces), ask()))
        return pick(got), mine

    def spread_two():
        got, second = lax.optimization_barrier((send(pieces), project(1)))
        later, mine = lax.optimization_barrier((send(second), ask()))
        return jnp.where((turn > 0)[:, None, None], pick(later), pick(got)), mine

    chosen, mine = lax.cond(crowded, spread_two, spread_one)

    before, after = lax.ppermute(chosen, "y", ring(1)), lax.ppermute(chosen, "y", ring(-1))
    half = most_tiles // 2
    opposite = [lax.ppermute(before[:half], "y", ring(1)), lax.ppermute(after[half:], "y", ring(-1))]
    parts = [chosen, before, after, *opposite]
    parts += [lax.ppermute(part, "c", [(0, 1), (1, 0)]) for part in parts]
    query = [mine[(at_x + s - at_doc) % 4] for s in range(4)]
    query = [query[0]] + [lax.ppermute(query[s], "x", ring(s)) for s in (1, 2, 3)]
    last_slot = jnp.array([1, 3, 2, 0], jnp.int32)[at_y]
    last_part = jnp.where(at_core == 1, last_slot, last_slot + 4)
    pad = 2 * HALF - tile_len
    pad_row = (last_part + 1) * ROWS - pad

    token_x = (at_x - jnp.arange(4, dtype=jnp.int32)) % 4
    blocks = ((at_y * 4 + token_x) * 2 + at_core) * row_count
    spans = jnp.concatenate([tile_low, tile_high])
    context = attend(jnp.stack(query), parts, jnp.concatenate([spans, blocks, pad_row[None]]), pad)
    context = [context[0]] + [lax.ppermute(context[k], "x", ring(-k)) for k in (1, 2, 3)]
    context = jnp.stack(context)
    return jnp.concatenate([context[(h - at_x) % 4] for h in range(heads_kv)], axis=1)


def solution(mesh):
    grid = Mesh(mesh.devices.reshape(4, 4, 4, 2), ("z", "y", "x", "c"))
    rows = ("z", "y", "x", "c")
    return jax.shard_map(
        local,
        mesh=grid,
        in_specs=(
            P(rows, None),
            P(),
            P(SEQ, None),
            P(SEQ, None),
            P(SEQ, None),
            P(),
            P(),
            P(rows, None, None),
            P(),
            P(),
            P(),
        ),
        out_specs=P(rows, None),
        check_vma=False,
    )
```
